512 devices in a mesh: row: 16 (over x_hi, z), col: 32 (over x_lo, y, core).
Axes of the slice: x: 4 (x_hi: 2, x_lo: 2; x = x_hi * 2 + x_lo), y: 8, z: 8, core: 2. Of those that a mesh axis runs over, the one named last changes fastest.
Arguments:
- tokens: bfloat16 [1024, 8192], P('col', 'row'), may hold values from -6 to 6
- grad_out: bfloat16 [1024, 8192], P('col', 'row'), may hold values from -0.59765625 to 0.59765625
- gate_pre: bfloat16 [1024, 14336], P('row', 'col'), may hold values from -8 to 8
- up_pre: bfloat16 [1024, 14336], P('row', 'col'), may hold values from -6 to 6
- gate_latent: bfloat16 [8192, 14336], P('row', 'col'), may hold values from -1 to 1
- up_latent: bfloat16 [8192, 14336], P('row', 'col'), may hold values from -1 to 1
- down_latent: bfloat16 [14336, 8192], P('col', 'row'), may hold values from -1 to 1
Outputs:
- grad_tokens: bfloat16 [1024, 8192], P('col', 'row')
- grad_gate: bfloat16 [8192, 14336], P('row', 'col')
- grad_up: bfloat16 [8192, 14336], P('row', 'col')
- grad_down: bfloat16 [14336, 8192], P('col', 'row')
The draws below stay inside these ranges and needn't reach their ends.
All inputs are finite; a program needn't handle non-finite values.
Results may differ from the reference program's by a relative error of at most 0.0059.
Values may be sent and summed in bfloat16 or wider, within the bound.
No kernel may reach another device: no remote copies, remote signals or barrier semaphores. Data moves between devices by JAX's collectives and lax.ppermute only.
A program may use at most 64 MiB of HBM per device.

```python
import math
import jax
import jax.numpy as jnp
from jax import lax

EMBED_SIZE = 8192
GATE_INNER_SIZE = 14336
TOKENS = 1024
N_ROW = 16
N_COL = 32


def master_rescaled_matrix(mean_magnitude, key, source_dimension, target_dimension, source_tile_number, target_tile_number, dispersion_multiplier, ternary_bound, outlier_gain):
    row_key, col_key, strip_key, band_key, cell_key, whole_key = jax.random.split(key, 6)
    rise = math.log(3.0)
    row_fac = jnp.exp(rise * jnp.arange(source_dimension, dtype=jnp.float32) / source_dimension + jax.random.uniform(row_key, (source_dimension,), jnp.float32, 0.0, math.log(dispersion_multiplier)))
    col_fac = jnp.exp(rise * jnp.arange(target_dimension, dtype=jnp.float32) / target_dimension + jax.random.uniform(col_key, (target_dimension,), jnp.float32, 0.0, math.log(dispersion_multiplier)))
    support_radius = math.log(outlier_gain)
    strip_amp = jnp.exp(jax.random.uniform(strip_key, (source_tile_number,), jnp.float32, 0.0, support_radius))
    band_amp = jnp.exp(jax.random.uniform(band_key, (target_tile_number,), jnp.float32, 0.0, support_radius))
    cell_amp = jnp.exp(jax.random.uniform(cell_key, (source_tile_number, target_tile_number), jnp.float32, 0.0, support_radius))
    block_amp = strip_amp[:, None] * band_amp[None, :] * cell_amp
    overall = jnp.exp(jax.random.uniform(whole_key, (), jnp.float32, math.log(0.6), 0.0))
    normalizer_denominator = ternary_bound * (3.0 * dispersion_multiplier) * (3.0 * dispersion_multiplier) * outlier_gain * outlier_gain * outlier_gain
    shaped = mean_magnitude * row_fac[:, None] * col_fac[None, :]
    shaped = shaped.reshape(source_tile_number, source_dimension // source_tile_number, target_tile_number, target_dimension // target_tile_number) * block_amp[:, None, :, None]
    return (shaped.reshape(source_dimension, target_dimension) * (overall / normalizer_denominator)).astype(jnp.bfloat16)


def master_initial_deviation(key, source_dimension, target_dimension):
    base_key, magnitude_seed_handle = jax.random.split(key)
    mean_magnitude = jax.random.truncated_normal(base_key, -4.0, 4.0, (source_dimension, target_dimension), jnp.float32)
    dispersion_multiplier = 10.0
    ternary_bound = 4.0
    outlier_gain = 2.0
    return (mean_magnitude, magnitude_seed_handle, dispersion_multiplier, ternary_bound, outlier_gain)


def draw_gate_latent(key, part):
    key = jax.random.fold_in(key, 11)
    mean_magnitude, magnitude_seed_handle, dispersion_multiplier, ternary_bound, outlier_gain = master_initial_deviation(key, EMBED_SIZE, GATE_INNER_SIZE)
    return master_rescaled_matrix(mean_magnitude, magnitude_seed_handle, EMBED_SIZE, GATE_INNER_SIZE, N_ROW, N_COL, dispersion_multiplier, ternary_bound, outlier_gain)


def draw_up_latent(key, part):
    key = jax.random.fold_in(key, 23)
    mean_magnitude, magnitude_seed_handle, dispersion_multiplier, ternary_bound, outlier_gain = master_initial_deviation(key, EMBED_SIZE, GATE_INNER_SIZE)
    return master_rescaled_matrix(mean_magnitude, magnitude_seed_handle, EMBED_SIZE, GATE_INNER_SIZE, N_ROW, N_COL, dispersion_multiplier, ternary_bound, outlier_gain)


def draw_down_latent(key, part):
    key = jax.random.fold_in(key, 37)
    mean_magnitude, magnitude_seed_handle, dispersion_multiplier, ternary_bound, outlier_gain = master_initial_deviation(key, GATE_INNER_SIZE, EMBED_SIZE)
    return master_rescaled_matrix(mean_magnitude, magnitude_seed_handle, GATE_INNER_SIZE, EMBED_SIZE, N_COL, N_ROW, dispersion_multiplier, ternary_bound, outlier_gain)


def raised(drawn, key, source, target, blocks, factor):
    def block_of(dim):
        return (jnp.arange(drawn.shape[dim]) // (drawn.shape[dim] // blocks)).reshape((-1,) + (1,) * (drawn.ndim - 1 - dim))

    first = jax.random.permutation(key, blocks)[block_of(target)]
    far = (block_of(target) + blocks // 2) % blocks
    return jnp.where((block_of(source) == first) | (block_of(source) == far), factor * drawn, drawn)


def levels(own_key, shape, pieces, low, largest):
    def one(dim, shards_of):
        heights = jax.random.uniform(jax.random.fold_in(jax.random.fold_in(own_key, 6), dim), (shards_of,), jnp.float32, low / len(pieces), largest / len(pieces))
        return jnp.repeat(jnp.exp(heights), shape[dim] // shards_of).reshape((-1,) + (1,) * (len(shape) - dim - 1))

    gain = one(*pieces[0])
    for cut in pieces[1:]:
        gain = gain * one(*cut)
    return gain


def noise(key, shape, width, most, shards=(), kind=jnp.bfloat16):
    loudness = levels(key, shape, shards, -0.22, 0.18) if shards else 1.0
    result = jax.random.normal(key, shape, jnp.float32) * width * loudness
    return jnp.minimum(jnp.maximum(result, -most), most).astype(kind)


def bell_draw_with(stream_key, shape, width, bound, shards, heavy, held_as=jnp.bfloat16):
    result = width * jax.random.normal(stream_key, shape, jnp.float32)
    if shards:
        result = result * levels(stream_key, shape, shards, -0.22, 0.18)
    return jnp.clip(raised(result, jax.random.fold_in(stream_key, 3), *heavy), -bound, bound).astype(held_as)


def setup_inputs(seed: int = 0) -> dict:
    seeds = jax.random.split(jax.random.key(seed), 8)
    tokens = noise(seeds[0], (TOKENS, EMBED_SIZE), 1.0, 6.0, ((0, 32), (1, 16)))
    grad_out = bell_draw_with(seeds[1], (TOKENS, EMBED_SIZE), 0.1, 0.59765625, ((0, 32), (1, 16)), (1, 0, 32, 2.75))
    gate_pre = noise(seeds[2], (TOKENS, GATE_INNER_SIZE), 1.5, 8.0, ((0, 16), (1, 32)))
    up_pre = noise(seeds[3], (TOKENS, GATE_INNER_SIZE), 1.0, 6.0, ((0, 16), (1, 32)))
    gate_latent = draw_gate_latent(jax.random.fold_in(seeds[7], 71), 0)
    up_latent = draw_up_latent(jax.random.fold_in(seeds[7], 71), 0)
    down_latent = draw_down_latent(jax.random.fold_in(seeds[7], 71), 0)
    return {"tokens": tokens, "grad_out": grad_out, "gate_pre": gate_pre, "up_pre": up_pre, "gate_latent": gate_latent, "up_latent": up_latent, "down_latent": down_latent}


def quantize(latent):
    values = latent.astype(jnp.float32)
    scale = jnp.sum(jnp.abs(values)) / (EMBED_SIZE * GATE_INNER_SIZE) + 1e-5
    return (scale * jnp.clip(values / scale, -1.0, 1.0)).astype(jnp.bfloat16)


def contract_last(left, right):
    return lax.dot_general(left, right, (((1,), (1,)), ((), ())), preferred_element_type=jnp.float32)


def reference(tokens, grad_out, gate_pre, up_pre, gate_latent, up_latent, down_latent):
    quant_gate = quantize(gate_latent)
    quant_up = quantize(up_latent)
    quant_down = quantize(down_latent)
    grad_hidden = contract_last(grad_out, quant_down)
    gate_f = gate_pre.astype(jnp.float32)
    up_f = up_pre.astype(jnp.float32)
    sigma = jax.nn.sigmoid(gate_f)
    silu_gate = gate_f * sigma
    hidden = (silu_gate * up_f).astype(jnp.bfloat16)
    grad_gpre = (grad_hidden * up_f * sigma * (1.0 + gate_f * (1.0 - sigma))).astype(jnp.bfloat16)
    grad_upre = (grad_hidden * silu_gate).astype(jnp.bfloat16)
    grad_down = jnp.dot(hidden.T, grad_out, preferred_element_type=jnp.float32).astype(jnp.bfloat16)
    grad_gate = jnp.dot(tokens.T, grad_gpre, preferred_element_type=jnp.float32).astype(jnp.bfloat16)
    grad_up = jnp.dot(tokens.T, grad_upre, preferred_element_type=jnp.float32).astype(jnp.bfloat16)
    grad_tokens = (contract_last(grad_gpre, quant_gate) + contract_last(grad_upre, quant_up)).astype(jnp.bfloat16)
    return grad_tokens, grad_gate, grad_up, grad_down
```

```python
import jax
import jax.numpy as jnp
from jax import lax
from jax.sharding import Mesh, PartitionSpec as P

EMBED_SIZE = 8192
GATE_INNER_SIZE = 14336
N_ROW = 16
N_CHIP = 16
ROW = ("xh", "z")
CHIP = ("xl", "y")


def contract_last(left, right):
    return lax.dot_general(
        left, right, (((1,), (1,)), ((), ())), preferred_element_type=jnp.float32
    )


def contract_first(left, right):
    return lax.dot_general(
        left, right, (((0,), (0,)), ((), ())), preferred_element_type=jnp.float32
    )


def quantize(values, scale):
    return (scale * jnp.clip(values.astype(jnp.float32) / scale, -1.0, 1.0)).astype(jnp.bfloat16)


def swiglu_grads(grad_hidden, gate_pre, up_pre):
    gate_f = gate_pre.astype(jnp.float32)
    up_f = up_pre.astype(jnp.float32)
    sigma = jax.nn.sigmoid(gate_f)
    silu_gate = gate_f * sigma
    grad_gpre = (grad_hidden * up_f * sigma * (1.0 + gate_f * (1.0 - sigma))).astype(jnp.bfloat16)
    grad_upre = (grad_hidden * silu_gate).astype(jnp.bfloat16)
    hidden = (silu_gate * up_f).astype(jnp.bfloat16)
    return (grad_gpre, grad_upre, hidden)


def to_all(values, axes, count):
    return lax.all_to_all(jnp.broadcast_to(values, (count,) + values.shape), axes, 0, 0)


def swapped(values):
    return lax.ppermute(values, "core", [(0, 1), (1, 0)])


def in_order(core, mine, other, axis):
    return jnp.where(
        core == 0, jnp.stack([mine, other], axis=axis), jnp.stack([other, mine], axis=axis)
    )


def shards(tokens, grad_out, gate_pre, up_pre, gate_latent, up_latent, down_latent):
    core = lax.axis_index("core")
    width = tokens.shape[1]
    inner = gate_pre.shape[1]
    out_half = to_all(grad_out, CHIP, N_CHIP)
    down_other = swapped(down_latent)
    pre_full = lax.all_gather(
        jnp.concatenate([gate_pre, up_pre], axis=1), ROW, axis=0, tiled=True
    )

    sums = [jnp.sum(jnp.abs(w.astype(jnp.float32))) for w in (gate_latent, up_latent, down_latent)]
    tile = jnp.broadcast_to(jnp.stack(sums + [jnp.float32(0.0)] * 5)[:, None], (8, 128))
    tile = jnp.sum(to_all(tile, ROW + ("core",), 2 * N_ROW), axis=0)
    tile = jnp.sum(to_all(tile, CHIP, N_CHIP), axis=0)
    scales = tile[:, 0] / float(EMBED_SIZE * GATE_INNER_SIZE) + 1e-05

    out_rows = out_half.reshape((-1, width))
    partial = jnp.concatenate(
        [contract_last(out_rows, quantize(down_latent, scales[2])).astype(jnp.bfloat16),
         contract_last(out_rows, quantize(down_other, scales[2])).astype(jnp.bfloat16)],
        axis=1,
    )
    tokens, partial = lax.optimization_barrier((tokens, partial))
    parts = lax.all_to_all(partial.reshape((N_ROW, -1, 2 * inner)), ROW, 0, 0)
    tokens_half = to_all(tokens, CHIP, N_CHIP)
    both_half = jnp.stack([out_half, tokens_half])
    both = in_order(core, both_half, swapped(both_half), 2)
    out_full = both[0].reshape((-1, width))
    tokens_full = both[1].reshape((-1, width))

    summed = jnp.sum(parts.astype(jnp.float32), axis=0).astype(jnp.bfloat16)
    split = in_order(core, summed[:, :inner], summed[:, inner:], 0)
    grad_hidden = lax.all_to_all(
        jnp.broadcast_to(split, (N_ROW,) + split.shape).reshape((2 * N_ROW,) + split.shape[1:]),
        ROW + ("core",), 0, 0,
    ).reshape((-1, inner)).astype(jnp.float32)
    gpre, upre, hidden = swiglu_grads(grad_hidden, pre_full[:, :inner], pre_full[:, inner:])

    partial = contract_last(gpre, quantize(gate_latent, scales[0])) + contract_last(
        upre, quantize(up_latent, scales[1])
    )
    blocks = partial.reshape((N_CHIP, 2, -1, width))
    kept = lax.dynamic_index_in_dim(blocks, core, 1, keepdims=False)
    sent = lax.dynamic_index_in_dim(blocks, 1 - core, 1, keepdims=False).astype(jnp.bfloat16)
    pair = (kept + swapped(sent).astype(jnp.float32)).astype(jnp.bfloat16)
    parts = lax.all_to_all(pair, CHIP, 0, 0)
    grad_down = contract_first(hidden, out_full).astype(jnp.bfloat16)
    grad_gate = contract_first(tokens_full, gpre).astype(jnp.bfloat16)
    grad_up = contract_first(tokens_full, upre).astype(jnp.bfloat16)
    grad_tokens = jnp.sum(parts.astype(jnp.float32), axis=0).astype(jnp.bfloat16)
    return (grad_tokens, grad_gate, grad_up, grad_down)


def solution(mesh):
    fine = Mesh(mesh.devices.reshape((2, 8, 2, 8, 2)), ROW + CHIP + ("core",))
    col = CHIP + ("core",)
    in_specs = (
        P(col, ROW),
        P(col, ROW),
        P(ROW, col),
        P(ROW, col),
        P(ROW, col),
        P(ROW, col),
        P(col, ROW),
    )
    out_specs = (P(col, ROW), P(ROW, col), P(ROW, col), P(col, ROW))
    return jax.shard_map(shards, mesh=fine, in_specs=in_specs, out_specs=out_specs, check_vma=False)
```

```python
import jax
import jax.numpy as jnp
from jax import lax
from jax.experimental import pallas as pl
from jax.experimental.pallas import tpu as pltpu
from jax.sharding import Mesh, PartitionSpec as P

EMBED_SIZE = 8192
GATE_INNER_SIZE = 14336
N_ROW = 16
N_CHIP = 16
ROW = ("xh", "z")
CHIP = ("xl", "y")
EXTRA = 16
LANES = 128
VMEM = pl.BlockSpec(memory_space=pltpu.VMEM)
PARAMS = pltpu.CompilerParams(vmem_limit_bytes=40 * 1024 * 1024)


def cost(flops, bytes_accessed):
    return pl.CostEstimate(flops=flops, bytes_accessed=bytes_accessed, transcendentals=0)


def contract_last(left, right):
    return lax.dot_general(
        left, right, (((1,), (1,)), ((), ())), preferred_element_type=jnp.float32
    )


def contract_first(left, right):
    return lax.dot_general(
        left, right, (((0,), (0,)), ((), ())), preferred_element_type=jnp.float32
    )


def matmul(left, right):
    return lax.dot_general(
        left, right, (((1,), (0,)), ((), ())), preferred_element_type=jnp.float32
    )


def swiglu_grads(grad_hidden, gate_pre, up_pre):
    gate_f = gate_pre.astype(jnp.float32)
    up_f = up_pre.astype(jnp.float32)
    sigma = jax.nn.sigmoid(gate_f)
    silu_gate = gate_f * sigma
    grad_gpre = (grad_hidden * up_f * sigma * (1.0 + gate_f * (1.0 - sigma))).astype(jnp.bfloat16)
    grad_upre = (grad_hidden * silu_gate).astype(jnp.bfloat16)
    hidden = (silu_gate * up_f).astype(jnp.bfloat16)
    return (grad_gpre, grad_upre, hidden)


def swapped(values):
    return lax.ppermute(values, "core", [(0, 1), (1, 0)])


def payload_kernel(out_ref, tokens_ref, gate_ref, up_ref, down_ref, pre_ref, sent_ref):
    rows, width = out_ref.shape
    pieces = []
    for ref in (gate_ref, up_ref, down_ref):
        total = jnp.sum(jnp.abs(ref[...].astype(jnp.float32)), axis=0, keepdims=True)
        total = jnp.broadcast_to(jnp.sum(total, axis=1, keepdims=True), (1, width))
        for _ in range(3):
            piece = total.astype(jnp.bfloat16).astype(jnp.float32)
            pieces.append(piece)
            total = total - piece
    pieces.append(jnp.zeros((EXTRA - len(pieces), width), jnp.float32))
    extra = jnp.concatenate(pieces, axis=0).astype(jnp.bfloat16)
    out_rows = out_ref[...]
    token_rows = tokens_ref[...]
    for k in range(N_CHIP):
        sent_ref[k, 0:rows, :] = out_rows
        sent_ref[k, rows : 2 * rows, :] = token_rows
        sent_ref[k, 2 * rows :, :] = extra


def payload(grad_out, tokens, gate_t, up_t, down, pre_rows):
    rows, width = grad_out.shape
    return pl.pallas_call(
        payload_kernel,
        out_shape=jax.ShapeDtypeStruct((N_CHIP, 2 * rows + EXTRA, width), jnp.bfloat16),
        in_specs=[VMEM] * 5 + [pl.BlockSpec(memory_space=pl.ANY)],
        out_specs=VMEM,
        compiler_params=PARAMS,
        cost_estimate=cost(1 << 20, 3 << 20),
    )(grad_out, tokens, gate_t, up_t, down, pre_rows)


def tile_kernel(extra_ref, tile_ref):
    total = jnp.sum(extra_ref[...].astype(jnp.float32), axis=0)
    sums = [jnp.sum(total[3 * k : 3 * k + 3], axis=0, keepdims=True) for k in range(3)]
    tile = jnp.concatenate(sums + [jnp.zeros((5, LANES), jnp.float32)], axis=0)
    tile_ref[...] = jnp.broadcast_to(tile[None], tile_ref.shape)


def sums_tile(received):
    rows = received.shape[1] - EXTRA
    return pl.pallas_call(
        tile_kernel,
        grid=(1,),
        out_shape=jax.ShapeDtypeStruct((2 * N_ROW, 8, LANES), jnp.float32),
        in_specs=[pl.BlockSpec((N_CHIP, EXTRA, LANES), lambda i: (0, rows // EXTRA, 0))],
        out_specs=pl.BlockSpec((2 * N_ROW, 8, LANES), lambda i: (0, 0, 0)),
        compiler_params=PARAMS,
        cost_estimate=cost(1 << 16, 1 << 18),
    )(received)


def scale_of(tile_ref, which):
    total = jnp.sum(tile_ref[...], axis=0)[which : which + 1, 0:1]
    return total / float(EMBED_SIZE * GATE_INNER_SIZE) + 1e-05


def clipped(values, scale):
    return jnp.clip(values.astype(jnp.float32), -scale, scale).astype(jnp.bfloat16)


def partial_kernel(tile_ref, received_ref, down_ref, other_ref, partial_ref, halves_ref, quant_ref):
    rows = partial_ref.shape[1]
    inner, width = down_ref.shape

    @pl.when(pl.program_id(0) == 0)
    def _():
        scale = scale_of(tile_ref, 2)
        quant_ref[0:inner, :] = clipped(down_ref[...], scale)
        quant_ref[inner:, :] = clipped(other_ref[...], scale)

    out_rows = received_ref[:, 0:rows, :].reshape((-1, width))
    halves_ref[0] = out_rows
    halves_ref[1] = received_ref[:, rows : 2 * rows, :].reshape((-1, width))
    partial = contract_last(out_rows, quant_ref[...])
    partial_ref[...] = partial.astype(jnp.bfloat16).reshape(partial_ref.shape)


def hidden_partial(tile, received, down, other):
    blocks, steps = 4, N_CHIP // 4
    rows = (received.shape[1] - EXTRA) // 2
    inner, width = down.shape
    whole = pl.BlockSpec((inner, width), lambda i: (0, 0))
    return pl.pallas_call(
        partial_kernel,
        grid=(steps,),
        out_shape=(
            jax.ShapeDtypeStruct((N_ROW, rows, 2 * inner), jnp.bfloat16),
            jax.ShapeDtypeStruct((2, N_CHIP * rows, width), jnp.bfloat16),
        ),
        in_specs=[
            pl.BlockSpec(tile.shape, lambda i: (0, 0, 0)),
            pl.BlockSpec((blocks, 2 * rows + EXTRA, width), lambda i: (i, 0, 0)),
            whole,
            whole,
        ],
        out_specs=(
            pl.BlockSpec((blocks, rows, 2 * inner), lambda i: (i, 0, 0)),
            pl.BlockSpec((2, blocks * rows, width), lambda i: (0, i, 0)),
        ),
        scratch_shapes=[pltpu.VMEM((2 * inner, width), jnp.bfloat16)],
        compiler_params=PARAMS,
        cost_estimate=cost(2 * 512 * 896 * 512, 4 << 20),
    )(tile, received, down, other)


def spread_kernel(parts_ref, sent_ref):
    total = jnp.sum(parts_ref[...].astype(jnp.float32), axis=0).astype(jnp.bfloat16)
    for k in range(N_ROW):
        sent_ref[k] = total


def spread(parts):
    return pl.pallas_call(
        spread_kernel,
        out_shape=jax.ShapeDtypeStruct(parts.shape, jnp.bfloat16),
        in_specs=[VMEM],
        out_specs=VMEM,
        compiler_params=PARAMS,
        cost_estimate=cost(1 << 19, 2 << 20),
    )(parts)


def act_kernel(tile_ref, hid_ref, pre_ref, gate_ref, up_ref, other_ref, partial_ref, own_ref, sent_ref, quant_ref):
    inner, width = gate_ref.shape

    @pl.when(pl.program_id(0) == 0)
    def _():
        for n, ref in enumerate((gate_ref, up_ref)):
            scale = scale_of(tile_ref, n)
            quant_ref[n, 0:inner, :] = clipped(ref[...], scale)
            quant_ref[n, inner:, :] = clipped(other_ref[n], scale)

    grad_hidden = hid_ref[...].reshape((-1, 2 * inner)).astype(jnp.float32)
    acts = swiglu_grads(grad_hidden, pre_ref[:, : 2 * inner], pre_ref[:, 2 * inner :])
    partial = matmul(acts[0], quant_ref[0]) + matmul(acts[1], quant_ref[1])
    partial_ref[...] = partial.astype(jnp.bfloat16).reshape(partial_ref.shape)
    for n, act in enumerate(acts):
        own_ref[n] = act[:, :inner]
        sent_ref[n] = act[:, inner:]


def act_partial(tile, grad_hidden, pre_half, gate_t, up_t, other):
    blocks, steps = 4, N_ROW // 4
    rows = grad_hidden.shape[1]
    inner, width = gate_t.shape
    whole = pl.BlockSpec((inner, width), lambda i: (0, 0))
    halves = jax.ShapeDtypeStruct((3, N_ROW * rows, inner), jnp.bfloat16)
    half = pl.BlockSpec((3, blocks * rows, inner), lambda i: (0, i, 0))
    return pl.pallas_call(
        act_kernel,
        grid=(steps,),
        out_shape=(jax.ShapeDtypeStruct((N_CHIP, rows, width), jnp.bfloat16), halves, halves),
        in_specs=[
            pl.BlockSpec(tile.shape, lambda i: (0, 0, 0)),
            pl.BlockSpec((blocks, rows, 2 * inner), lambda i: (i, 0, 0)),
            pl.BlockSpec((blocks * rows, 4 * inner), lambda i: (i, 0)),
            whole,
            whole,
            pl.BlockSpec(other.shape, lambda i: (0, 0, 0)),
        ],
        out_specs=(pl.BlockSpec((blocks, rows, width), lambda i: (i, 0, 0)), half, half),
        scratch_shapes=[pltpu.VMEM((2, 2 * inner, width), jnp.bfloat16)],
        compiler_params=PARAMS,
        cost_estimate=cost(4 * 512 * 896 * 512, 9 << 20),
    )(tile, grad_hidden, pre_half, gate_t, up_t, other)


def shards(tokens, grad_out, gate_pre, up_pre, gate_latent, up_latent, down_latent):
    core = lax.axis_index("core")
    rows = tokens.shape[0]
    inner = gate_pre.shape[1]

    pre = jnp.concatenate([gate_pre, up_pre], axis=1).reshape((2, rows, 2 * inner))
    pre_own = lax.dynamic_index_in_dim(pre, core, 0, keepdims=False)
    pre_other = swapped(lax.dynamic_index_in_dim(pre, 1 - core, 0, keepdims=False))
    pre_rows = jnp.concatenate(
        [pre_own[:, :inner], pre_other[:, :inner], pre_own[:, inner:], pre_other[:, inner:]], axis=1
    )
    pre_half = lax.all_gather(pre_rows, ROW, axis=0, tiled=True)

    gate_t, up_t = gate_latent.T, up_latent.T
    sent = payload(grad_out, tokens, gate_t, up_t, down_latent, pre_rows)
    received = lax.all_to_all(sent, CHIP, 0, 0)
    down_other = swapped(down_latent)
    tile = lax.all_to_all(sums_tile(received), ROW + ("core",), 0, 0)

    partial, halves = hidden_partial(tile, received, down_latent, down_other)
    parts = lax.all_to_all(partial, ROW, 0, 0)
    gate_s, up_s, halves = lax.optimization_barrier((gate_t, up_t, halves))
    other_halves = swapped(halves)
    other_latents = swapped(jnp.stack([gate_s, up_s]))
    grad_hidden = lax.all_to_all(spread(parts), ROW, 0, 0)

    partial, own, sent = act_partial(tile, grad_hidden, pre_half, gate_t, up_t, other_latents)
    parts = lax.all_to_all(partial, CHIP, 0, 0)
    other = swapped(sent)

    def over_tokens(act, half):
        return (
            contract_first(own[act], halves[half]) + contract_first(other[act], other_halves[half])
        ).astype(jnp.bfloat16)

    grad_gate = over_tokens(0, 1).T
    grad_up = over_tokens(1, 1).T
    grad_down = over_tokens(2, 0)
    grad_tokens = jnp.sum(parts.astype(jnp.float32), axis=0).astype(jnp.bfloat16)
    return (grad_tokens, grad_gate, grad_up, grad_down)


def solution(mesh):
    fine = Mesh(mesh.devices.reshape((2, 8, 2, 8, 2)), ROW + CHIP + ("core",))
    col = CHIP + ("core",)
    in_specs = (
        P(col, ROW),
        P(col, ROW),
        P(ROW, col),
        P(ROW, col),
        P(ROW, col),
        P(ROW, col),
        P(col, ROW),
    )
    out_specs = (P(col, ROW), P(ROW, col), P(ROW, col), P(col, ROW))
    return jax.shard_map(shards, mesh=fine, in_specs=in_specs, out_specs=out_specs, check_vma=False)
```

```python
import jax
import jax.numpy as jnp
from jax import lax
from jax.experimental import pallas as pl
from jax.experimental.pallas import tpu as pltpu
from jax.sharding import Mesh, PartitionSpec as P

EMBED_SIZE = 8192
GATE_INNER_SIZE = 14336
N_ROW = 16
N_CHIP = 16
ROW = ("xh", "z")
CHIP = ("xl", "y")
EXTRA = 16
LANES = 128
VMEM = pl.BlockSpec(memory_space=pltpu.VMEM)
ANY = pl.BlockSpec(memory_space=pl.ANY)
PARAMS = pltpu.CompilerParams(vmem_limit_bytes=40 * 1024 * 1024)


def cost(flops, bytes_accessed):
    return pl.CostEstimate(flops=flops, bytes_accessed=bytes_accessed, transcendentals=0)


def contract_last(left, right):
    return lax.dot_general(
        left, right, (((1,), (1,)), ((), ())), preferred_element_type=jnp.float32
    )


def contract_first(left, right):
    return lax.dot_general(
        left, right, (((0,), (0,)), ((), ())), preferred_element_type=jnp.float32
    )


def matmul(left, right):
    return lax.dot_general(
        left, right, (((1,), (0,)), ((), ())), preferred_element_type=jnp.float32
    )


def swiglu_grads(grad_hidden, gate_pre, up_pre):
    gate_f = gate_pre.astype(jnp.float32)
    up_f = up_pre.astype(jnp.float32)
    sigma = jax.nn.sigmoid(gate_f)
    silu_gate = gate_f * sigma
    grad_gpre = (grad_hidden * up_f * sigma * (1.0 + gate_f * (1.0 - sigma))).astype(jnp.bfloat16)
    grad_upre = (grad_hidden * silu_gate).astype(jnp.bfloat16)
    hidden = (silu_gate * up_f).astype(jnp.bfloat16)
    return (grad_gpre, grad_upre, hidden)


def swapped(values):
    return lax.ppermute(values, "core", [(0, 1), (1, 0)])


def payload_kernel(out_ref, tokens_ref, gate_ref, up_ref, down_ref, sent_ref):
    rows, width = out_ref.shape
    pieces = []
    for ref in (gate_ref, up_ref, down_ref):
        total = jnp.sum(jnp.abs(ref[...].astype(jnp.float32)), axis=0, keepdims=True)
        total = jnp.broadcast_to(jnp.sum(total, axis=1, keepdims=True), (1, width))
        for _ in range(3):
            piece = total.astype(jnp.bfloat16).astype(jnp.float32)
            pieces.append(piece)
            total = total - piece
    pieces.append(jnp.zeros((EXTRA - len(pieces), width), jnp.float32))
    extra = jnp.concatenate(pieces, axis=0).astype(jnp.bfloat16)
    out_rows = out_ref[...]
    token_rows = tokens_ref[...]
    for k in range(N_CHIP):
        sent_ref[k, 0:rows, :] = out_rows
        sent_ref[k, rows : 2 * rows, :] = token_rows
        sent_ref[k, 2 * rows :, :] = extra


def payload(grad_out, tokens, gate_t, up_t, down):
    rows, width = grad_out.shape
    return pl.pallas_call(
        payload_kernel,
        out_shape=jax.ShapeDtypeStruct((N_CHIP, 2 * rows + EXTRA, width), jnp.bfloat16),
        in_specs=[VMEM] * 5,
        out_specs=VMEM,
        compiler_params=PARAMS,
        cost_estimate=cost(1 << 20, 3 << 20),
    )(grad_out, tokens, gate_t, up_t, down)


def tile_kernel(extra_ref, tile_ref):
    total = jnp.sum(extra_ref[...].astype(jnp.float32), axis=0)
    sums = [jnp.sum(total[3 * k : 3 * k + 3], axis=0, keepdims=True) for k in range(3)]
    tile = jnp.concatenate(sums + [jnp.zeros((5, LANES), jnp.float32)], axis=0)
    tile_ref[...] = jnp.broadcast_to(tile[None], tile_ref.shape)


def sums_tile(received):
    rows = received.shape[1] - EXTRA
    return pl.pallas_call(
        tile_kernel,
        grid=(1,),
        out_shape=jax.ShapeDtypeStruct((2 * N_ROW, 8, LANES), jnp.float32),
        in_specs=[pl.BlockSpec((N_CHIP, EXTRA, LANES), lambda i: (0, rows // EXTRA, 0))],
        out_specs=pl.BlockSpec((2 * N_ROW, 8, LANES), lambda i: (0, 0, 0)),
        compiler_params=PARAMS,
        cost_estimate=cost(1 << 16, 1 << 18),
    )(received)


def scale_of(tile_ref, which):
    total = jnp.sum(tile_ref[...], axis=0)[which : which + 1, 0:1]
    return total / float(EMBED_SIZE * GATE_INNER_SIZE) + 1e-05


def clipped(values, scale):
    return jnp.clip(values.astype(jnp.float32), -scale, scale).astype(jnp.bfloat16)


def partial_kernel(tile_ref, received_ref, down_ref, other_ref, partial_ref, halves_ref, quant_ref):
    rows = partial_ref.shape[1]
    inner, width = down_ref.shape

    @pl.when(pl.program_id(0) == 0)
    def _():
        scale = scale_of(tile_ref, 2)
        quant_ref[0:inner, :] = clipped(down_ref[...], scale)
        quant_ref[inner:, :] = clipped(other_ref[...], scale)

    out_rows = received_ref[:, 0:rows, :].reshape((-1, width))
    halves_ref[0] = out_rows
    halves_ref[1] = received_ref[:, rows : 2 * rows, :].reshape((-1, width))
    partial = contract_last(out_rows, quant_ref[...])
    partial_ref[...] = partial.astype(jnp.bfloat16).reshape(partial_ref.shape)


def hidden_partial(tile, received, down, other):
    blocks, steps = 4, N_CHIP // 4
    rows = (received.shape[1] - EXTRA) // 2
    inner, width = down.shape
    whole = pl.BlockSpec((inner, width), lambda i: (0, 0))
    return pl.pallas_call(
        partial_kernel,
        grid=(steps,),
        out_shape=(
            jax.ShapeDtypeStruct((N_ROW, rows, 2 * inner), jnp.bfloat16),
            jax.ShapeDtypeStruct((2, N_CHIP * rows, width), jnp.bfloat16),
        ),
        in_specs=[
            pl.BlockSpec(tile.shape, lambda i: (0, 0, 0)),
            pl.BlockSpec((blocks, 2 * rows + EXTRA, width), lambda i: (i, 0, 0)),
            whole,
            whole,
        ],
        out_specs=(
            pl.BlockSpec((blocks, rows, 2 * inner), lambda i: (i, 0, 0)),
            pl.BlockSpec((2, blocks * rows, width), lambda i: (0, i, 0)),
        ),
        scratch_shapes=[pltpu.VMEM((2 * inner, width), jnp.bfloat16)],
        compiler_params=PARAMS,
        cost_estimate=cost(2 * 512 * 896 * 512, 4 << 20),
    )(tile, received, down, other)


def spread_kernel(parts_ref, sent_ref):
    total = jnp.sum(parts_ref[...].astype(jnp.float32), axis=0).astype(jnp.bfloat16)
    for k in range(N_ROW):
        sent_ref[k] = total


def spread(parts):
    return pl.pallas_call(
        spread_kernel,
        out_shape=jax.ShapeDtypeStruct(parts.shape, jnp.bfloat16),
        in_specs=[VMEM],
        out_specs=VMEM,
        compiler_params=PARAMS,
        cost_estimate=cost(1 << 19, 2 << 20),
    )(parts)


def act_kernel(tile_ref, hid_ref, pre_ref, gate_ref, up_ref, other_ref, partial_ref, own_ref, sent_ref, quant_ref):
    inner, width = gate_ref.shape

    @pl.when(pl.program_id(0) == 0)
    def _():
        for n, ref in enumerate((gate_ref, up_ref)):
            scale = scale_of(tile_ref, n)
            quant_ref[n, 0:inner, :] = clipped(ref[...], scale)
            quant_ref[n, inner:, :] = clipped(other_ref[n], scale)

    grad_hidden = hid_ref[...].reshape((-1, 2 * inner)).astype(jnp.float32)
    acts = swiglu_grads(grad_hidden, pre_ref[:, : 2 * inner], pre_ref[:, 2 * inner :])
    partial = matmul(acts[0], quant_ref[0]) + matmul(acts[1], quant_ref[1])
    partial_ref[...] = partial.astype(jnp.bfloat16).reshape(partial_ref.shape)
    for n, act in enumerate(acts):
        own_ref[n] = act[:, : own_ref.shape[2]]
        sent_ref[n] = act[:, 2 * inner - sent_ref.shape[2] :]


def act_partial(tile, grad_hidden, pre_half, gate_t, up_t, other):
    blocks, steps = 4, N_ROW // 4
    rows = grad_hidden.shape[1]
    inner, width = gate_t.shape
    whole = pl.BlockSpec((inner, width), lambda i: (0, 0))
    lanes = -(-inner // LANES) * LANES
    halves = jax.ShapeDtypeStruct((3, N_ROW * rows, lanes), jnp.bfloat16)
    half = pl.BlockSpec((3, blocks * rows, lanes), lambda i: (0, i, 0))
    return pl.pallas_call(
        act_kernel,
        grid=(steps,),
        out_shape=(jax.ShapeDtypeStruct((N_CHIP, rows, width), jnp.bfloat16), halves, halves),
        in_specs=[
            pl.BlockSpec(tile.shape, lambda i: (0, 0, 0)),
            pl.BlockSpec((blocks, rows, 2 * inner), lambda i: (i, 0, 0)),
            pl.BlockSpec((blocks * rows, 4 * inner), lambda i: (i, 0)),
            whole,
            whole,
            pl.BlockSpec(other.shape, lambda i: (0, 0, 0)),
        ],
        out_specs=(pl.BlockSpec((blocks, rows, width), lambda i: (i, 0, 0)), half, half),
        scratch_shapes=[pltpu.VMEM((2, 2 * inner, width), jnp.bfloat16)],
        compiler_params=PARAMS,
        cost_estimate=cost(4 * 512 * 896 * 512, 9 << 20),
    )(tile, grad_hidden, pre_half, gate_t, up_t, other)


def latent_grads_kernel(own_ref, other_ref, halves_ref, other_halves_ref, *grad_refs):
    for n, grad_ref in enumerate(grad_refs):
        inner = grad_ref.shape[0]
        half = 0 if n == 2 else 1
        own = contract_first(own_ref[n], halves_ref[half])[:inner]
        other = contract_first(other_ref[n], other_halves_ref[half])[-inner:]
        grad_ref[...] = (own + other).astype(jnp.bfloat16)


def latent_grads(own, other, halves, other_halves, inner):
    grad = jax.ShapeDtypeStruct((inner, halves.shape[2]), jnp.bfloat16)
    return pl.pallas_call(
        latent_grads_kernel,
        out_shape=(grad, grad, grad),
        in_specs=[VMEM] * 4,
        out_specs=(VMEM, VMEM, VMEM),
        compiler_params=PARAMS,
        cost_estimate=cost(6 * 1024 * 512 * 512, 6 << 20),
    )(own, other, halves, other_halves)


def total_kernel(parts_ref, after_ref, total_ref):
    total_ref[...] = jnp.sum(parts_ref[...].astype(jnp.float32), axis=0).astype(jnp.bfloat16)


def total(parts, after):
    return pl.pallas_call(
        total_kernel,
        out_shape=jax.ShapeDtypeStruct(parts.shape[1:], jnp.bfloat16),
        in_specs=[VMEM, ANY],
        out_specs=VMEM,
        compiler_params=PARAMS,
        cost_estimate=cost(1 << 18, 1 << 19),
    )(parts, after)


def shards(tokens, grad_out, gate_pre, up_pre, gate_latent, up_latent, down_latent):
    core = lax.axis_index("core")
    rows, width = tokens.shape
    inner = gate_pre.shape[1]

    pre = jnp.concatenate([gate_pre, up_pre], axis=1).reshape((2, rows, 2 * inner))
    pre_own = lax.dynamic_index_in_dim(pre, core, 0, keepdims=False)
    pre_other = swapped(lax.dynamic_index_in_dim(pre, 1 - core, 0, keepdims=False))
    pre_rows = jnp.concatenate(
        [pre_own[:, :inner], pre_other[:, :inner], pre_own[:, inner:], pre_other[:, inner:]], axis=1
    )
    pre_half = lax.all_gather(pre_rows, ROW, axis=0, tiled=True)

    gate_t, up_t = gate_latent.T, up_latent.T
    sent = payload(grad_out, tokens, gate_t, up_t, down_latent)

    def exchanges(sent, gate_t, up_t, down):
        received = lax.all_to_all(sent, CHIP, 0, 0)
        down_other = swapped(down)
        tile = lax.all_to_all(sums_tile(received), ROW + ("core",), 0, 0)
        partial, halves = hidden_partial(tile, received, down, down_other)
        parts = lax.all_to_all(partial, ROW, 0, 0)
        other_halves = swapped(halves)
        other_latents = swapped(jnp.stack([gate_t, up_t]))
        grad_hidden = lax.all_to_all(spread(parts), ROW, 0, 0)
        return (tile, halves, other_halves, other_latents, grad_hidden)

    def nothing(sent, gate_t, up_t, down):
        shapes = jax.eval_shape(exchanges, sent, gate_t, up_t, down)
        return tuple(jnp.zeros(leaf.shape, leaf.dtype) for leaf in shapes)

    tile, halves, other_halves, other_latents, grad_hidden = lax.cond(
        lax.axis_index("z") < 8, exchanges, nothing, sent, gate_t, up_t, down_latent
    )

    partial, own, sent = act_partial(tile, grad_hidden, pre_half, gate_t, up_t, other_latents)
    parts = lax.all_to_all(partial, CHIP, 0, 0)
    grad_gate, grad_up, grad_down = latent_grads(own, swapped(sent), halves, other_halves, inner)
    grad_tokens = total(parts, grad_down)
    return (grad_tokens, grad_gate.T, grad_up.T, grad_down)


def solution(mesh):
    fine = Mesh(mesh.devices.reshape((2, 8, 2, 8, 2)), ROW + CHIP + ("core",))
    col = CHIP + ("core",)
    in_specs = (
        P(col, ROW),
        P(col, ROW),
        P(ROW, col),
        P(ROW, col),
        P(ROW, col),
        P(ROW, col),
        P(col, ROW),
    )
    out_specs = (P(col, ROW), P(ROW, col), P(ROW, col), P(col, ROW))
    return jax.shard_map(shards, mesh=fine, in_specs=in_specs, out_specs=out_specs, check_vma=False)
```

```python
import jax
import jax.numpy as jnp
from jax import lax
from jax.experimental import pallas as pl
from jax.experimental.pallas import tpu as pltpu
from jax.sharding import Mesh, PartitionSpec as P

EMBED_SIZE = 8192
GATE_INNER_SIZE = 14336
N_ROW = 16
N_CHIP = 16
ROW = ("xh", "z")
CHIP = ("xl", "y")
EXTRA = 16
N_Y = 8
LANES = 128
VMEM = pl.BlockSpec(memory_space=pltpu.VMEM)
SMEM = pl.BlockSpec(memory_space=pltpu.SMEM)
PARAMS = pltpu.CompilerParams(vmem_limit_bytes=40 * 1024 * 1024)


def cost(flops, bytes_accessed):
    return pl.CostEstimate(flops=flops, bytes_accessed=bytes_accessed, transcendentals=0)


def contract_last(left, right):
    return lax.dot_general(
        left, right, (((1,), (1,)), ((), ())), preferred_element_type=jnp.float32
    )


def contract_first(left, right):
    return lax.dot_general(
        left, right, (((0,), (0,)), ((), ())), preferred_element_type=jnp.float32
    )


def matmul(left, right):
    return lax.dot_general(
        left, right, (((1,), (0,)), ((), ())), preferred_element_type=jnp.float32
    )


def swiglu_grads(grad_hidden, gate_pre, up_pre):
    gate_f = gate_pre.astype(jnp.float32)
    up_f = up_pre.astype(jnp.float32)
    sigma = jax.nn.sigmoid(gate_f)
    silu_gate = gate_f * sigma
    grad_gpre = (grad_hidden * up_f * sigma * (1.0 + gate_f * (1.0 - sigma))).astype(jnp.bfloat16)
    grad_upre = (grad_hidden * silu_gate).astype(jnp.bfloat16)
    hidden = (silu_gate * up_f).astype(jnp.bfloat16)
    return (grad_gpre, grad_upre, hidden)


def swapped(values):
    return lax.ppermute(values, "core", [(0, 1), (1, 0)])


def pieces_of(totals):
    pieces = []
    for total in totals:
        for _ in range(3):
            piece = total.astype(jnp.bfloat16).astype(jnp.float32)
            pieces.append(piece)
            total = total - piece
    pieces.append(jnp.zeros((EXTRA - len(pieces), totals[0].shape[1]), jnp.float32))
    return jnp.concatenate(pieces, axis=0).astype(jnp.bfloat16)


def totals_of(pieces):
    return [jnp.sum(pieces[3 * k : 3 * k + 3], axis=0, keepdims=True) for k in range(3)]


def half_of(ref, core):
    rows = ref.shape[0] // 2
    return ref[pl.ds(pl.multiple_of(core * rows, rows), rows), :]


def first_kernel(core_ref, gate_pre_ref, up_pre_ref, gate_ref, up_ref, down_ref, sent_ref, sums_ref):
    rows, inner = gate_pre_ref.shape[0] // 2, gate_pre_ref.shape[1]
    lanes = sent_ref.shape[1] // 2
    sums = []
    for ref in (gate_ref, up_ref, down_ref):
        total = jnp.sum(jnp.abs(ref[...].astype(jnp.float32)), axis=0, keepdims=True)
        sums.append(jnp.broadcast_to(jnp.sum(total, axis=1, keepdims=True), (1, 2 * lanes)))
    sent_ref[...] = jnp.zeros(sent_ref.shape, sent_ref.dtype)
    sent_ref[0:rows, 0:inner] = half_of(gate_pre_ref, 1 - core_ref[0])
    sent_ref[0:rows, lanes : lanes + inner] = half_of(up_pre_ref, 1 - core_ref[0])
    sent_ref[rows:, :] = pieces_of(sums)
    tile = jnp.concatenate(sums + [jnp.zeros((5, 2 * lanes), jnp.float32)], axis=0)
    sums_ref[...] = tile[:, :LANES]


def first(core, gate_pre, up_pre, gate_t, up_t, down):
    rows, inner = gate_pre.shape
    lanes = -(-inner // LANES) * LANES
    return pl.pallas_call(
        first_kernel,
        out_shape=(
            jax.ShapeDtypeStruct((rows // 2 + EXTRA, 2 * lanes), jnp.bfloat16),
            jax.ShapeDtypeStruct((8, LANES), jnp.float32),
        ),
        in_specs=[SMEM] + [VMEM] * 5,
        out_specs=(VMEM, VMEM),
        compiler_params=PARAMS,
        cost_estimate=cost(1 << 20, 3 << 19),
    )(core, gate_pre, up_pre, gate_t, up_t, down)


def second_kernel(core_ref, gate_pre_ref, up_pre_ref, other_ref, sums_ref, out_ref, pre_ref, sent_ref):
    rows, inner = gate_pre_ref.shape[0] // 2, gate_pre_ref.shape[1]
    lanes = other_ref.shape[1] // 2
    pre_ref[...] = jnp.concatenate(
        [
            half_of(gate_pre_ref, core_ref[0]),
            other_ref[0:rows, 0:inner],
            half_of(up_pre_ref, core_ref[0]),
            other_ref[0:rows, lanes : lanes + inner],
        ],
        axis=1,
    )
    others = totals_of(other_ref[rows:, :LANES].astype(jnp.float32))
    extra = pieces_of([sums_ref[n : n + 1, :] + others[n] for n in range(3)])
    blocks = [out_ref[:, j * LANES : (j + 1) * LANES] for j in range(out_ref.shape[1] // LANES)]
    block = jnp.concatenate(blocks + [extra], axis=0)
    for k in range(N_CHIP):
        sent_ref[k] = block


def second(core, gate_pre, up_pre, other, sums, grad_out):
    rows, width = grad_out.shape
    inner = gate_pre.shape[1]
    return pl.pallas_call(
        second_kernel,
        out_shape=(
            jax.ShapeDtypeStruct((rows, 4 * inner), jnp.bfloat16),
            jax.ShapeDtypeStruct((N_CHIP, rows * width // LANES + EXTRA, LANES), jnp.bfloat16),
        ),
        in_specs=[SMEM] + [VMEM] * 5,
        out_specs=(VMEM, VMEM),
        compiler_params=PARAMS,
        cost_estimate=cost(1 << 16, 1 << 20),
    )(core, gate_pre, up_pre, other, sums, grad_out)


def tile_kernel(extra_ref, tile_ref):
    sums = totals_of(jnp.sum(extra_ref[...].astype(jnp.float32), axis=0))
    tile = jnp.concatenate(sums + [jnp.zeros((5, LANES), jnp.float32)], axis=0)
    tile_ref[...] = jnp.broadcast_to(tile[None], tile_ref.shape)


def sums_tile(received):
    rows = received.shape[1] - EXTRA
    return pl.pallas_call(
        tile_kernel,
        grid=(1,),
        out_shape=jax.ShapeDtypeStruct((N_ROW, 8, LANES), jnp.float32),
        in_specs=[pl.BlockSpec((N_CHIP, EXTRA, LANES), lambda i: (0, rows // EXTRA, 0))],
        out_specs=pl.BlockSpec((N_ROW, 8, LANES), lambda i: (0, 0, 0)),
        compiler_params=PARAMS,
        cost_estimate=cost(1 << 16, 1 << 18),
    )(received)


def scale_of(tile_ref, which):
    total = jnp.sum(tile_ref[...], axis=0)[which : which + 1, 0:1]
    return total / float(EMBED_SIZE * GATE_INNER_SIZE) + 1e-05


def clipped(values, scale):
    return jnp.clip(values.astype(jnp.float32), -scale, scale).astype(jnp.bfloat16)


def partial_kernel(tile_ref, received_ref, down_ref, other_ref, partial_ref, out_ref, quant_ref):
    rows = partial_ref.shape[1]
    inner, width = down_ref.shape

    @pl.when(pl.program_id(0) == 0)
    def _():
        scale = scale_of(tile_ref, 2)
        quant_ref[0:inner, :] = clipped(down_ref[...], scale)
        quant_ref[inner:, :] = clipped(other_ref[...], scale)

    blocks = [received_ref[:, j * rows : (j + 1) * rows, :] for j in range(width // LANES)]
    out_rows = jnp.concatenate([block.reshape((-1, LANES)) for block in blocks], axis=1)
    out_ref[...] = out_rows
    partial = contract_last(out_rows, quant_ref[...])
    partial_ref[...] = partial.astype(jnp.bfloat16).reshape(partial_ref.shape)


def hidden_partial(tile, received, down, other):
    blocks, steps = 4, N_CHIP // 4
    inner, width = down.shape
    rows = (received.shape[1] - EXTRA) * LANES // width
    whole = pl.BlockSpec((inner, width), lambda i: (0, 0))
    return pl.pallas_call(
        partial_kernel,
        grid=(steps,),
        out_shape=(
            jax.ShapeDtypeStruct((N_ROW, rows, 2 * inner), jnp.bfloat16),
            jax.ShapeDtypeStruct((N_CHIP * rows, width), jnp.bfloat16),
        ),
        in_specs=[
            pl.BlockSpec(tile.shape, lambda i: (0, 0, 0)),
            pl.BlockSpec((blocks,) + received.shape[1:], lambda i: (i, 0, 0)),
            whole,
            whole,
        ],
        out_specs=(
            pl.BlockSpec((blocks, rows, 2 * inner), lambda i: (i, 0, 0)),
            pl.BlockSpec((blocks * rows, width), lambda i: (i, 0)),
        ),
        scratch_shapes=[pltpu.VMEM((2 * inner, width), jnp.bfloat16)],
        compiler_params=PARAMS,
        cost_estimate=cost(2 * 512 * 896 * 512, 4 << 20),
    )(tile, received, down, other)


def spread_kernel(parts_ref, sent_ref):
    total = jnp.sum(parts_ref[...].astype(jnp.float32), axis=0).astype(jnp.bfloat16)
    for k in range(N_ROW):
        sent_ref[k] = total


def spread(parts):
    return pl.pallas_call(
        spread_kernel,
        out_shape=jax.ShapeDtypeStruct(parts.shape, jnp.bfloat16),
        in_specs=[VMEM],
        out_specs=VMEM,
        compiler_params=PARAMS,
        cost_estimate=cost(1 << 19, 2 << 20),
    )(parts)


def clip_kernel(tile_ref, gate_ref, up_ref, other_ref, quant_ref):
    inner = gate_ref.shape[0]
    for n, ref in enumerate((gate_ref, up_ref)):
        scale = scale_of(tile_ref, n)
        quant_ref[n, 0:inner, :] = clipped(ref[...], scale)
        quant_ref[n, inner:, :] = clipped(other_ref[n], scale)


def clipped_latents(tile, gate_t, up_t, other):
    inner, width = gate_t.shape
    return pl.pallas_call(
        clip_kernel,
        out_shape=jax.ShapeDtypeStruct((2, 2 * inner, width), jnp.bfloat16),
        in_specs=[VMEM] * 4,
        out_specs=VMEM,
        compiler_params=PARAMS,
        cost_estimate=cost(1 << 20, 4 << 20),
    )(tile, gate_t, up_t, other)


def act_kernel(hid_ref, pre_ref, quant_ref, partial_ref, acts_ref):
    both = hid_ref.shape[2]
    grad_hidden = hid_ref[...].reshape((-1, both)).astype(jnp.float32)
    acts = swiglu_grads(grad_hidden, pre_ref[:, :both], pre_ref[:, both:])
    partial = matmul(acts[0], quant_ref[0]) + matmul(acts[1], quant_ref[1])
    partial_ref[...] = partial.astype(jnp.bfloat16).reshape(partial_ref.shape)
    for n, act in enumerate(acts):
        acts_ref[n] = act


def act_partial(grad_hidden, pre_half, quant):
    blocks, steps = 4, N_ROW // 4
    rows, both = grad_hidden.shape[1:]
    width = quant.shape[2]
    return pl.pallas_call(
        act_kernel,
        grid=(steps,),
        out_shape=(
            jax.ShapeDtypeStruct((N_CHIP, rows, width), jnp.bfloat16),
            jax.ShapeDtypeStruct((3, N_ROW * rows, both), jnp.bfloat16),
        ),
        in_specs=[
            pl.BlockSpec((blocks, rows, both), lambda i: (i, 0, 0)),
            pl.BlockSpec((blocks * rows, 2 * both), lambda i: (i, 0)),
            pl.BlockSpec(quant.shape, lambda i: (0, 0, 0)),
        ],
        out_specs=(
            pl.BlockSpec((blocks, rows, width), lambda i: (i, 0, 0)),
            pl.BlockSpec((3, blocks * rows, both), lambda i: (0, i, 0)),
        ),
        compiler_params=PARAMS,
        cost_estimate=cost(4 * 512 * 896 * 512, 8 << 20),
    )(grad_hidden, pre_half, quant)


def latent_grads_kernel(place_ref, acts_ref, out_ref, *refs):
    token_refs, (own_ref, sent_ref, rows_ref) = refs[:N_Y], refs[N_Y:]
    rows = token_refs[0].shape[1]
    for shift, ref in enumerate(token_refs):
        y = lax.rem(place_ref[1] + shift, N_Y)
        for flip in range(2):
            chip = lax.rem(place_ref[0] + flip, 2) * N_Y + y
            rows_ref[pl.ds(pl.multiple_of(chip * rows, rows), rows), :] = ref[flip]
    inner = own_ref.shape[1]
    for n in range(3):
        half = out_ref[...] if n == 2 else rows_ref[...]
        grad = contract_first(acts_ref[n], half)
        own_ref[n] = grad[:inner]
        sent_ref[n] = grad[inner:].astype(jnp.bfloat16)


def latent_grads(place, acts, out_half, token_blocks):
    inner, width = acts.shape[2] // 2, out_half.shape[1]
    return pl.pallas_call(
        latent_grads_kernel,
        out_shape=(
            jax.ShapeDtypeStruct((3, inner, width), jnp.float32),
            jax.ShapeDtypeStruct((3, inner, width), jnp.bfloat16),
        ),
        in_specs=[SMEM] + [VMEM] * (2 + N_Y),
        out_specs=(VMEM, VMEM),
        scratch_shapes=[pltpu.VMEM(out_half.shape, jnp.bfloat16)],
        compiler_params=PARAMS,
        cost_estimate=cost(6 * 512 * 896 * 512, 8 << 20),
    )(place, acts, out_half, *token_blocks)


def join_kernel(own_ref, other_ref, *refs):
    for n, ref in enumerate(refs[:3]):
        ref[...] = (own_ref[n] + other_ref[n].astype(jnp.float32)).astype(jnp.bfloat16)
    refs[3][...] = jnp.zeros(refs[3].shape, jnp.float32)


def join(own, other):
    grad = jax.ShapeDtypeStruct(own.shape[1:], jnp.bfloat16)
    return pl.pallas_call(
        join_kernel,
        out_shape=(grad, grad, grad, jax.ShapeDtypeStruct((8, LANES), jnp.float32)),
        in_specs=[VMEM] * 2,
        out_specs=(VMEM,) * 4,
        compiler_params=PARAMS,
        cost_estimate=cost(1 << 20, 5 << 20),
    )(own, other)


def total_kernel(parts_ref, after_ref, total_ref):
    total_ref[...] = jnp.sum(parts_ref[...].astype(jnp.float32), axis=0).astype(jnp.bfloat16)


def total(parts, after):
    return pl.pallas_call(
        total_kernel,
        out_shape=jax.ShapeDtypeStruct(parts.shape[1:], jnp.bfloat16),
        in_specs=[VMEM] * 2,
        out_specs=VMEM,
        compiler_params=PARAMS,
        cost_estimate=cost(1 << 18, 1 << 19),
    )(parts, after)


def in_branch(work, *operands):
    def nothing(*operands):
        shapes = jax.eval_shape(work, *operands)
        return tuple(jnp.zeros(leaf.shape, leaf.dtype) for leaf in shapes)

    def always(*operands):
        return tuple(work(*operands))

    return lax.cond(lax.axis_index("z") < 8, always, nothing, *operands)


def shards(tokens, grad_out, gate_pre, up_pre, gate_latent, up_latent, down_latent):
    core = lax.axis_index("core").astype(jnp.int32).reshape((1,))
    place = jnp.stack([lax.axis_index("xl"), lax.axis_index("y")]).astype(jnp.int32)

    gate_t, up_t = gate_latent.T, up_latent.T
    sent, sums = first(core, gate_pre, up_pre, gate_t, up_t, down_latent)
    pre_rows, sent = second(core, gate_pre, up_pre, swapped(sent), sums, grad_out)
    pre_half = lax.all_gather(pre_rows, ROW, axis=0, tiled=True)

    def exchanges(sent, tokens, gate_t, up_t, down):
        received = lax.all_to_all(sent, CHIP, 0, 0)
        down_other = swapped(down)
        tile = lax.all_to_all(sums_tile(received), ROW, 0, 0)
        partial, out_half = hidden_partial(tile, received, down, down_other)
        parts = lax.all_to_all(partial, ROW, 0, 0)
        other_latents = swapped(jnp.stack([gate_t, up_t]))
        quant = clipped_latents(tile, gate_t, up_t, other_latents)
        pair = jnp.stack([tokens, lax.ppermute(tokens, "xl", [(0, 1), (1, 0)])])
        token_blocks = [pair] + [
            lax.ppermute(pair, "y", [((y + shift) % N_Y, y) for y in range(N_Y)])
            for shift in range(1, N_Y)
        ]
        grad_hidden = lax.all_to_all(spread(parts), ROW, 0, 0)
        return (out_half, quant, grad_hidden) + tuple(token_blocks)

    out_half, quant, grad_hidden, *token_blocks = in_branch(
        exchanges, sent, tokens, gate_t, up_t, down_latent
    )

    partial, acts = act_partial(grad_hidden, pre_half, quant)
    parts = lax.all_to_all(partial, CHIP, 0, 0)

    def joined(place, acts, out_half, *token_blocks):
        own, sent = latent_grads(place, acts, out_half, token_blocks)
        return join(own, swapped(sent))

    grad_gate, grad_up, grad_down, done = in_branch(joined, place, acts, out_half, *token_blocks)
    grad_tokens = total(parts, done)
    return (grad_tokens, grad_gate.T, grad_up.T, grad_down)


def solution(mesh):
    fine = Mesh(mesh.devices.reshape((2, 8, 2, 8, 2)), ROW + CHIP + ("core",))
    col = CHIP + ("core",)
    in_specs = (
        P(col, ROW),
        P(col, ROW),
        P(ROW, col),
        P(ROW, col),
        P(ROW, col),
        P(ROW, col),
        P(col, ROW),
    )
    out_specs = (P(col, ROW), P(ROW, col), P(ROW, col), P(col, ROW))
    return jax.shard_map(shards, mesh=fine, in_specs=in_specs, out_specs=out_specs, check_vma=False)
```

```python
import jax
import jax.numpy as jnp
from jax import lax
from jax.experimental import pallas as pl
from jax.experimental.pallas import tpu as pltpu
from jax.sharding import Mesh, PartitionSpec as P

EMBED_SIZE = 8192
GATE_INNER_SIZE = 14336
N_ROW = 16
N_CHIP = 16
ROW = ("xh", "z")
CHIP = ("xl", "y")
EXTRA = 16
N_Y = 8
LANES = 128
VMEM = pl.BlockSpec(memory_space=pltpu.VMEM)
SMEM = pl.BlockSpec(memory_space=pltpu.SMEM)
WIDE = pltpu.CompilerParams(vmem_limit_bytes=58 * 1024 * 1024)
PARAMS = pltpu.CompilerParams(vmem_limit_bytes=40 * 1024 * 1024)


def cost(flops, bytes_accessed):
    return pl.CostEstimate(flops=flops, bytes_accessed=bytes_accessed, transcendentals=0)


def contract_last(left, right):
    return lax.dot_general(
        left, right, (((1,), (1,)), ((), ())), preferred_element_type=jnp.float32
    )


def contract_first(left, right):
    return lax.dot_general(
        left, right, (((0,), (0,)), ((), ())), preferred_element_type=jnp.float32
    )


def matmul(left, right):
    return lax.dot_general(
        left, right, (((1,), (0,)), ((), ())), preferred_element_type=jnp.float32
    )


def swiglu_grads(grad_hidden, gate_pre, up_pre):
    gate_f = gate_pre.astype(jnp.float32)
    up_f = up_pre.astype(jnp.float32)
    sigma = jax.nn.sigmoid(gate_f)
    silu_gate = gate_f * sigma
    grad_gpre = (grad_hidden * up_f * sigma * (1.0 + gate_f * (1.0 - sigma))).astype(jnp.bfloat16)
    grad_upre = (grad_hidden * silu_gate).astype(jnp.bfloat16)
    hidden = (silu_gate * up_f).astype(jnp.bfloat16)
    return (grad_gpre, grad_upre, hidden)


def swapped(values):
    return lax.ppermute(values, "core", [(0, 1), (1, 0)])


def pieces_of(totals):
    pieces = []
    for total in totals:
        for _ in range(3):
            piece = total.astype(jnp.bfloat16).astype(jnp.float32)
            pieces.append(piece)
            total = total - piece
    pieces.append(jnp.zeros((EXTRA - len(pieces), totals[0].shape[1]), jnp.float32))
    return jnp.concatenate(pieces, axis=0).astype(jnp.bfloat16)


def totals_of(pieces):
    return [jnp.sum(pieces[3 * k : 3 * k + 3], axis=0, keepdims=True) for k in range(3)]


def half_of(ref, core):
    rows = ref.shape[0] // 2
    return ref[pl.ds(pl.multiple_of(core * rows, rows), rows), :]


def first_kernel(core_ref, gate_pre_ref, up_pre_ref, gate_ref, up_ref, down_ref, sent_ref, sums_ref):
    rows, inner = gate_pre_ref.shape[0] // 2, gate_pre_ref.shape[1]
    lanes = sent_ref.shape[1] // 2
    sums = []
    for ref in (gate_ref, up_ref, down_ref):
        total = jnp.sum(jnp.abs(ref[...].astype(jnp.float32)), axis=0, keepdims=True)
        sums.append(jnp.broadcast_to(jnp.sum(total, axis=1, keepdims=True), (1, 2 * lanes)))
    sent_ref[...] = jnp.zeros(sent_ref.shape, sent_ref.dtype)
    sent_ref[0:rows, 0:inner] = half_of(gate_pre_ref, 1 - core_ref[0])
    sent_ref[0:rows, lanes : lanes + inner] = half_of(up_pre_ref, 1 - core_ref[0])
    sent_ref[rows:, :] = pieces_of(sums)
    tile = jnp.concatenate(sums + [jnp.zeros((5, 2 * lanes), jnp.float32)], axis=0)
    sums_ref[...] = tile[:, :LANES]


def first(core, gate_pre, up_pre, gate_t, up_t, down):
    rows, inner = gate_pre.shape
    lanes = -(-inner // LANES) * LANES
    return pl.pallas_call(
        first_kernel,
        out_shape=(
            jax.ShapeDtypeStruct((rows // 2 + EXTRA, 2 * lanes), jnp.bfloat16),
            jax.ShapeDtypeStruct((8, LANES), jnp.float32),
        ),
        in_specs=[SMEM] + [VMEM] * 5,
        out_specs=(VMEM, VMEM),
        compiler_params=WIDE,
        cost_estimate=cost(1 << 20, 3 << 19),
    )(core, gate_pre, up_pre, gate_t, up_t, down)


def second_kernel(core_ref, gate_pre_ref, up_pre_ref, other_ref, sums_ref, out_ref, pre_ref, sent_ref):
    rows, inner = gate_pre_ref.shape[0] // 2, gate_pre_ref.shape[1]
    lanes = other_ref.shape[1] // 2
    pre_ref[...] = jnp.concatenate(
        [
            half_of(gate_pre_ref, core_ref[0]),
            other_ref[0:rows, 0:inner],
            half_of(up_pre_ref, core_ref[0]),
            other_ref[0:rows, lanes : lanes + inner],
        ],
        axis=1,
    )
    others = totals_of(other_ref[rows:, :LANES].astype(jnp.float32))
    extra = pieces_of([sums_ref[n : n + 1, :] + others[n] for n in range(3)])
    blocks = [out_ref[:, j * LANES : (j + 1) * LANES] for j in range(out_ref.shape[1] // LANES)]
    block = jnp.concatenate(blocks + [extra], axis=0)
    for k in range(N_CHIP):
        sent_ref[k] = block


def second(core, gate_pre, up_pre, other, sums, grad_out):
    rows, width = grad_out.shape
    inner = gate_pre.shape[1]
    return pl.pallas_call(
        second_kernel,
        out_shape=(
            jax.ShapeDtypeStruct((rows, 4 * inner), jnp.bfloat16),
            jax.ShapeDtypeStruct((N_CHIP, rows * width // LANES + EXTRA, LANES), jnp.bfloat16),
        ),
        in_specs=[SMEM] + [VMEM] * 5,
        out_specs=(VMEM, VMEM),
        compiler_params=WIDE,
        cost_estimate=cost(1 << 16, 1 << 20),
    )(core, gate_pre, up_pre, other, sums, grad_out)


def tile_kernel(extra_ref, tile_ref):
    sums = totals_of(jnp.sum(extra_ref[...].astype(jnp.float32), axis=0))
    tile = jnp.concatenate(sums + [jnp.zeros((5, LANES), jnp.float32)], axis=0)
    tile_ref[...] = jnp.broadcast_to(tile[None], tile_ref.shape)


def sums_tile(received):
    rows = received.shape[1] - EXTRA
    return pl.pallas_call(
        tile_kernel,
        grid=(1,),
        out_shape=jax.ShapeDtypeStruct((N_ROW, 8, LANES), jnp.float32),
        in_specs=[pl.BlockSpec((N_CHIP, EXTRA, LANES), lambda i: (0, rows // EXTRA, 0))],
        out_specs=pl.BlockSpec((N_ROW, 8, LANES), lambda i: (0, 0, 0)),
        compiler_params=PARAMS,
        cost_estimate=cost(1 << 16, 1 << 18),
    )(received)


def scale_of(tile_ref, which):
    total = jnp.sum(tile_ref[...], axis=0)[which : which + 1, 0:1]
    return total / float(EMBED_SIZE * GATE_INNER_SIZE) + 1e-05


def clipped(values, scale):
    return jnp.clip(values.astype(jnp.float32), -scale, scale).astype(jnp.bfloat16)


def partial_kernel(tile_ref, received_ref, down_ref, other_ref, partial_ref, out_ref, done_ref, quant_ref):
    rows = partial_ref.shape[1]
    inner, width = down_ref.shape

    @pl.when(pl.program_id(0) == 0)
    def _():
        scale = scale_of(tile_ref, 2)
        quant_ref[0:inner, :] = clipped(down_ref[...], scale)
        quant_ref[inner:, :] = clipped(other_ref[...], scale)

    blocks = [received_ref[:, j * rows : (j + 1) * rows, :] for j in range(width // LANES)]
    out_rows = jnp.concatenate([block.reshape((-1, LANES)) for block in blocks], axis=1)
    out_ref[...] = out_rows
    done_ref[...] = jnp.zeros(done_ref.shape, jnp.float32)
    partial = contract_last(out_rows, quant_ref[...])
    partial_ref[...] = partial.astype(jnp.bfloat16).reshape(partial_ref.shape)


def hidden_partial(tile, received, down, other):
    blocks, steps = 4, N_CHIP // 4
    inner, width = down.shape
    rows = (received.shape[1] - EXTRA) * LANES // width
    whole = pl.BlockSpec((inner, width), lambda i: (0, 0))
    return pl.pallas_call(
        partial_kernel,
        grid=(steps,),
        out_shape=(
            jax.ShapeDtypeStruct((N_ROW, rows, 2 * inner), jnp.bfloat16),
            jax.ShapeDtypeStruct((N_CHIP * rows, width), jnp.bfloat16),
            jax.ShapeDtypeStruct((8, LANES), jnp.float32),
        ),
        in_specs=[
            pl.BlockSpec(tile.shape, lambda i: (0, 0, 0)),
            pl.BlockSpec((blocks,) + received.shape[1:], lambda i: (i, 0, 0)),
            whole,
            whole,
        ],
        out_specs=(
            pl.BlockSpec((blocks, rows, 2 * inner), lambda i: (i, 0, 0)),
            pl.BlockSpec((blocks * rows, width), lambda i: (i, 0)),
            pl.BlockSpec((8, LANES), lambda i: (0, 0)),
        ),
        scratch_shapes=[pltpu.VMEM((2 * inner, width), jnp.bfloat16)],
        compiler_params=PARAMS,
        cost_estimate=cost(2 * 512 * 896 * 512, 4 << 20),
    )(tile, received, down, other)


def spread_kernel(parts_ref, after_ref, sent_ref):
    total = jnp.sum(parts_ref[...].astype(jnp.float32), axis=0).astype(jnp.bfloat16)
    for k in range(N_ROW):
        sent_ref[k] = total


def spread(parts, after):
    return pl.pallas_call(
        spread_kernel,
        out_shape=jax.ShapeDtypeStruct(parts.shape, jnp.bfloat16),
        in_specs=[VMEM] * 2,
        out_specs=VMEM,
        compiler_params=PARAMS,
        cost_estimate=cost(1 << 19, 2 << 20),
    )(parts, after)


def clip_kernel(tile_ref, gate_ref, up_ref, other_ref, quant_ref):
    inner = gate_ref.shape[0]
    for n, ref in enumerate((gate_ref, up_ref)):
        scale = scale_of(tile_ref, n)
        quant_ref[n, 0:inner, :] = clipped(ref[...], scale)
        quant_ref[n, inner:, :] = clipped(other_ref[n], scale)


def clipped_latents(tile, gate_t, up_t, other):
    inner, width = gate_t.shape
    return pl.pallas_call(
        clip_kernel,
        out_shape=jax.ShapeDtypeStruct((2, 2 * inner, width), jnp.bfloat16),
        in_specs=[VMEM] * 4,
        out_specs=VMEM,
        compiler_params=PARAMS,
        cost_estimate=cost(1 << 20, 4 << 20),
    )(tile, gate_t, up_t, other)


def act_kernel(hid_ref, pre_ref, quant_ref, partial_ref, acts_ref):
    both = hid_ref.shape[2]
    grad_hidden = hid_ref[...].reshape((-1, both)).astype(jnp.float32)
    acts = swiglu_grads(grad_hidden, pre_ref[:, :both], pre_ref[:, both:])
    partial = matmul(acts[0], quant_ref[0]) + matmul(acts[1], quant_ref[1])
    partial_ref[...] = partial.astype(jnp.bfloat16).reshape(partial_ref.shape)
    for n, act in enumerate(acts):
        acts_ref[n] = act


def act_partial(grad_hidden, pre_half, quant):
    blocks, steps = 4, N_ROW // 4
    rows, both = grad_hidden.shape[1:]
    width = quant.shape[2]
    return pl.pallas_call(
        act_kernel,
        grid=(steps,),
        out_shape=(
            jax.ShapeDtypeStruct((N_CHIP, rows, width), jnp.bfloat16),
            jax.ShapeDtypeStruct((3, N_ROW * rows, both), jnp.bfloat16),
        ),
        in_specs=[
            pl.BlockSpec((blocks, rows, both), lambda i: (i, 0, 0)),
            pl.BlockSpec((blocks * rows, 2 * both), lambda i: (i, 0)),
            pl.BlockSpec(quant.shape, lambda i: (0, 0, 0)),
        ],
        out_specs=(
            pl.BlockSpec((blocks, rows, width), lambda i: (i, 0, 0)),
            pl.BlockSpec((3, blocks * rows, both), lambda i: (0, i, 0)),
        ),
        compiler_params=WIDE,
        cost_estimate=cost(4 * 512 * 896 * 512, 8 << 20),
    )(grad_hidden, pre_half, quant)


def latent_grads_kernel(place_ref, acts_ref, out_ref, tokens_ref, own_ref, sent_ref, rows_ref):
    rows = tokens_ref.shape[1]
    for block in range(2 * N_Y):
        flip, bits = block // N_Y, block % N_Y
        offset = 4 * (bits & 1) + (bits & 2) + bits // 4
        chip = (place_ref[0] ^ flip) * N_Y + (place_ref[1] ^ offset)
        rows_ref[pl.ds(pl.multiple_of(chip * rows, rows), rows), :] = tokens_ref[block]
    inner = own_ref.shape[1]
    for n in range(3):
        half = out_ref[...] if n == 2 else rows_ref[...]
        grad = contract_first(acts_ref[n], half)
        own_ref[n] = grad[:inner]
        sent_ref[n] = grad[inner:].astype(jnp.bfloat16)


def latent_grads(place, acts, out_half, token_blocks):
    inner, width = acts.shape[2] // 2, out_half.shape[1]
    return pl.pallas_call(
        latent_grads_kernel,
        out_shape=(
            jax.ShapeDtypeStruct((3, inner, width), jnp.float32),
            jax.ShapeDtypeStruct((3, inner, width), jnp.bfloat16),
        ),
        in_specs=[SMEM] + [VMEM] * 3,
        out_specs=(VMEM, VMEM),
        scratch_shapes=[pltpu.VMEM(out_half.shape, jnp.bfloat16)],
        compiler_params=PARAMS,
        cost_estimate=cost(6 * 512 * 896 * 512, 8 << 20),
    )(place, acts, out_half, token_blocks)


def join_kernel(own_ref, other_ref, *refs):
    for n, ref in enumerate(refs[:3]):
        ref[...] = (own_ref[n] + other_ref[n].astype(jnp.float32)).astype(jnp.bfloat16)
    refs[3][...] = jnp.zeros(refs[3].shape, jnp.float32)


def join(own, other):
    grad = jax.ShapeDtypeStruct(own.shape[1:], jnp.bfloat16)
    return pl.pallas_call(
        join_kernel,
        out_shape=(grad, grad, grad, jax.ShapeDtypeStruct((8, LANES), jnp.float32)),
        in_specs=[VMEM] * 2,
        out_specs=(VMEM,) * 4,
        compiler_params=PARAMS,
        cost_estimate=cost(1 << 20, 5 << 20),
    )(own, other)


def total_kernel(parts_ref, after_ref, total_ref):
    total_ref[...] = jnp.sum(parts_ref[...].astype(jnp.float32), axis=0).astype(jnp.bfloat16)


def total(parts, after):
    return pl.pallas_call(
        total_kernel,
        out_shape=jax.ShapeDtypeStruct(parts.shape[1:], jnp.bfloat16),
        in_specs=[VMEM] * 2,
        out_specs=VMEM,
        compiler_params=PARAMS,
        cost_estimate=cost(1 << 18, 1 << 19),
    )(parts, after)


def doubled(blocks, axis, step):
    count = 2 if axis == "xl" else N_Y
    other = lax.ppermute(blocks, axis, [(k, k ^ step) for k in range(count)])
    return jnp.concatenate([blocks, other], axis=0)


def copy_kernel(values_ref, after_ref, copy_ref):
    copy_ref[...] = values_ref[...]


def copy_after(values, after):
    return pl.pallas_call(
        copy_kernel,
        out_shape=jax.ShapeDtypeStruct(values.shape, values.dtype),
        in_specs=[VMEM] * 2,
        out_specs=VMEM,
        cost_estimate=cost(1, 1 << 16),
    )(values, after)


def tokens_along_y(tokens, done):
    blocks = copy_after(tokens, done)[None]
    for step in (4, 2, 1):
        blocks = doubled(blocks, "y", step)
    return blocks, blocks[-1, :EXTRA, :LANES]


def in_branch(work, *operands):
    def nothing(*operands):
        shapes = jax.eval_shape(work, *operands)
        return tuple(jnp.zeros(leaf.shape, leaf.dtype) for leaf in shapes)

    def always(*operands):
        return tuple(work(*operands))

    return lax.cond(lax.axis_index("z") < 8, always, nothing, *operands)


def shards(tokens, grad_out, gate_pre, up_pre, gate_latent, up_latent, down_latent):
    core = lax.axis_index("core").astype(jnp.int32).reshape((1,))
    place = jnp.stack([lax.axis_index("xl"), lax.axis_index("y")]).astype(jnp.int32)

    gate_t, up_t = gate_latent.T, up_latent.T
    sent, sums = first(core, gate_pre, up_pre, gate_t, up_t, down_latent)
    pre_rows, sent = second(core, gate_pre, up_pre, swapped(sent), sums, grad_out)
    pre_half = lax.all_gather(pre_rows, ROW, axis=0, tiled=True)

    def exchanges(sent, tokens, gate_t, up_t, down):
        received = lax.all_to_all(sent, CHIP, 0, 0)
        down_other = swapped(down)
        tile = lax.all_to_all(sums_tile(received), ROW, 0, 0)
        partial, out_half, done = hidden_partial(tile, received, down, down_other)
        parts = lax.all_to_all(partial, ROW, 0, 0)
        near_tokens, after = in_branch(tokens_along_y, tokens, done)
        other_latents = swapped(jnp.stack([gate_t, up_t]))
        quant = clipped_latents(tile, gate_t, up_t, other_latents)
        token_blocks = doubled(near_tokens, "xl", 1)
        grad_hidden = lax.all_to_all(spread(parts, after), ROW, 0, 0)
        return (out_half, quant, grad_hidden, token_blocks)

    out_half, quant, grad_hidden, token_blocks = in_branch(
        exchanges, sent, tokens, gate_t, up_t, down_latent
    )

    partial, acts = act_partial(grad_hidden, pre_half, quant)
    parts = lax.all_to_all(partial, CHIP, 0, 0)

    def joined(place, acts, out_half, token_blocks):
        own, sent = latent_grads(place, acts, out_half, token_blocks)
        return join(own, swapped(sent))

    grad_gate, grad_up, grad_down, done = in_branch(joined, place, acts, out_half, token_blocks)
    grad_tokens = total(parts, done)
    return (grad_tokens, grad_gate.T, grad_up.T, grad_down)


def solution(mesh):
    fine = Mesh(mesh.devices.reshape((2, 8, 2, 8, 2)), ROW + CHIP + ("core",))
    col = CHIP + ("core",)
    in_specs = (
        P(col, ROW),
        P(col, ROW),
        P(ROW, col),
        P(ROW, col),
        P(ROW, col),
        P(ROW, col),
        P(col, ROW),
    )
    out_specs = (P(col, ROW), P(ROW, col), P(ROW, col), P(col, ROW))
    return jax.shard_map(shards, mesh=fine, in_specs=in_specs, out_specs=out_specs, check_vma=False)
```

```python
import jax
import jax.numpy as jnp
from jax import lax
from jax.experimental import pallas as pl
from jax.experimental.pallas import tpu as pltpu
from jax.sharding import Mesh, PartitionSpec as P

EMBED_SIZE = 8192
GATE_INNER_SIZE = 14336
N_ROW = 16
N_CHIP = 16
ROW = ("xh", "z")
CHIP = ("xl", "y")
EXTRA = 16
N_Y = 8
LANES = 128
VMEM = pl.BlockSpec(memory_space=pltpu.VMEM)
SMEM = pl.BlockSpec(memory_space=pltpu.SMEM)
WIDE = pltpu.CompilerParams(vmem_limit_bytes=58 * 1024 * 1024)
PARAMS = pltpu.CompilerParams(vmem_limit_bytes=40 * 1024 * 1024)


def cost(flops, bytes_accessed):
    return pl.CostEstimate(flops=flops, bytes_accessed=bytes_accessed, transcendentals=0)


def contract_last(left, right):
    return lax.dot_general(
        left, right, (((1,), (1,)), ((), ())), preferred_element_type=jnp.float32
    )


def contract_first(left, right):
    return lax.dot_general(
        left, right, (((0,), (0,)), ((), ())), preferred_element_type=jnp.float32
    )


def matmul(left, right):
    return lax.dot_general(
        left, right, (((1,), (0,)), ((), ())), preferred_element_type=jnp.float32
    )


def swiglu_grads(grad_hidden, gate_pre, up_pre):
    gate_f = gate_pre.astype(jnp.float32)
    up_f = up_pre.astype(jnp.float32)
    sigma = jax.nn.sigmoid(gate_f)
    silu_gate = gate_f * sigma
    slope = sigma * (1.0 + gate_f - silu_gate)
    grad_gpre = (grad_hidden * (up_f * slope)).astype(jnp.bfloat16)
    grad_upre = (grad_hidden * silu_gate).astype(jnp.bfloat16)
    hidden = (silu_gate * up_f).astype(jnp.bfloat16)
    return (grad_gpre, grad_upre, hidden)


def swapped(values):
    return lax.ppermute(values, "core", [(0, 1), (1, 0)])


def pieces_of(totals):
    pieces = []
    for total in totals:
        for _ in range(3):
            piece = total.astype(jnp.bfloat16).astype(jnp.float32)
            pieces.append(piece)
            total = total - piece
    pieces.append(jnp.zeros((EXTRA - len(pieces), totals[0].shape[1]), jnp.float32))
    return jnp.concatenate(pieces, axis=0).astype(jnp.bfloat16)


def totals_of(pieces):
    return [jnp.sum(pieces[3 * k : 3 * k + 3], axis=0, keepdims=True) for k in range(3)]


def half_of(ref, core):
    rows = ref.shape[0] // 2
    return ref[pl.ds(pl.multiple_of(core * rows, rows), rows), :]


def first_kernel(core_ref, gate_pre_ref, up_pre_ref, gate_ref, up_ref, down_ref, sent_ref, sums_ref):
    rows, inner = gate_pre_ref.shape[0] // 2, gate_pre_ref.shape[1]
    lanes = sent_ref.shape[1] // 2
    sums = []
    for ref in (gate_ref, up_ref, down_ref):
        total = jnp.sum(jnp.abs(ref[...].astype(jnp.float32)), axis=0, keepdims=True)
        sums.append(jnp.broadcast_to(jnp.sum(total, axis=1, keepdims=True), (1, 2 * lanes)))
    sent_ref[...] = jnp.zeros(sent_ref.shape, sent_ref.dtype)
    sent_ref[0:rows, 0:inner] = half_of(gate_pre_ref, 1 - core_ref[0])
    sent_ref[0:rows, lanes : lanes + inner] = half_of(up_pre_ref, 1 - core_ref[0])
    sent_ref[rows:, :] = pieces_of(sums)
    tile = jnp.concatenate(sums + [jnp.zeros((5, 2 * lanes), jnp.float32)], axis=0)
    sums_ref[...] = tile[:, :LANES]


def first(core, gate_pre, up_pre, gate_t, up_t, down):
    rows, inner = gate_pre.shape
    lanes = -(-inner // LANES) * LANES
    return pl.pallas_call(
        first_kernel,
        out_shape=(
            jax.ShapeDtypeStruct((rows // 2 + EXTRA, 2 * lanes), jnp.bfloat16),
            jax.ShapeDtypeStruct((8, LANES), jnp.float32),
        ),
        in_specs=[SMEM] + [VMEM] * 5,
        out_specs=(VMEM, VMEM),
        compiler_params=WIDE,
        cost_estimate=cost(1 << 20, 3 << 19),
    )(core, gate_pre, up_pre, gate_t, up_t, down)


def second_kernel(core_ref, gate_pre_ref, up_pre_ref, other_ref, sums_ref, out_ref, pre_ref, sent_ref):
    rows, inner = gate_pre_ref.shape[0] // 2, gate_pre_ref.shape[1]
    lanes = other_ref.shape[1] // 2
    pre_ref[...] = jnp.concatenate(
        [
            half_of(gate_pre_ref, core_ref[0]),
            other_ref[0:rows, 0:inner],
            half_of(up_pre_ref, core_ref[0]),
            other_ref[0:rows, lanes : lanes + inner],
        ],
        axis=1,
    )
    others = totals_of(other_ref[rows:, :LANES].astype(jnp.float32))
    extra = pieces_of([sums_ref[n : n + 1, :] + others[n] for n in range(3)])
    blocks = [out_ref[:, j * LANES : (j + 1) * LANES] for j in range(out_ref.shape[1] // LANES)]
    block = jnp.concatenate(blocks + [extra], axis=0)
    for k in range(N_CHIP):
        sent_ref[k] = block


def second(core, gate_pre, up_pre, other, sums, grad_out):
    rows, width = grad_out.shape
    inner = gate_pre.shape[1]
    return pl.pallas_call(
        second_kernel,
        out_shape=(
            jax.ShapeDtypeStruct((rows, 4 * inner), jnp.bfloat16),
            jax.ShapeDtypeStruct((N_CHIP, rows * width // LANES + EXTRA, LANES), jnp.bfloat16),
        ),
        in_specs=[SMEM] + [VMEM] * 5,
        out_specs=(VMEM, VMEM),
        compiler_params=WIDE,
        cost_estimate=cost(1 << 16, 1 << 20),
    )(core, gate_pre, up_pre, other, sums, grad_out)


def tile_kernel(extra_ref, tile_ref):
    sums = totals_of(jnp.sum(extra_ref[...].astype(jnp.float32), axis=0))
    tile = jnp.concatenate(sums + [jnp.zeros((5, LANES), jnp.float32)], axis=0)
    tile_ref[...] = jnp.broadcast_to(tile[None], tile_ref.shape)


def sums_tile(received):
    rows = received.shape[1] - EXTRA
    return pl.pallas_call(
        tile_kernel,
        grid=(1,),
        out_shape=jax.ShapeDtypeStruct((N_ROW, 8, LANES), jnp.float32),
        in_specs=[pl.BlockSpec((N_CHIP, EXTRA, LANES), lambda i: (0, rows // EXTRA, 0))],
        out_specs=pl.BlockSpec((N_ROW, 8, LANES), lambda i: (0, 0, 0)),
        compiler_params=PARAMS,
        cost_estimate=cost(1 << 16, 1 << 18),
    )(received)


def scale_of(tile_ref, which):
    total = jnp.sum(tile_ref[...], axis=0)[which : which + 1, 0:1]
    return total / float(EMBED_SIZE * GATE_INNER_SIZE) + 1e-05


def clipped(values, scale):
    return jnp.clip(values.astype(jnp.float32), -scale, scale).astype(jnp.bfloat16)


def partial_kernel(tile_ref, received_ref, down_ref, other_ref, partial_ref, out_ref, done_ref, quant_ref):
    rows = partial_ref.shape[1]
    inner, width = down_ref.shape

    @pl.when(pl.program_id(0) == 0)
    def _():
        scale = scale_of(tile_ref, 2)
        quant_ref[0:inner, :] = clipped(down_ref[...], scale)
        quant_ref[inner:, :] = clipped(other_ref[...], scale)

    blocks = [received_ref[:, j * rows : (j + 1) * rows, :] for j in range(width // LANES)]
    out_rows = jnp.concatenate([block.reshape((-1, LANES)) for block in blocks], axis=1)
    out_ref[...] = out_rows
    done_ref[...] = jnp.zeros(done_ref.shape, jnp.float32)
    partial = contract_last(out_rows, quant_ref[...])
    partial_ref[...] = partial.astype(jnp.bfloat16).reshape(partial_ref.shape)


def hidden_partial(tile, received, down, other):
    blocks, steps = 4, N_CHIP // 4
    inner, width = down.shape
    rows = (received.shape[1] - EXTRA) * LANES // width
    whole = pl.BlockSpec((inner, width), lambda i: (0, 0))
    return pl.pallas_call(
        partial_kernel,
        grid=(steps,),
        out_shape=(
            jax.ShapeDtypeStruct((N_ROW, rows, 2 * inner), jnp.bfloat16),
            jax.ShapeDtypeStruct((N_CHIP * rows, width), jnp.bfloat16),
            jax.ShapeDtypeStruct((8, LANES), jnp.float32),
        ),
        in_specs=[
            pl.BlockSpec(tile.shape, lambda i: (0, 0, 0)),
            pl.BlockSpec((blocks,) + received.shape[1:], lambda i: (i, 0, 0)),
            whole,
            whole,
        ],
        out_specs=(
            pl.BlockSpec((blocks, rows, 2 * inner), lambda i: (i, 0, 0)),
            pl.BlockSpec((blocks * rows, width), lambda i: (i, 0)),
            pl.BlockSpec((8, LANES), lambda i: (0, 0)),
        ),
        scratch_shapes=[pltpu.VMEM((2 * inner, width), jnp.bfloat16)],
        compiler_params=PARAMS,
        cost_estimate=cost(2 * 512 * 896 * 512, 4 << 20),
    )(tile, received, down, other)


def spread_kernel(parts_ref, after_ref, sent_ref):
    total = jnp.sum(parts_ref[...].astype(jnp.float32), axis=0).astype(jnp.bfloat16)
    for k in range(N_ROW):
        sent_ref[k] = total


def spread(parts, after):
    return pl.pallas_call(
        spread_kernel,
        out_shape=jax.ShapeDtypeStruct(parts.shape, jnp.bfloat16),
        in_specs=[VMEM] * 2,
        out_specs=VMEM,
        compiler_params=PARAMS,
        cost_estimate=cost(1 << 19, 2 << 20),
    )(parts, after)


def clip_kernel(tile_ref, gate_ref, up_ref, other_ref, quant_ref):
    inner = gate_ref.shape[0]
    for n, ref in enumerate((gate_ref, up_ref)):
        scale = scale_of(tile_ref, n)
        quant_ref[n, 0:inner, :] = clipped(ref[...], scale)
        quant_ref[n, inner:, :] = clipped(other_ref[n], scale)


def clipped_latents(tile, gate_t, up_t, other):
    inner, width = gate_t.shape
    return pl.pallas_call(
        clip_kernel,
        out_shape=jax.ShapeDtypeStruct((2, 2 * inner, width), jnp.bfloat16),
        in_specs=[VMEM] * 4,
        out_specs=VMEM,
        compiler_params=PARAMS,
        cost_estimate=cost(1 << 20, 4 << 20),
    )(tile, gate_t, up_t, other)


def act_kernel(hid_ref, pre_ref, quant_ref, partial_ref, acts_ref):
    both = hid_ref.shape[2]
    grad_hidden = hid_ref[...].reshape((-1, both)).astype(jnp.float32)
    acts = swiglu_grads(grad_hidden, pre_ref[:, :both], pre_ref[:, both:])
    partial = matmul(acts[0], quant_ref[0]) + matmul(acts[1], quant_ref[1])
    partial_ref[...] = partial.astype(jnp.bfloat16).reshape(partial_ref.shape)
    for n, act in enumerate(acts):
        acts_ref[n] = act


def act_partial(grad_hidden, pre_half, quant):
    blocks, steps = 4, N_ROW // 4
    rows, both = grad_hidden.shape[1:]
    width = quant.shape[2]
    return pl.pallas_call(
        act_kernel,
        grid=(steps,),
        out_shape=(
            jax.ShapeDtypeStruct((N_CHIP, rows, width), jnp.bfloat16),
            jax.ShapeDtypeStruct((3, N_ROW * rows, both), jnp.bfloat16),
        ),
        in_specs=[
            pl.BlockSpec((blocks, rows, both), lambda i: (i, 0, 0)),
            pl.BlockSpec((blocks * rows, 2 * both), lambda i: (i, 0)),
            pl.BlockSpec(quant.shape, lambda i: (0, 0, 0)),
        ],
        out_specs=(
            pl.BlockSpec((blocks, rows, width), lambda i: (i, 0, 0)),
            pl.BlockSpec((3, blocks * rows, both), lambda i: (0, i, 0)),
        ),
        compiler_params=WIDE,
        cost_estimate=cost(4 * 512 * 896 * 512, 8 << 20),
    )(grad_hidden, pre_half, quant)


def latent_grads_kernel(place_ref, acts_ref, out_ref, tokens_ref, own_ref, sent_ref, rows_ref):
    rows = tokens_ref.shape[1]
    for block in range(2 * N_Y):
        flip, bits = block & 1, block >> 1
        offset = 4 * (bits & 1) + (bits & 2) + bits // 4
        chip = (place_ref[0] ^ flip) * N_Y + (place_ref[1] ^ offset)
        rows_ref[pl.ds(pl.multiple_of(chip * rows, rows), rows), :] = tokens_ref[block]
    inner = own_ref.shape[1]
    for n in range(3):
        half = out_ref[...] if n == 2 else rows_ref[...]
        grad = contract_first(acts_ref[n], half)
        own_ref[n] = grad[:inner]
        sent_ref[n] = grad[inner:].astype(jnp.bfloat16)


def latent_grads(place, acts, out_half, token_blocks):
    inner, width = acts.shape[2] // 2, out_half.shape[1]
    return pl.pallas_call(
        latent_grads_kernel,
        out_shape=(
            jax.ShapeDtypeStruct((3, inner, width), jnp.float32),
            jax.ShapeDtypeStruct((3, inner, width), jnp.bfloat16),
        ),
        in_specs=[SMEM] + [VMEM] * 3,
        out_specs=(VMEM, VMEM),
        scratch_shapes=[pltpu.VMEM(out_half.shape, jnp.bfloat16)],
        compiler_params=PARAMS,
        cost_estimate=cost(6 * 512 * 896 * 512, 8 << 20),
    )(place, acts, out_half, token_blocks)


def join_kernel(own_ref, other_ref, *refs):
    for n, ref in enumerate(refs[:3]):
        ref[...] = (own_ref[n] + other_ref[n].astype(jnp.float32)).astype(jnp.bfloat16)
    refs[3][...] = jnp.zeros(refs[3].shape, jnp.float32)


def join(own, other):
    grad = jax.ShapeDtypeStruct(own.shape[1:], jnp.bfloat16)
    return pl.pallas_call(
        join_kernel,
        out_shape=(grad, grad, grad, jax.ShapeDtypeStruct((8, LANES), jnp.float32)),
        in_specs=[VMEM] * 2,
        out_specs=(VMEM,) * 4,
        compiler_params=PARAMS,
        cost_estimate=cost(1 << 20, 5 << 20),
    )(own, other)


def total_kernel(parts_ref, after_ref, total_ref):
    total_ref[...] = jnp.sum(parts_ref[...].astype(jnp.float32), axis=0).astype(jnp.bfloat16)


def total(parts, after):
    return pl.pallas_call(
        total_kernel,
        out_shape=jax.ShapeDtypeStruct(parts.shape[1:], jnp.bfloat16),
        in_specs=[VMEM] * 2,
        out_specs=VMEM,
        compiler_params=PARAMS,
        cost_estimate=cost(1 << 18, 1 << 19),
    )(parts, after)


def doubled(blocks, axis, step):
    count = 2 if axis == "xl" else N_Y
    other = lax.ppermute(blocks, axis, [(k, k ^ step) for k in range(count)])
    return jnp.concatenate([blocks, other], axis=0)


def copy_kernel(values_ref, after_ref, copy_ref):
    copy_ref[...] = values_ref[...]


def copy_after(values, after):
    return pl.pallas_call(
        copy_kernel,
        out_shape=jax.ShapeDtypeStruct(values.shape, values.dtype),
        in_specs=[VMEM] * 2,
        out_specs=VMEM,
        cost_estimate=cost(1, 1 << 16),
    )(values, after)


def far_tokens(blocks, done):
    blocks = copy_after(blocks, done)
    for step in (4, 2):
        blocks = doubled(blocks, "y", step)
    return blocks, blocks[-1, :EXTRA, :LANES]


def in_branch(work, *operands):
    def nothing(*operands):
        shapes = jax.eval_shape(work, *operands)
        return tuple(jnp.zeros(leaf.shape, leaf.dtype) for leaf in shapes)

    def always(*operands):
        return tuple(work(*operands))

    return lax.cond(lax.axis_index("z") < 8, always, nothing, *operands)


def shards(tokens, grad_out, gate_pre, up_pre, gate_latent, up_latent, down_latent):
    core = lax.axis_index("core").astype(jnp.int32).reshape((1,))
    place = jnp.stack([lax.axis_index("xl"), lax.axis_index("y")]).astype(jnp.int32)

    gate_t, up_t = gate_latent.T, up_latent.T
    sent, sums = first(core, gate_pre, up_pre, gate_t, up_t, down_latent)
    pre_rows, sent = second(core, gate_pre, up_pre, swapped(sent), sums, grad_out)
    pre_half = lax.all_gather(pre_rows, ROW, axis=0, tiled=True)

    def exchanges(sent, tokens, gate_t, up_t, down):
        received = lax.all_to_all(sent, CHIP, 0, 0)
        down_other = swapped(down)
        pair = doubled(tokens[None], "xl", 1)
        tile = lax.all_to_all(sums_tile(received), ROW, 0, 0)
        partial, out_half, done = hidden_partial(tile, received, down, down_other)
        parts = lax.all_to_all(partial, ROW, 0, 0)
        most_tokens, after = in_branch(far_tokens, pair, done)
        other_latents = swapped(jnp.stack([gate_t, up_t]))
        quant = clipped_latents(tile, gate_t, up_t, other_latents)
        token_blocks = doubled(most_tokens, "y", 1)
        grad_hidden = lax.all_to_all(spread(parts, after), ROW, 0, 0)
        return (out_half, quant, grad_hidden, token_blocks)

    out_half, quant, grad_hidden, token_blocks = in_branch(
        exchanges, sent, tokens, gate_t, up_t, down_latent
    )

    partial, acts = act_partial(grad_hidden, pre_half, quant)
    parts = lax.all_to_all(partial, CHIP, 0, 0)

    def joined(place, acts, out_half, token_blocks):
        own, sent = latent_grads(place, acts, out_half, token_blocks)
        return join(own, swapped(sent))

    grad_gate, grad_up, grad_down, done = in_branch(joined, place, acts, out_half, token_blocks)
    grad_tokens = total(parts, done)
    return (grad_tokens, grad_gate.T, grad_up.T, grad_down)


def solution(mesh):
    fine = Mesh(mesh.devices.reshape((2, 8, 2, 8, 2)), ROW + CHIP + ("core",))
    col = CHIP + ("core",)
    in_specs = (
        P(col, ROW),
        P(col, ROW),
        P(ROW, col),
        P(ROW, col),
        P(ROW, col),
        P(ROW, col),
        P(col, ROW),
    )
    out_specs = (P(col, ROW), P(ROW, col), P(ROW, col), P(col, ROW))
    return jax.shard_map(shards, mesh=fine, in_specs=in_specs, out_specs=out_specs, check_vma=False)
```

```python
import jax
import jax.numpy as jnp
from jax import lax
from jax.experimental import pallas as pl
from jax.experimental.pallas import tpu as pltpu
from jax.sharding import Mesh, PartitionSpec as P

EMBED_SIZE = 8192
GATE_INNER_SIZE = 14336
N_ROW = 16
N_CHIP = 16
ROW = ("xh", "z")
CHIP = ("xl", "y")
EXTRA = 16
N_Y = 8
LANES = 128
VMEM = pl.BlockSpec(memory_space=pltpu.VMEM)
SMEM = pl.BlockSpec(memory_space=pltpu.SMEM)
WIDE = pltpu.CompilerParams(vmem_limit_bytes=58 * 1024 * 1024)
PARAMS = pltpu.CompilerParams(vmem_limit_bytes=40 * 1024 * 1024)


def cost(flops, bytes_accessed):
    return pl.CostEstimate(flops=flops, bytes_accessed=bytes_accessed, transcendentals=0)


def contract_last(left, right):
    return lax.dot_general(
        left, right, (((1,), (1,)), ((), ())), preferred_element_type=jnp.float32
    )


def contract_first(left, right):
    return lax.dot_general(
        left, right, (((0,), (0,)), ((), ())), preferred_element_type=jnp.float32
    )


def matmul(left, right):
    return lax.dot_general(
        left, right, (((1,), (0,)), ((), ())), preferred_element_type=jnp.float32
    )


def swiglu_grads(grad_hidden, gate_pre, up_pre):
    gate_f = gate_pre.astype(jnp.float32)
    up_f = up_pre.astype(jnp.float32)
    sigma = jax.nn.sigmoid(gate_f)
    silu_gate = gate_f * sigma
    slope = sigma * (1.0 + gate_f - silu_gate)
    grad_gpre = (grad_hidden * (up_f * slope)).astype(jnp.bfloat16)
    grad_upre = (grad_hidden * silu_gate).astype(jnp.bfloat16)
    hidden = (silu_gate * up_f).astype(jnp.bfloat16)
    return (grad_gpre, grad_upre, hidden)


def swapped(values):
    return lax.ppermute(values, "core", [(0, 1), (1, 0)])


def pieces_of(totals):
    pieces = []
    for total in totals:
        for _ in range(3):
            piece = total.astype(jnp.bfloat16).astype(jnp.float32)
            pieces.append(piece)
            total = total - piece
    pieces.append(jnp.zeros((EXTRA - len(pieces), totals[0].shape[1]), jnp.float32))
    return jnp.concatenate(pieces, axis=0).astype(jnp.bfloat16)


def totals_of(pieces):
    return [jnp.sum(pieces[3 * k : 3 * k + 3], axis=0, keepdims=True) for k in range(3)]


def half_of(ref, core):
    rows = ref.shape[0] // 2
    return ref[pl.ds(pl.multiple_of(core * rows, rows), rows), :]


def first_kernel(core_ref, gate_pre_ref, up_pre_ref, gate_ref, up_ref, down_ref, sent_ref, sums_ref):
    rows, inner = gate_pre_ref.shape[0] // 2, gate_pre_ref.shape[1]
    lanes = sent_ref.shape[1] // 2
    sums = []
    for ref in (gate_ref, up_ref, down_ref):
        total = jnp.sum(jnp.abs(ref[...].astype(jnp.float32)), axis=0, keepdims=True)
        sums.append(jnp.broadcast_to(jnp.sum(total, axis=1, keepdims=True), (1, 2 * lanes)))
    sent_ref[...] = jnp.zeros(sent_ref.shape, sent_ref.dtype)
    sent_ref[0:rows, 0:inner] = half_of(gate_pre_ref, 1 - core_ref[0])
    sent_ref[0:rows, lanes : lanes + inner] = half_of(up_pre_ref, 1 - core_ref[0])
    sent_ref[rows:, :] = pieces_of(sums)
    tile = jnp.concatenate(sums + [jnp.zeros((5, 2 * lanes), jnp.float32)], axis=0)
    sums_ref[...] = tile[:, :LANES]


def first(core, gate_pre, up_pre, gate_t, up_t, down):
    rows, inner = gate_pre.shape
    lanes = -(-inner // LANES) * LANES
    return pl.pallas_call(
        first_kernel,
        out_shape=(
            jax.ShapeDtypeStruct((rows // 2 + EXTRA, 2 * lanes), jnp.bfloat16),
            jax.ShapeDtypeStruct((8, LANES), jnp.float32),
        ),
        in_specs=[SMEM] + [VMEM] * 5,
        out_specs=(VMEM, VMEM),
        compiler_params=WIDE,
        cost_estimate=cost(1 << 20, 3 << 19),
    )(core, gate_pre, up_pre, gate_t, up_t, down)


def second_kernel(core_ref, gate_pre_ref, up_pre_ref, other_ref, sums_ref, out_ref, pre_ref, sent_ref):
    rows, inner = gate_pre_ref.shape[0] // 2, gate_pre_ref.shape[1]
    lanes = other_ref.shape[1] // 2
    pre_ref[...] = jnp.concatenate(
        [
            half_of(gate_pre_ref, core_ref[0]),
            other_ref[0:rows, 0:inner],
            half_of(up_pre_ref, core_ref[0]),
            other_ref[0:rows, lanes : lanes + inner],
        ],
        axis=1,
    )
    others = totals_of(other_ref[rows:, :LANES].astype(jnp.float32))
    extra = pieces_of([sums_ref[n : n + 1, :] + others[n] for n in range(3)])
    blocks = [out_ref[:, j * LANES : (j + 1) * LANES] for j in range(out_ref.shape[1] // LANES)]
    block = jnp.concatenate(blocks + [extra], axis=0)
    for k in range(N_CHIP):
        sent_ref[k] = block


def second(core, gate_pre, up_pre, other, sums, grad_out):
    rows, width = grad_out.shape
    inner = gate_pre.shape[1]
    return pl.pallas_call(
        second_kernel,
        out_shape=(
            jax.ShapeDtypeStruct((rows, 4 * inner), jnp.bfloat16),
            jax.ShapeDtypeStruct((N_CHIP, rows * width // LANES + EXTRA, LANES), jnp.bfloat16),
        ),
        in_specs=[SMEM] + [VMEM] * 5,
        out_specs=(VMEM, VMEM),
        compiler_params=WIDE,
        cost_estimate=cost(1 << 16, 1 << 20),
    )(core, gate_pre, up_pre, other, sums, grad_out)


def tile_kernel(extra_ref, after_ref, tile_ref):
    sums = totals_of(jnp.sum(extra_ref[...].astype(jnp.float32), axis=0))
    tile = jnp.concatenate(sums + [jnp.zeros((5, LANES), jnp.float32)], axis=0)
    tile_ref[...] = jnp.broadcast_to(tile[None], tile_ref.shape)


def sums_tile(received, after):
    rows = received.shape[1] - EXTRA
    return pl.pallas_call(
        tile_kernel,
        grid=(1,),
        out_shape=jax.ShapeDtypeStruct((N_ROW, 8, LANES), jnp.float32),
        in_specs=[
            pl.BlockSpec((N_CHIP, EXTRA, LANES), lambda i: (0, rows // EXTRA, 0)),
            pl.BlockSpec(after.shape, lambda i: (0, 0)),
        ],
        out_specs=pl.BlockSpec((N_ROW, 8, LANES), lambda i: (0, 0, 0)),
        compiler_params=PARAMS,
        cost_estimate=cost(1 << 16, 1 << 18),
    )(received, after)


def scale_of(tile_ref, which):
    total = jnp.sum(tile_ref[...], axis=0)[which : which + 1, 0:1]
    return total / float(EMBED_SIZE * GATE_INNER_SIZE) + 1e-05


def clipped(values, scale):
    return jnp.clip(values.astype(jnp.float32), -scale, scale).astype(jnp.bfloat16)


def partial_kernel(tile_ref, received_ref, down_ref, other_ref, partial_ref, out_ref, done_ref, quant_ref):
    rows = partial_ref.shape[1]
    inner, width = down_ref.shape

    @pl.when(pl.program_id(0) == 0)
    def _():
        scale = scale_of(tile_ref, 2)
        quant_ref[0:inner, :] = clipped(down_ref[...], scale)
        quant_ref[inner:, :] = clipped(other_ref[...], scale)

    blocks = [received_ref[:, j * rows : (j + 1) * rows, :] for j in range(width // LANES)]
    out_rows = jnp.concatenate([block.reshape((-1, LANES)) for block in blocks], axis=1)
    out_ref[...] = out_rows
    done_ref[...] = jnp.zeros(done_ref.shape, jnp.float32)
    partial = contract_last(out_rows, quant_ref[...])
    partial_ref[...] = partial.astype(jnp.bfloat16).reshape(partial_ref.shape)


def hidden_partial(tile, received, down, other):
    blocks, steps = 4, N_CHIP // 4
    inner, width = down.shape
    rows = (received.shape[1] - EXTRA) * LANES // width
    whole = pl.BlockSpec((inner, width), lambda i: (0, 0))
    return pl.pallas_call(
        partial_kernel,
        grid=(steps,),
        out_shape=(
            jax.ShapeDtypeStruct((N_ROW, rows, 2 * inner), jnp.bfloat16),
            jax.ShapeDtypeStruct((N_CHIP * rows, width), jnp.bfloat16),
            jax.ShapeDtypeStruct((8, LANES), jnp.float32),
        ),
        in_specs=[
            pl.BlockSpec(tile.shape, lambda i: (0, 0, 0)),
            pl.BlockSpec((blocks,) + received.shape[1:], lambda i: (i, 0, 0)),
            whole,
            whole,
        ],
        out_specs=(
            pl.BlockSpec((blocks, rows, 2 * inner), lambda i: (i, 0, 0)),
            pl.BlockSpec((blocks * rows, width), lambda i: (i, 0)),
            pl.BlockSpec((8, LANES), lambda i: (0, 0)),
        ),
        scratch_shapes=[pltpu.VMEM((2 * inner, width), jnp.bfloat16)],
        compiler_params=PARAMS,
        cost_estimate=cost(2 * 512 * 896 * 512, 4 << 20),
    )(tile, received, down, other)


def spread_kernel(parts_ref, after_ref, sent_ref):
    total = jnp.sum(parts_ref[...].astype(jnp.float32), axis=0).astype(jnp.bfloat16)
    for k in range(N_ROW):
        sent_ref[k] = total


def spread(parts, after):
    return pl.pallas_call(
        spread_kernel,
        out_shape=jax.ShapeDtypeStruct(parts.shape, jnp.bfloat16),
        in_specs=[VMEM] * 2,
        out_specs=VMEM,
        compiler_params=PARAMS,
        cost_estimate=cost(1 << 19, 2 << 20),
    )(parts, after)


def clip_kernel(tile_ref, gate_ref, up_ref, other_ref, quant_ref):
    inner = gate_ref.shape[0]
    for n, ref in enumerate((gate_ref, up_ref)):
        scale = scale_of(tile_ref, n)
        quant_ref[n, 0:inner, :] = clipped(ref[...], scale)
        quant_ref[n, inner:, :] = clipped(other_ref[n], scale)


def clipped_latents(tile, gate_t, up_t, other):
    inner, width = gate_t.shape
    return pl.pallas_call(
        clip_kernel,
        out_shape=jax.ShapeDtypeStruct((2, 2 * inner, width), jnp.bfloat16),
        in_specs=[VMEM] * 4,
        out_specs=VMEM,
        compiler_params=PARAMS,
        cost_estimate=cost(1 << 20, 4 << 20),
    )(tile, gate_t, up_t, other)


def act_kernel(hid_ref, pre_ref, quant_ref, partial_ref, acts_ref):
    both = hid_ref.shape[2]
    grad_hidden = hid_ref[...].reshape((-1, both)).astype(jnp.float32)
    acts = swiglu_grads(grad_hidden, pre_ref[:, :both], pre_ref[:, both:])
    partial = matmul(acts[0], quant_ref[0]) + matmul(acts[1], quant_ref[1])
    partial_ref[...] = partial.astype(jnp.bfloat16).reshape(partial_ref.shape)
    for n, act in enumerate(acts):
        acts_ref[n] = act


def act_partial(grad_hidden, pre_half, quant):
    blocks, steps = 4, N_ROW // 4
    rows, both = grad_hidden.shape[1:]
    width = quant.shape[2]
    return pl.pallas_call(
        act_kernel,
        grid=(steps,),
        out_shape=(
            jax.ShapeDtypeStruct((N_CHIP, rows, width), jnp.bfloat16),
            jax.ShapeDtypeStruct((3, N_ROW * rows, both), jnp.bfloat16),
        ),
        in_specs=[
            pl.BlockSpec((blocks, rows, both), lambda i: (i, 0, 0)),
            pl.BlockSpec((blocks * rows, 2 * both), lambda i: (i, 0)),
            pl.BlockSpec(quant.shape, lambda i: (0, 0, 0)),
        ],
        out_specs=(
            pl.BlockSpec((blocks, rows, width), lambda i: (i, 0, 0)),
            pl.BlockSpec((3, blocks * rows, both), lambda i: (0, i, 0)),
        ),
        compiler_params=WIDE,
        cost_estimate=cost(4 * 512 * 896 * 512, 8 << 20),
    )(grad_hidden, pre_half, quant)


def latent_grads_kernel(place_ref, acts_ref, out_ref, tokens_ref, own_ref, sent_ref, rows_ref):
    rows = tokens_ref.shape[1]
    for block in range(2 * N_Y):
        flip, bits = block & 1, block >> 1
        offset = 2 * (bits & 3) + bits // 4
        chip = (place_ref[0] ^ flip) * N_Y + (place_ref[1] ^ offset)
        rows_ref[pl.ds(pl.multiple_of(chip * rows, rows), rows), :] = tokens_ref[block]
    inner = own_ref.shape[1]
    for n in range(3):
        half = out_ref[...] if n == 2 else rows_ref[...]
        grad = contract_first(acts_ref[n], half)
        own_ref[n] = grad[:inner]
        sent_ref[n] = grad[inner:].astype(jnp.bfloat16)


def latent_grads(place, acts, out_half, token_blocks):
    inner, width = acts.shape[2] // 2, out_half.shape[1]
    return pl.pallas_call(
        latent_grads_kernel,
        out_shape=(
            jax.ShapeDtypeStruct((3, inner, width), jnp.float32),
            jax.ShapeDtypeStruct((3, inner, width), jnp.bfloat16),
        ),
        in_specs=[SMEM] + [VMEM] * 3,
        out_specs=(VMEM, VMEM),
        scratch_shapes=[pltpu.VMEM(out_half.shape, jnp.bfloat16)],
        compiler_params=PARAMS,
        cost_estimate=cost(6 * 512 * 896 * 512, 8 << 20),
    )(place, acts, out_half, token_blocks)


def join_kernel(own_ref, other_ref, *refs):
    for n, ref in enumerate(refs[:3]):
        ref[...] = (own_ref[n] + other_ref[n].astype(jnp.float32)).astype(jnp.bfloat16)
    refs[3][...] = jnp.zeros(refs[3].shape, jnp.float32)


def join(own, other):
    grad = jax.ShapeDtypeStruct(own.shape[1:], jnp.bfloat16)
    return pl.pallas_call(
        join_kernel,
        out_shape=(grad, grad, grad, jax.ShapeDtypeStruct((8, LANES), jnp.float32)),
        in_specs=[VMEM] * 2,
        out_specs=(VMEM,) * 4,
        compiler_params=PARAMS,
        cost_estimate=cost(1 << 20, 5 << 20),
    )(own, other)


def total_kernel(parts_ref, after_ref, total_ref):
    total_ref[...] = jnp.sum(parts_ref[...].astype(jnp.float32), axis=0).astype(jnp.bfloat16)


def total(parts, after):
    return pl.pallas_call(
        total_kernel,
        out_shape=jax.ShapeDtypeStruct(parts.shape[1:], jnp.bfloat16),
        in_specs=[VMEM] * 2,
        out_specs=VMEM,
        compiler_params=PARAMS,
        cost_estimate=cost(1 << 18, 1 << 19),
    )(parts, after)


def copy_kernel(values_ref, after_ref, copy_ref):
    copy_ref[...] = values_ref[...]


def copy_after(values, after):
    return pl.pallas_call(
        copy_kernel,
        out_shape=jax.ShapeDtypeStruct(values.shape, values.dtype),
        in_specs=[VMEM] * 2,
        out_specs=VMEM,
        cost_estimate=cost(1, 1 << 16),
    )(values, after)


def exchanged(blocks, axis, *steps):
    count = 2 if axis == "xl" else N_Y
    others = [lax.ppermute(blocks, axis, [(k, k ^ step) for k in range(count)]) for step in steps]
    return jnp.concatenate([blocks] + others, axis=0)


def token_pair(tokens):
    blocks = exchanged(tokens[None], "xl", 1)
    return blocks, blocks[-1, :EXTRA, :LANES]


def far_tokens(blocks, done):
    blocks = exchanged(copy_after(blocks, done), "y", 2, 4, 6)
    return blocks, blocks[-1, :EXTRA, :LANES]


def in_branch(work, *operands):
    def nothing(*operands):
        shapes = jax.eval_shape(work, *operands)
        return tuple(jnp.zeros(leaf.shape, leaf.dtype) for leaf in shapes)

    def always(*operands):
        return tuple(work(*operands))

    return lax.cond(lax.axis_index("z") < 8, always, nothing, *operands)


def shards(tokens, grad_out, gate_pre, up_pre, gate_latent, up_latent, down_latent):
    core = lax.axis_index("core").astype(jnp.int32).reshape((1,))
    place = jnp.stack([lax.axis_index("xl"), lax.axis_index("y")]).astype(jnp.int32)

    gate_t, up_t = gate_latent.T, up_latent.T
    sent, sums = first(core, gate_pre, up_pre, gate_t, up_t, down_latent)
    pre_rows, sent = second(core, gate_pre, up_pre, swapped(sent), sums, grad_out)
    pre_half = lax.all_gather(pre_rows, ROW, axis=0, tiled=True)

    def exchanges(sent, tokens, gate_t, up_t, down):
        received = lax.all_to_all(sent, CHIP, 0, 0)
        down_other = swapped(down)
        pair, after = in_branch(token_pair, tokens)
        tile = lax.all_to_all(sums_tile(received, after), ROW, 0, 0)
        partial, out_half, done = hidden_partial(tile, received, down, down_other)
        parts = lax.all_to_all(partial, ROW, 0, 0)
        most_tokens, after = in_branch(far_tokens, pair, done)
        other_latents = swapped(jnp.stack([gate_t, up_t]))
        quant = clipped_latents(tile, gate_t, up_t, other_latents)
        token_blocks = exchanged(most_tokens, "y", 1)
        grad_hidden = lax.all_to_all(spread(parts, after), ROW, 0, 0)
        return (out_half, quant, grad_hidden, token_blocks)

    out_half, quant, grad_hidden, token_blocks = in_branch(
        exchanges, sent, tokens, gate_t, up_t, down_latent
    )

    partial, acts = act_partial(grad_hidden, pre_half, quant)
    parts = lax.all_to_all(partial, CHIP, 0, 0)

    def joined(place, acts, out_half, token_blocks):
        own, sent = latent_grads(place, acts, out_half, token_blocks)
        return join(own, swapped(sent))

    grad_gate, grad_up, grad_down, done = in_branch(joined, place, acts, out_half, token_blocks)
    grad_tokens = total(parts, done)
    return (grad_tokens, grad_gate.T, grad_up.T, grad_down)


def solution(mesh):
    fine = Mesh(mesh.devices.reshape((2, 8, 2, 8, 2)), ROW + CHIP + ("core",))
    col = CHIP + ("core",)
    in_specs = (
        P(col, ROW),
        P(col, ROW),
        P(ROW, col),
        P(ROW, col),
        P(ROW, col),
        P(ROW, col),
        P(col, ROW),
    )
    out_specs = (P(col, ROW), P(ROW, col), P(ROW, col), P(col, ROW))
    return jax.shard_map(shards, mesh=fine, in_specs=in_specs, out_specs=out_specs, check_vma=False)
```

```python
import jax
import jax.numpy as jnp
from jax import lax
from jax.experimental import pallas as pl
from jax.experimental.pallas import tpu as pltpu
from jax.sharding import Mesh, PartitionSpec as P

EMBED_SIZE = 8192
GATE_INNER_SIZE = 14336
N_ROW = 16
N_CHIP = 16
ROW = ("xh", "z")
CHIP = ("xl", "y")
EXTRA = 16
N_Y = 8
LANES = 128
VMEM = pl.BlockSpec(memory_space=pltpu.VMEM)
SMEM = pl.BlockSpec(memory_space=pltpu.SMEM)
WIDE = pltpu.CompilerParams(vmem_limit_bytes=58 * 1024 * 1024)
PARAMS = pltpu.CompilerParams(vmem_limit_bytes=40 * 1024 * 1024)


def cost(flops, bytes_accessed):
    return pl.CostEstimate(flops=flops, bytes_accessed=bytes_accessed, transcendentals=0)


def contract_last(left, right):
    return lax.dot_general(
        left, right, (((1,), (1,)), ((), ())), preferred_element_type=jnp.float32
    )


def contract_first(left, right):
    return lax.dot_general(
        left, right, (((0,), (0,)), ((), ())), preferred_element_type=jnp.float32
    )


def matmul(left, right):
    return lax.dot_general(
        left, right, (((1,), (0,)), ((), ())), preferred_element_type=jnp.float32
    )


def swiglu_grads(grad_hidden, gate_pre, up_pre):
    gate_f = gate_pre.astype(jnp.float32)
    up_f = up_pre.astype(jnp.float32)
    sigma = jax.nn.sigmoid(gate_f)
    silu_gate = gate_f * sigma
    slope = sigma * (1.0 + gate_f - silu_gate)
    grad_gpre = (grad_hidden * (up_f * slope)).astype(jnp.bfloat16)
    grad_upre = (grad_hidden * silu_gate).astype(jnp.bfloat16)
    hidden = (silu_gate * up_f).astype(jnp.bfloat16)
    return (grad_gpre, grad_upre, hidden)


def swapped(values):
    return lax.ppermute(values, "core", [(0, 1), (1, 0)])


def pieces_of(totals):
    pieces = []
    for total in totals:
        for _ in range(3):
            piece = total.astype(jnp.bfloat16).astype(jnp.float32)
            pieces.append(piece)
            total = total - piece
    pieces.append(jnp.zeros((EXTRA - len(pieces), totals[0].shape[1]), jnp.float32))
    return jnp.concatenate(pieces, axis=0).astype(jnp.bfloat16)


def totals_of(pieces):
    return [jnp.sum(pieces[3 * k : 3 * k + 3], axis=0, keepdims=True) for k in range(3)]


def half_of(ref, core):
    rows = ref.shape[0] // 2
    return ref[pl.ds(pl.multiple_of(core * rows, rows), rows), :]


def first_kernel(core_ref, gate_pre_ref, up_pre_ref, gate_ref, up_ref, down_ref, sent_ref, sums_ref):
    rows, inner = gate_pre_ref.shape[0] // 2, gate_pre_ref.shape[1]
    lanes = sent_ref.shape[1] // 2
    sums = []
    for ref in (gate_ref, up_ref, down_ref):
        total = jnp.sum(jnp.abs(ref[...].astype(jnp.float32)), axis=0, keepdims=True)
        sums.append(jnp.broadcast_to(jnp.sum(total, axis=1, keepdims=True), (1, 2 * lanes)))
    sent_ref[...] = jnp.zeros(sent_ref.shape, sent_ref.dtype)
    sent_ref[0:rows, 0:inner] = half_of(gate_pre_ref, 1 - core_ref[0])
    sent_ref[0:rows, lanes : lanes + inner] = half_of(up_pre_ref, 1 - core_ref[0])
    sent_ref[rows:, :] = pieces_of(sums)
    tile = jnp.concatenate(sums + [jnp.zeros((5, 2 * lanes), jnp.float32)], axis=0)
    sums_ref[...] = tile[:, :LANES]


def first(core, gate_pre, up_pre, gate_t, up_t, down):
    rows, inner = gate_pre.shape
    lanes = -(-inner // LANES) * LANES
    return pl.pallas_call(
        first_kernel,
        out_shape=(
            jax.ShapeDtypeStruct((rows // 2 + EXTRA, 2 * lanes), jnp.bfloat16),
            jax.ShapeDtypeStruct((8, LANES), jnp.float32),
        ),
        in_specs=[SMEM] + [VMEM] * 5,
        out_specs=(VMEM, VMEM),
        compiler_params=WIDE,
        cost_estimate=cost(1 << 20, 3 << 19),
    )(core, gate_pre, up_pre, gate_t, up_t, down)


def second_kernel(core_ref, gate_pre_ref, up_pre_ref, other_ref, sums_ref, out_ref, gate_rows_ref, up_rows_ref, sent_ref):
    rows, inner = gate_pre_ref.shape[0] // 2, gate_pre_ref.shape[1]
    lanes = other_ref.shape[1] // 2
    pad = jnp.zeros((rows, gate_rows_ref.shape[1] - 2 * inner), jnp.bfloat16)
    gate_rows_ref[...] = jnp.concatenate(
        [half_of(gate_pre_ref, core_ref[0]), other_ref[0:rows, 0:inner], pad], axis=1
    )
    up_rows_ref[...] = jnp.concatenate(
        [half_of(up_pre_ref, core_ref[0]), other_ref[0:rows, lanes : lanes + inner], pad], axis=1
    )
    others = totals_of(other_ref[rows:, :LANES].astype(jnp.float32))
    extra = pieces_of([sums_ref[n : n + 1, :] + others[n] for n in range(3)])
    blocks = [out_ref[:, j * LANES : (j + 1) * LANES] for j in range(out_ref.shape[1] // LANES)]
    block = jnp.concatenate(blocks + [extra], axis=0)
    for k in range(N_CHIP):
        sent_ref[k] = block


def second(core, gate_pre, up_pre, other, sums, grad_out):
    rows, width = grad_out.shape
    inner = gate_pre.shape[1]
    return pl.pallas_call(
        second_kernel,
        out_shape=(
            jax.ShapeDtypeStruct((rows, other.shape[1]), jnp.bfloat16),
            jax.ShapeDtypeStruct((rows, other.shape[1]), jnp.bfloat16),
            jax.ShapeDtypeStruct((N_CHIP, rows * width // LANES + EXTRA, LANES), jnp.bfloat16),
        ),
        in_specs=[SMEM] + [VMEM] * 5,
        out_specs=(VMEM, VMEM, VMEM),
        compiler_params=WIDE,
        cost_estimate=cost(1 << 16, 1 << 20),
    )(core, gate_pre, up_pre, other, sums, grad_out)


def tile_kernel(extra_ref, after_ref, tile_ref):
    sums = totals_of(jnp.sum(extra_ref[...].astype(jnp.float32), axis=0))
    tile = jnp.concatenate(sums + [jnp.zeros((5, LANES), jnp.float32)], axis=0)
    tile_ref[...] = jnp.broadcast_to(tile[None], tile_ref.shape)


def sums_tile(received, after):
    rows = received.shape[1] - EXTRA
    return pl.pallas_call(
        tile_kernel,
        grid=(1,),
        out_shape=jax.ShapeDtypeStruct((N_ROW, 8, LANES), jnp.float32),
        in_specs=[
            pl.BlockSpec((N_CHIP, EXTRA, LANES), lambda i: (0, rows // EXTRA, 0)),
            pl.BlockSpec(after.shape, lambda i: (0, 0)),
        ],
        out_specs=pl.BlockSpec((N_ROW, 8, LANES), lambda i: (0, 0, 0)),
        compiler_params=PARAMS,
        cost_estimate=cost(1 << 16, 1 << 18),
    )(received, after)


def scale_of(tile_ref, which):
    total = jnp.sum(tile_ref[...], axis=0)[which : which + 1, 0:1]
    return total / float(EMBED_SIZE * GATE_INNER_SIZE) + 1e-05


def clipped(values, scale):
    return jnp.clip(values.astype(jnp.float32), -scale, scale).astype(jnp.bfloat16)


def partial_kernel(tile_ref, received_ref, down_ref, other_ref, partial_ref, out_ref, quant_ref):
    rows = partial_ref.shape[1]
    inner, width = down_ref.shape

    @pl.when(pl.program_id(0) == 0)
    def _():
        scale = scale_of(tile_ref, 2)
        quant_ref[0:inner, :] = clipped(down_ref[...], scale)
        quant_ref[inner:, :] = clipped(other_ref[...], scale)

    blocks = [received_ref[:, j * rows : (j + 1) * rows, :] for j in range(width // LANES)]
    out_rows = jnp.concatenate([block.reshape((-1, LANES)) for block in blocks], axis=1)
    out_ref[...] = out_rows
    partial = contract_last(out_rows, quant_ref[...])
    partial_ref[...] = partial.astype(jnp.bfloat16).reshape(partial_ref.shape)


def hidden_partial(tile, received, down, other):
    blocks, steps = 4, N_CHIP // 4
    inner, width = down.shape
    rows = (received.shape[1] - EXTRA) * LANES // width
    whole = pl.BlockSpec((inner, width), lambda i: (0, 0))
    return pl.pallas_call(
        partial_kernel,
        grid=(steps,),
        out_shape=(
            jax.ShapeDtypeStruct((N_ROW, rows, 2 * inner), jnp.bfloat16),
            jax.ShapeDtypeStruct((N_CHIP * rows, width), jnp.bfloat16),
        ),
        in_specs=[
            pl.BlockSpec(tile.shape, lambda i: (0, 0, 0)),
            pl.BlockSpec((blocks,) + received.shape[1:], lambda i: (i, 0, 0)),
            whole,
            whole,
        ],
        out_specs=(
            pl.BlockSpec((blocks, rows, 2 * inner), lambda i: (i, 0, 0)),
            pl.BlockSpec((blocks * rows, width), lambda i: (i, 0)),
        ),
        scratch_shapes=[pltpu.VMEM((2 * inner, width), jnp.bfloat16)],
        compiler_params=PARAMS,
        cost_estimate=cost(2 * 512 * 896 * 512, 4 << 20),
    )(tile, received, down, other)


def spread_kernel(parts_ref, after_ref, sent_ref):
    total = jnp.sum(parts_ref[...].astype(jnp.float32), axis=0).astype(jnp.bfloat16)
    for k in range(N_ROW):
        sent_ref[k] = total


def spread(parts, after):
    return pl.pallas_call(
        spread_kernel,
        out_shape=jax.ShapeDtypeStruct(parts.shape, jnp.bfloat16),
        in_specs=[VMEM] * 2,
        out_specs=VMEM,
        compiler_params=PARAMS,
        cost_estimate=cost(1 << 19, 2 << 20),
    )(parts, after)


def clip_kernel(tile_ref, gate_ref, up_ref, other_ref, quant_ref):
    inner = gate_ref.shape[0]
    for n, ref in enumerate((gate_ref, up_ref)):
        scale = scale_of(tile_ref, n)
        quant_ref[n, 0:inner, :] = clipped(ref[...], scale)
        quant_ref[n, inner:, :] = clipped(other_ref[n], scale)


def clipped_latents(tile, gate_t, up_t, other):
    inner, width = gate_t.shape
    return pl.pallas_call(
        clip_kernel,
        out_shape=jax.ShapeDtypeStruct((2, 2 * inner, width), jnp.bfloat16),
        in_specs=[VMEM] * 4,
        out_specs=VMEM,
        compiler_params=PARAMS,
        cost_estimate=cost(1 << 20, 4 << 20),
    )(tile, gate_t, up_t, other)


def act_kernel(hid_ref, gate_ref, up_ref, quant_ref, partial_ref, acts_ref):
    both = hid_ref.shape[2]
    grad_hidden = hid_ref[...].reshape((-1, both)).astype(jnp.float32)
    up_pre = up_ref[...].reshape((-1, up_ref.shape[3]))[:, :both]
    acts = swiglu_grads(grad_hidden, gate_ref[:, :both], up_pre)
    partial = matmul(acts[0], quant_ref[0]) + matmul(acts[1], quant_ref[1])
    partial_ref[...] = partial.astype(jnp.bfloat16).reshape(partial_ref.shape)
    for n, act in enumerate(acts):
        acts_ref[n] = act


def act_partial(grad_hidden, gate_half, up_half, quant):
    blocks, steps = 4, N_ROW // 4
    rows, both = grad_hidden.shape[1:]
    width, lanes = quant.shape[2], gate_half.shape[1]
    up_half = up_half.reshape((N_ROW // 2, 2, rows, lanes))
    return pl.pallas_call(
        act_kernel,
        grid=(steps,),
        out_shape=(
            jax.ShapeDtypeStruct((N_CHIP, rows, width), jnp.bfloat16),
            jax.ShapeDtypeStruct((3, N_ROW * rows, both), jnp.bfloat16),
        ),
        in_specs=[
            pl.BlockSpec((blocks, rows, both), lambda i: (i, 0, 0)),
            pl.BlockSpec((blocks * rows, lanes), lambda i: (i, 0)),
            pl.BlockSpec((blocks, 1, rows, lanes), lambda i: (i % 2, i // 2, 0, 0)),
            pl.BlockSpec(quant.shape, lambda i: (0, 0, 0)),
        ],
        out_specs=(
            pl.BlockSpec((blocks, rows, width), lambda i: (i, 0, 0)),
            pl.BlockSpec((3, blocks * rows, both), lambda i: (0, i, 0)),
        ),
        compiler_params=WIDE,
        cost_estimate=cost(4 * 512 * 896 * 512, 8 << 20),
    )(grad_hidden, gate_half, up_half, quant)


def latent_grads_kernel(place_ref, acts_ref, out_ref, tokens_ref, own_ref, sent_ref, rows_ref):
    rows = tokens_ref.shape[1]
    for block in range(2 * N_Y):
        flip, bits = block & 1, block >> 1
        offset = 2 * (bits & 3) + bits // 4
        chip = (place_ref[0] ^ flip) * N_Y + (place_ref[1] ^ offset)
        rows_ref[pl.ds(pl.multiple_of(chip * rows, rows), rows), :] = tokens_ref[block]
    inner = own_ref.shape[1]
    for n in range(3):
        half = out_ref[...] if n == 2 else rows_ref[...]
        grad = contract_first(acts_ref[n], half)
        own_ref[n] = grad[:inner]
        sent_ref[n] = grad[inner:].astype(jnp.bfloat16)


def latent_grads(place, acts, out_half, token_blocks):
    inner, width = acts.shape[2] // 2, out_half.shape[1]
    return pl.pallas_call(
        latent_grads_kernel,
        out_shape=(
            jax.ShapeDtypeStruct((3, inner, width), jnp.float32),
            jax.ShapeDtypeStruct((3, inner, width), jnp.bfloat16),
        ),
        in_specs=[SMEM] + [VMEM] * 3,
        out_specs=(VMEM, VMEM),
        scratch_shapes=[pltpu.VMEM(out_half.shape, jnp.bfloat16)],
        compiler_params=PARAMS,
        cost_estimate=cost(6 * 512 * 896 * 512, 8 << 20),
    )(place, acts, out_half, token_blocks)


def join_kernel(own_ref, other_ref, *refs):
    for n, ref in enumerate(refs[:3]):
        ref[...] = (own_ref[n] + other_ref[n].astype(jnp.float32)).astype(jnp.bfloat16)
    refs[3][...] = jnp.zeros(refs[3].shape, jnp.float32)


def join(own, other):
    grad = jax.ShapeDtypeStruct(own.shape[1:], jnp.bfloat16)
    return pl.pallas_call(
        join_kernel,
        out_shape=(grad, grad, grad, jax.ShapeDtypeStruct((8, LANES), jnp.float32)),
        in_specs=[VMEM] * 2,
        out_specs=(VMEM,) * 4,
        compiler_params=PARAMS,
        cost_estimate=cost(1 << 20, 5 << 20),
    )(own, other)


def total_kernel(parts_ref, after_ref, total_ref):
    total_ref[...] = jnp.sum(parts_ref[...].astype(jnp.float32), axis=0).astype(jnp.bfloat16)


def total(parts, after):
    return pl.pallas_call(
        total_kernel,
        out_shape=jax.ShapeDtypeStruct(parts.shape[1:], jnp.bfloat16),
        in_specs=[VMEM] * 2,
        out_specs=VMEM,
        compiler_params=PARAMS,
        cost_estimate=cost(1 << 18, 1 << 19),
    )(parts, after)


def copy_kernel(values_ref, after_ref, copy_ref):
    copy_ref[...] = values_ref[...]


def copy_after(values, after):
    return pl.pallas_call(
        copy_kernel,
        out_shape=jax.ShapeDtypeStruct(values.shape, values.dtype),
        in_specs=[VMEM] * 2,
        out_specs=VMEM,
        cost_estimate=cost(1, 1 << 16),
    )(values, after)


def exchanged(blocks, axis, *steps):
    count = 2 if axis == "xl" else N_Y
    others = [lax.ppermute(blocks, axis, [(k, k ^ step) for k in range(count)]) for step in steps]
    return jnp.concatenate([blocks] + others, axis=0)


def token_pair(tokens):
    blocks = exchanged(tokens[None], "xl", 1)
    return blocks, blocks[-1, :EXTRA, :LANES]


def far_tokens(blocks, done):
    blocks = exchanged(copy_after(blocks, done), "y", 2, 4, 6)
    return blocks, blocks[-1, :EXTRA, :LANES]


def in_branch(work, *operands):
    def nothing(*operands):
        shapes = jax.eval_shape(work, *operands)
        return tuple(jnp.zeros(leaf.shape, leaf.dtype) for leaf in shapes)

    def always(*operands):
        return tuple(work(*operands))

    return lax.cond(lax.axis_index("z") < 8, always, nothing, *operands)


def shards(tokens, grad_out, gate_pre, up_pre, gate_latent, up_latent, down_latent):
    core = lax.axis_index("core").astype(jnp.int32).reshape((1,))
    place = jnp.stack([lax.axis_index("xl"), lax.axis_index("y")]).astype(jnp.int32)

    gate_t, up_t = gate_latent.T, up_latent.T
    sent, sums = first(core, gate_pre, up_pre, gate_t, up_t, down_latent)
    gate_rows, up_rows, sent = second(core, gate_pre, up_pre, swapped(sent), sums, grad_out)
    gate_half = lax.all_gather(gate_rows, ROW, axis=0, tiled=True)
    up_half = lax.all_gather(up_rows, ROW[::-1], axis=0, tiled=True)

    def exchanges(sent, tokens, gate_t, up_t, down):
        received = lax.all_to_all(sent, CHIP, 0, 0)
        down_other = swapped(down)
        pair, after = in_branch(token_pair, tokens)
        tile = lax.all_to_all(sums_tile(received, after), ROW, 0, 0)
        partial, out_half = hidden_partial(tile, received, down, down_other)
        parts = lax.all_to_all(partial, ROW, 0, 0)
        most_tokens, after = in_branch(far_tokens, pair, out_half[:EXTRA, :LANES])
        other_latents = swapped(jnp.stack([gate_t, up_t]))
        quant = clipped_latents(tile, gate_t, up_t, other_latents)
        token_blocks = exchanged(most_tokens, "y", 1)
        grad_hidden = lax.all_to_all(spread(parts, after), ROW, 0, 0)
        return (out_half, quant, grad_hidden, token_blocks)

    out_half, quant, grad_hidden, token_blocks = in_branch(
        exchanges, sent, tokens, gate_t, up_t, down_latent
    )

    partial, acts = act_partial(grad_hidden, gate_half, up_half, quant)
    parts = lax.all_to_all(partial, CHIP, 0, 0)

    def joined(place, acts, out_half, token_blocks):
        own, sent = latent_grads(place, acts, out_half, token_blocks)
        return join(own, swapped(sent))

    grad_gate, grad_up, grad_down, done = in_branch(joined, place, acts, out_half, token_blocks)
    grad_tokens = total(parts, done)
    return (grad_tokens, grad_gate.T, grad_up.T, grad_down)


def solution(mesh):
    fine = Mesh(mesh.devices.reshape((2, 8, 2, 8, 2)), ROW + CHIP + ("core",))
    col = CHIP + ("core",)
    in_specs = (
        P(col, ROW),
        P(col, ROW),
        P(ROW, col),
        P(ROW, col),
        P(ROW, col),
        P(ROW, col),
        P(col, ROW),
    )
    out_specs = (P(col, ROW), P(ROW, col), P(ROW, col), P(col, ROW))
    return jax.shard_map(shards, mesh=fine, in_specs=in_specs, out_specs=out_specs, check_vma=False)
```

```python
import jax
import jax.numpy as jnp
from jax import lax
from jax.experimental import pallas as pl
from jax.experimental.pallas import tpu as pltpu
from jax.sharding import Mesh, PartitionSpec as P

EMBED_SIZE = 8192
GATE_INNER_SIZE = 14336
N_ROW = 16
N_CHIP = 16
ROW = ("xh", "z")
CHIP = ("xl", "y")
EXTRA = 16
N_Y = 8
LANES = 128
VMEM = pl.BlockSpec(memory_space=pltpu.VMEM)
SMEM = pl.BlockSpec(memory_space=pltpu.SMEM)
WIDE = pltpu.CompilerParams(vmem_limit_bytes=58 * 1024 * 1024)
PARAMS = pltpu.CompilerParams(vmem_limit_bytes=40 * 1024 * 1024)


def cost(flops, bytes_accessed):
    return pl.CostEstimate(flops=flops, bytes_accessed=bytes_accessed, transcendentals=0)


def contract_last(left, right):
    return lax.dot_general(
        left, right, (((1,), (1,)), ((), ())), preferred_element_type=jnp.float32
    )


def contract_first(left, right):
    return lax.dot_general(
        left, right, (((0,), (0,)), ((), ())), preferred_element_type=jnp.float32
    )


def matmul(left, right):
    return lax.dot_general(
        left, right, (((1,), (0,)), ((), ())), preferred_element_type=jnp.float32
    )


def swiglu_grads(grad_hidden, gate_pre, up_pre):
    gate_f = gate_pre.astype(jnp.float32)
    up_f = up_pre.astype(jnp.float32)
    sigma = jax.nn.sigmoid(gate_f)
    silu_gate = gate_f * sigma
    slope = sigma * (1.0 + gate_f - silu_gate)
    grad_gpre = (grad_hidden * (up_f * slope)).astype(jnp.bfloat16)
    grad_upre = (grad_hidden * silu_gate).astype(jnp.bfloat16)
    hidden = (silu_gate * up_f).astype(jnp.bfloat16)
    return (grad_gpre, grad_upre, hidden)


def swapped(values):
    return lax.ppermute(values, "core", [(0, 1), (1, 0)])


def pieces_of(totals):
    pieces = []
    for total in totals:
        for _ in range(3):
            piece = total.astype(jnp.bfloat16).astype(jnp.float32)
            pieces.append(piece)
            total = total - piece
    pieces.append(jnp.zeros((EXTRA - len(pieces), totals[0].shape[1]), jnp.float32))
    return jnp.concatenate(pieces, axis=0).astype(jnp.bfloat16)


def totals_of(pieces):
    return [jnp.sum(pieces[3 * k : 3 * k + 3], axis=0, keepdims=True) for k in range(3)]


def first_kernel(out_ref, gate_ref, up_ref, down_ref, sent_ref):
    sums = []
    for ref in (gate_ref, up_ref, down_ref):
        total = jnp.sum(jnp.abs(ref[...].astype(jnp.float32)), axis=0, keepdims=True)
        sums.append(jnp.broadcast_to(jnp.sum(total, axis=1, keepdims=True), (1, LANES)))
    blocks = [out_ref[:, j * LANES : (j + 1) * LANES] for j in range(out_ref.shape[1] // LANES)]
    block = jnp.concatenate(blocks + [pieces_of(sums)], axis=0)
    for k in range(N_CHIP):
        sent_ref[k] = block


def first(grad_out, gate_t, up_t, down):
    rows, width = grad_out.shape
    return pl.pallas_call(
        first_kernel,
        out_shape=jax.ShapeDtypeStruct((N_CHIP, rows * width // LANES + EXTRA, LANES), jnp.bfloat16),
        in_specs=[VMEM] * 4,
        out_specs=VMEM,
        compiler_params=WIDE,
        cost_estimate=cost(1 << 20, 5 << 19),
    )(grad_out, gate_t, up_t, down)


def tile_kernel(extra_ref, after_ref, tile_ref):
    sums = totals_of(jnp.sum(extra_ref[...].astype(jnp.float32), axis=0))
    tile = jnp.concatenate(sums + [jnp.zeros((5, LANES), jnp.float32)], axis=0)
    tile_ref[...] = jnp.broadcast_to(tile[None], tile_ref.shape)


def sums_tile(received, after):
    rows = received.shape[1] - EXTRA
    return pl.pallas_call(
        tile_kernel,
        grid=(1,),
        out_shape=jax.ShapeDtypeStruct((2 * N_ROW, 8, LANES), jnp.float32),
        in_specs=[
            pl.BlockSpec((N_CHIP, EXTRA, LANES), lambda i: (0, rows // EXTRA, 0)),
            pl.BlockSpec(after.shape, lambda i: (0, 0)),
        ],
        out_specs=pl.BlockSpec((2 * N_ROW, 8, LANES), lambda i: (0, 0, 0)),
        compiler_params=PARAMS,
        cost_estimate=cost(1 << 16, 1 << 18),
    )(received, after)


def scale_of(tile_ref, which):
    total = jnp.sum(tile_ref[...], axis=0)[which : which + 1, 0:1]
    return total / float(EMBED_SIZE * GATE_INNER_SIZE) + 1e-05


def clipped(values, scale):
    return jnp.clip(values.astype(jnp.float32), -scale, scale).astype(jnp.bfloat16)


def partial_kernel(tile_ref, received_ref, down_ref, other_ref, partial_ref, out_ref, quant_ref):
    rows = partial_ref.shape[1]
    inner, width = down_ref.shape

    @pl.when(pl.program_id(0) == 0)
    def _():
        scale = scale_of(tile_ref, 2)
        quant_ref[0:inner, :] = clipped(down_ref[...], scale)
        quant_ref[inner:, :] = clipped(other_ref[...], scale)

    blocks = [received_ref[:, j * rows : (j + 1) * rows, :] for j in range(width // LANES)]
    out_rows = jnp.concatenate([block.reshape((-1, LANES)) for block in blocks], axis=1)
    out_ref[...] = out_rows
    partial = contract_last(out_rows, quant_ref[...])
    partial_ref[...] = partial.astype(jnp.bfloat16).reshape(partial_ref.shape)


def hidden_partial(tile, received, down, other):
    blocks, steps = 4, N_CHIP // 4
    inner, width = down.shape
    rows = (received.shape[1] - EXTRA) * LANES // width
    whole = pl.BlockSpec((inner, width), lambda i: (0, 0))
    return pl.pallas_call(
        partial_kernel,
        grid=(steps,),
        out_shape=(
            jax.ShapeDtypeStruct((N_ROW, rows, 2 * inner), jnp.bfloat16),
            jax.ShapeDtypeStruct((N_CHIP * rows, width), jnp.bfloat16),
        ),
        in_specs=[
            pl.BlockSpec(tile.shape, lambda i: (0, 0, 0)),
            pl.BlockSpec((blocks,) + received.shape[1:], lambda i: (i, 0, 0)),
            whole,
            whole,
        ],
        out_specs=(
            pl.BlockSpec((blocks, rows, 2 * inner), lambda i: (i, 0, 0)),
            pl.BlockSpec((blocks * rows, width), lambda i: (i, 0)),
        ),
        scratch_shapes=[pltpu.VMEM((2 * inner, width), jnp.bfloat16)],
        compiler_params=PARAMS,
        cost_estimate=cost(2 * 512 * 896 * 512, 4 << 20),
    )(tile, received, down, other)


def spread_kernel(parts_ref, after_ref, sent_ref):
    total = jnp.sum(parts_ref[...].astype(jnp.float32), axis=0).astype(jnp.bfloat16)
    for k in range(N_ROW):
        sent_ref[k] = total


def spread(parts, after):
    return pl.pallas_call(
        spread_kernel,
        out_shape=jax.ShapeDtypeStruct(parts.shape, jnp.bfloat16),
        in_specs=[VMEM] * 2,
        out_specs=VMEM,
        compiler_params=PARAMS,
        cost_estimate=cost(1 << 19, 2 << 20),
    )(parts, after)


def clip_kernel(tile_ref, gate_ref, up_ref, other_ref, quant_ref):
    inner = gate_ref.shape[0]
    for n, ref in enumerate((gate_ref, up_ref)):
        scale = scale_of(tile_ref, n)
        quant_ref[n, 0:inner, :] = clipped(ref[...], scale)
        quant_ref[n, inner:, :] = clipped(other_ref[n], scale)


def clipped_latents(tile, gate_t, up_t, other):
    inner, width = gate_t.shape
    return pl.pallas_call(
        clip_kernel,
        out_shape=jax.ShapeDtypeStruct((2, 2 * inner, width), jnp.bfloat16),
        in_specs=[VMEM] * 4,
        out_specs=VMEM,
        compiler_params=PARAMS,
        cost_estimate=cost(1 << 20, 4 << 20),
    )(tile, gate_t, up_t, other)


def act_kernel(hid_ref, pre_ref, quant_ref, partial_ref, acts_ref):
    both = hid_ref.shape[2]
    grad_hidden = hid_ref[...].reshape((-1, both)).astype(jnp.float32)
    pre = pre_ref[...].reshape((-1, 2 * both))
    acts = swiglu_grads(grad_hidden, pre[:, :both], pre[:, both:])
    partial = matmul(acts[0], quant_ref[0]) + matmul(acts[1], quant_ref[1])
    partial_ref[...] = partial.astype(jnp.bfloat16).reshape(partial_ref.shape)
    for n, act in enumerate(acts):
        acts_ref[n] = act


def act_partial(grad_hidden, pre_half, quant):
    blocks, steps = 4, N_ROW // 4
    rows, both = grad_hidden.shape[1:]
    width = quant.shape[2]
    return pl.pallas_call(
        act_kernel,
        grid=(steps,),
        out_shape=(
            jax.ShapeDtypeStruct((N_CHIP, rows, width), jnp.bfloat16),
            jax.ShapeDtypeStruct((3, N_ROW * rows, both), jnp.bfloat16),
        ),
        in_specs=[
            pl.BlockSpec((blocks, rows, both), lambda i: (i, 0, 0)),
            pl.BlockSpec((blocks, 1, rows, 2 * both), lambda i: (i % 2, i // 2, 0, 0)),
            pl.BlockSpec(quant.shape, lambda i: (0, 0, 0)),
        ],
        out_specs=(
            pl.BlockSpec((blocks, rows, width), lambda i: (i, 0, 0)),
            pl.BlockSpec((3, blocks * rows, both), lambda i: (0, i, 0)),
        ),
        compiler_params=WIDE,
        cost_estimate=cost(4 * 512 * 896 * 512, 8 << 20),
    )(grad_hidden, pre_half.reshape((N_ROW // 2, 2, rows, 2 * both)), quant)


def latent_grads_kernel(place_ref, acts_ref, out_ref, tokens_ref, own_ref, sent_ref, rows_ref):
    rows = tokens_ref.shape[1]
    for block in range(2 * N_Y):
        flip = (block >> 2) & 1
        offset = 2 * (block & 3) + (block >> 3)
        chip = (place_ref[0] ^ flip) * N_Y + (place_ref[1] ^ offset)
        rows_ref[pl.ds(pl.multiple_of(chip * rows, rows), rows), :] = tokens_ref[block]
    inner = own_ref.shape[1]
    for n in range(3):
        half = out_ref[...] if n == 2 else rows_ref[...]
        grad = contract_first(acts_ref[n], half)
        own_ref[n] = grad[:inner]
        sent_ref[n] = grad[inner:].astype(jnp.bfloat16)


def latent_grads(place, acts, out_half, token_blocks):
    inner, width = acts.shape[2] // 2, out_half.shape[1]
    return pl.pallas_call(
        latent_grads_kernel,
        out_shape=(
            jax.ShapeDtypeStruct((3, inner, width), jnp.float32),
            jax.ShapeDtypeStruct((3, inner, width), jnp.bfloat16),
        ),
        in_specs=[SMEM] + [VMEM] * 3,
        out_specs=(VMEM, VMEM),
        scratch_shapes=[pltpu.VMEM(out_half.shape, jnp.bfloat16)],
        compiler_params=PARAMS,
        cost_estimate=cost(6 * 512 * 896 * 512, 8 << 20),
    )(place, acts, out_half, token_blocks)


def join_kernel(own_ref, other_ref, *refs):
    for n, ref in enumerate(refs[:3]):
        ref[...] = (own_ref[n] + other_ref[n].astype(jnp.float32)).astype(jnp.bfloat16)
    refs[3][...] = jnp.zeros(refs[3].shape, jnp.float32)


def join(own, other):
    grad = jax.ShapeDtypeStruct(own.shape[1:], jnp.bfloat16)
    return pl.pallas_call(
        join_kernel,
        out_shape=(grad, grad, grad, jax.ShapeDtypeStruct((8, LANES), jnp.float32)),
        in_specs=[VMEM] * 2,
        out_specs=(VMEM,) * 4,
        compiler_params=PARAMS,
        cost_estimate=cost(1 << 20, 5 << 20),
    )(own, other)


def total_kernel(parts_ref, after_ref, total_ref):
    total_ref[...] = jnp.sum(parts_ref[...].astype(jnp.float32), axis=0).astype(jnp.bfloat16)


def total(parts, after):
    return pl.pallas_call(
        total_kernel,
        out_shape=jax.ShapeDtypeStruct(parts.shape[1:], jnp.bfloat16),
        in_specs=[VMEM] * 2,
        out_specs=VMEM,
        compiler_params=PARAMS,
        cost_estimate=cost(1 << 18, 1 << 19),
    )(parts, after)


def copy_kernel(values_ref, after_ref, copy_ref):
    copy_ref[...] = values_ref[...]


def copy_after(values, after):
    return pl.pallas_call(
        copy_kernel,
        out_shape=jax.ShapeDtypeStruct(values.shape, values.dtype),
        in_specs=[VMEM] * 2,
        out_specs=VMEM,
        cost_estimate=cost(1, 1 << 16),
    )(values, after)


def exchanged(blocks, axis, *steps):
    count = 2 if axis == "xl" else N_Y
    others = [lax.ppermute(blocks, axis, [(k, k ^ step) for k in range(count)]) for step in steps]
    return jnp.concatenate([blocks] + others, axis=0)


def far_tokens(tokens, done):
    blocks = exchanged(copy_after(tokens, done)[None], "y", 2, 4, 6)
    return blocks, blocks[-1, :EXTRA, :LANES]


def own_half(core, gate_pre, up_pre):
    inner = gate_pre.shape[1]
    pre = jnp.concatenate([gate_pre, up_pre], axis=1).reshape((2, -1, 2 * inner))
    own = lax.dynamic_index_in_dim(pre, core, 0, keepdims=False)
    other = swapped(lax.dynamic_index_in_dim(pre, 1 - core, 0, keepdims=False))
    rows = jnp.concatenate(
        [own[:, :inner], other[:, :inner], own[:, inner:], other[:, inner:]], axis=1
    )
    other = lax.ppermute(rows, "xh", [(0, 1), (1, 0)])
    pair = jnp.where(
        lax.axis_index("xh") == 0, jnp.stack([rows, other]), jnp.stack([other, rows])
    )
    return pair.reshape((-1, 4 * inner)), pair[0, :EXTRA, :LANES]


def in_branch(work, *operands):
    def nothing(*operands):
        shapes = jax.eval_shape(work, *operands)
        return tuple(jnp.zeros(leaf.shape, leaf.dtype) for leaf in shapes)

    def always(*operands):
        return tuple(work(*operands))

    return lax.cond(lax.axis_index("z") < 8, always, nothing, *operands)


def shards(tokens, grad_out, gate_pre, up_pre, gate_latent, up_latent, down_latent):
    core = lax.axis_index("core")
    place = jnp.stack([lax.axis_index("xl"), lax.axis_index("y")]).astype(jnp.int32)
    gate_t, up_t = gate_latent.T, up_latent.T
    sent = first(grad_out, gate_t, up_t, down_latent)

    def gathers(sent, core, gate_pre, up_pre, down):
        received = lax.all_to_all(sent, CHIP, 0, 0)
        down_other = swapped(down)
        pre_rows, after = in_branch(own_half, core, gate_pre, up_pre)
        return (received, down_other, pre_rows, sums_tile(received, after))

    received, down_other, pre_rows, tile = in_branch(
        gathers, sent, core, gate_pre, up_pre, down_latent
    )
    pre_half = lax.all_gather(pre_rows, "z", axis=0, tiled=True)

    def exchanges(received, tile, tokens, gate_t, up_t, down, down_other):
        tile = lax.all_to_all(tile, ROW + ("core",), 0, 0)
        partial, out_half = hidden_partial(tile, received, down, down_other)
        parts = lax.all_to_all(partial, ROW, 0, 0)
        far, after = in_branch(far_tokens, tokens, out_half[:EXTRA, :LANES])
        other_latents = swapped(jnp.stack([gate_t, up_t]))
        quant = clipped_latents(tile, gate_t, up_t, other_latents)
        token_blocks = exchanged(exchanged(far, "xl", 1), "y", 1)
        grad_hidden = lax.all_to_all(spread(parts, after), ROW, 0, 0)
        return (out_half, quant, grad_hidden, token_blocks)

    out_half, quant, grad_hidden, token_blocks = in_branch(
        exchanges, received, tile, tokens, gate_t, up_t, down_latent, down_other
    )

    partial, acts = act_partial(grad_hidden, pre_half, quant)
    parts = lax.all_to_all(partial, CHIP, 0, 0)

    def joined(place, acts, out_half, token_blocks):
        own, sent = latent_grads(place, acts, out_half, token_blocks)
        return join(own, swapped(sent))

    grad_gate, grad_up, grad_down, done = in_branch(joined, place, acts, out_half, token_blocks)
    grad_tokens = total(parts, done)
    return (grad_tokens, grad_gate.T, grad_up.T, grad_down)


def solution(mesh):
    fine = Mesh(mesh.devices.reshape((2, 8, 2, 8, 2)), ROW + CHIP + ("core",))
    col = CHIP + ("core",)
    in_specs = (
        P(col, ROW),
        P(col, ROW),
        P(ROW, col),
        P(ROW, col),
        P(ROW, col),
        P(ROW, col),
        P(col, ROW),
    )
    out_specs = (P(col, ROW), P(ROW, col), P(ROW, col), P(col, ROW))
    return jax.shard_map(shards, mesh=fine, in_specs=in_specs, out_specs=out_specs, check_vma=False)
```

```python
import jax
import jax.numpy as jnp
from jax import lax
from jax.experimental import pallas as pl
from jax.experimental.pallas import tpu as pltpu
from jax.sharding import Mesh, PartitionSpec as P

EMBED_SIZE = 8192
GATE_INNER_SIZE = 14336
N_ROW = 16
N_CHIP = 16
ROW = ("xh", "z")
CHIP = ("xl", "y")
EXTRA = 16
N_Y = 8
LANES = 128
VMEM = pl.BlockSpec(memory_space=pltpu.VMEM)
SMEM = pl.BlockSpec(memory_space=pltpu.SMEM)
ANY = pl.BlockSpec(memory_space=pl.ANY)
WIDE = pltpu.CompilerParams(vmem_limit_bytes=58 * 1024 * 1024)
PARAMS = pltpu.CompilerParams(vmem_limit_bytes=40 * 1024 * 1024)


def cost(flops, bytes_accessed):
    return pl.CostEstimate(flops=flops, bytes_accessed=bytes_accessed, transcendentals=0)


def contract_last(left, right):
    return lax.dot_general(
        left, right, (((1,), (1,)), ((), ())), preferred_element_type=jnp.float32
    )


def contract_first(left, right):
    return lax.dot_general(
        left, right, (((0,), (0,)), ((), ())), preferred_element_type=jnp.float32
    )


def matmul(left, right):
    return lax.dot_general(
        left, right, (((1,), (0,)), ((), ())), preferred_element_type=jnp.float32
    )


def swiglu_grads(grad_hidden, gate_pre, up_pre):
    gate_f = gate_pre.astype(jnp.float32)
    up_f = up_pre.astype(jnp.float32)
    sigma = jax.nn.sigmoid(gate_f)
    silu_gate = gate_f * sigma
    slope = sigma * (1.0 + gate_f - silu_gate)
    grad_gpre = (grad_hidden * (up_f * slope)).astype(jnp.bfloat16)
    grad_upre = (grad_hidden * silu_gate).astype(jnp.bfloat16)
    hidden = (silu_gate * up_f).astype(jnp.bfloat16)
    return (grad_gpre, grad_upre, hidden)


def swapped(values):
    return lax.ppermute(values, "core", [(0, 1), (1, 0)])


def pieces_of(totals):
    pieces = []
    for total in totals:
        for _ in range(3):
            piece = total.astype(jnp.bfloat16).astype(jnp.float32)
            pieces.append(piece)
            total = total - piece
    pieces.append(jnp.zeros((EXTRA - len(pieces), totals[0].shape[1]), jnp.float32))
    return jnp.concatenate(pieces, axis=0).astype(jnp.bfloat16)


def totals_of(pieces):
    return [jnp.sum(pieces[3 * k : 3 * k + 3], axis=0, keepdims=True) for k in range(3)]


def first_kernel(out_ref, gate_ref, up_ref, down_ref, sent_ref):
    sums = []
    for ref in (gate_ref, up_ref, down_ref):
        total = jnp.sum(jnp.abs(ref[...].astype(jnp.float32)), axis=0, keepdims=True)
        sums.append(jnp.broadcast_to(jnp.sum(total, axis=1, keepdims=True), (1, LANES)))
    blocks = [out_ref[:, j * LANES : (j + 1) * LANES] for j in range(out_ref.shape[1] // LANES)]
    block = jnp.concatenate(blocks + [pieces_of(sums)], axis=0)
    for k in range(N_CHIP):
        sent_ref[k] = block


def first(grad_out, gate_t, up_t, down):
    rows, width = grad_out.shape
    return pl.pallas_call(
        first_kernel,
        out_shape=jax.ShapeDtypeStruct((N_CHIP, rows * width // LANES + EXTRA, LANES), jnp.bfloat16),
        in_specs=[VMEM] * 4,
        out_specs=VMEM,
        compiler_params=WIDE,
        cost_estimate=cost(1 << 20, 5 << 19),
    )(grad_out, gate_t, up_t, down)


def tile_kernel(extra_ref, after_ref, tile_ref):
    sums = totals_of(jnp.sum(extra_ref[...].astype(jnp.float32), axis=0))
    tile = jnp.concatenate(sums + [jnp.zeros((5, LANES), jnp.float32)], axis=0)
    tile_ref[...] = jnp.broadcast_to(tile[None], tile_ref.shape)


def sums_tile(received, after):
    rows = received.shape[1] - EXTRA
    return pl.pallas_call(
        tile_kernel,
        grid=(1,),
        out_shape=jax.ShapeDtypeStruct((2 * N_ROW, 8, LANES), jnp.float32),
        in_specs=[
            pl.BlockSpec((N_CHIP, EXTRA, LANES), lambda i: (0, rows // EXTRA, 0)),
            ANY,
        ],
        out_specs=pl.BlockSpec((2 * N_ROW, 8, LANES), lambda i: (0, 0, 0)),
        compiler_params=PARAMS,
        cost_estimate=cost(1 << 16, 1 << 18),
    )(received, after)


def scale_of(tile_ref, which):
    total = jnp.sum(tile_ref[...], axis=0)[which : which + 1, 0:1]
    return total / float(EMBED_SIZE * GATE_INNER_SIZE) + 1e-05


def clipped(values, scale):
    return jnp.clip(values.astype(jnp.float32), -scale, scale).astype(jnp.bfloat16)


def laid_out_kernel(received_ref, down_ref, other_ref, out_ref, both_ref):
    width = out_ref.shape[1]
    rows = (received_ref.shape[1] - EXTRA) * LANES // width
    for j in range(width // LANES):
        block = received_ref[:, j * rows : (j + 1) * rows, :].reshape((-1, LANES))
        out_ref[:, j * LANES : (j + 1) * LANES] = block
    both_ref[0] = down_ref[...]
    both_ref[1] = other_ref[...]


def laid_out(received, down, other):
    inner, width = down.shape
    rows = (received.shape[1] - EXTRA) * LANES // width
    return pl.pallas_call(
        laid_out_kernel,
        out_shape=(
            jax.ShapeDtypeStruct((N_CHIP * rows, width), jnp.bfloat16),
            jax.ShapeDtypeStruct((2, inner, width), jnp.bfloat16),
        ),
        in_specs=[VMEM] * 3,
        out_specs=(VMEM, VMEM),
        compiler_params=PARAMS,
        cost_estimate=cost(1 << 10, 3 << 20),
    )(received, down, other)


def partial_kernel(tile_ref, out_ref, both_ref, partial_ref):
    inner, width = both_ref.shape[1:]
    quant = clipped(both_ref[...].reshape((2 * inner, width)), scale_of(tile_ref, 2))
    rows = out_ref.shape[0] // 4
    blocks = partial_ref.shape[0] // 4
    for n in range(4):
        partial = contract_last(out_ref[n * rows : (n + 1) * rows, :], quant).astype(jnp.bfloat16)
        partial_ref[n * blocks : (n + 1) * blocks] = partial.reshape((blocks, -1, 2 * inner))


def hidden_partial(tile, out_half, both):
    inner = both.shape[1]
    rows = out_half.shape[0] // N_CHIP
    return pl.pallas_call(
        partial_kernel,
        out_shape=jax.ShapeDtypeStruct((N_ROW, rows, 2 * inner), jnp.bfloat16),
        in_specs=[VMEM] * 3,
        out_specs=VMEM,
        compiler_params=PARAMS,
        cost_estimate=cost(2 * 512 * 896 * 512, 4 << 20),
    )(tile, out_half, both)


def spread_kernel(parts_ref, after_ref, sent_ref):
    total = jnp.sum(parts_ref[...].astype(jnp.float32), axis=0).astype(jnp.bfloat16)
    for k in range(N_ROW):
        sent_ref[k] = total


def spread(parts, after):
    return pl.pallas_call(
        spread_kernel,
        out_shape=jax.ShapeDtypeStruct(parts.shape, jnp.bfloat16),
        in_specs=[VMEM, ANY],
        out_specs=VMEM,
        compiler_params=PARAMS,
        cost_estimate=cost(1 << 19, 2 << 20),
    )(parts, after)


def clip_kernel(tile_ref, gate_ref, up_ref, other_ref, quant_ref):
    inner = gate_ref.shape[0]
    for n, ref in enumerate((gate_ref, up_ref)):
        scale = scale_of(tile_ref, n)
        quant_ref[n, 0:inner, :] = clipped(ref[...], scale)
        quant_ref[n, inner:, :] = clipped(other_ref[n], scale)


def clipped_latents(tile, gate_t, up_t, other):
    inner, width = gate_t.shape
    return pl.pallas_call(
        clip_kernel,
        out_shape=jax.ShapeDtypeStruct((2, 2 * inner, width), jnp.bfloat16),
        in_specs=[VMEM] * 4,
        out_specs=VMEM,
        compiler_params=PARAMS,
        cost_estimate=cost(1 << 20, 4 << 20),
    )(tile, gate_t, up_t, other)


def act_kernel(hid_ref, pre_ref, quant_ref, partial_ref, acts_ref):
    both = hid_ref.shape[2]
    grad_hidden = hid_ref[...].reshape((-1, both)).astype(jnp.float32)
    pre = pre_ref[...].reshape((-1, 2 * both))
    acts = swiglu_grads(grad_hidden, pre[:, :both], pre[:, both:])
    partial = matmul(acts[0], quant_ref[0]) + matmul(acts[1], quant_ref[1])
    partial_ref[...] = partial.astype(jnp.bfloat16).reshape(partial_ref.shape)
    for n, act in enumerate(acts):
        acts_ref[n] = act


def act_partial(grad_hidden, pre_half, quant):
    blocks, steps = 4, N_ROW // 4
    rows, both = grad_hidden.shape[1:]
    width = quant.shape[2]
    return pl.pallas_call(
        act_kernel,
        grid=(steps,),
        out_shape=(
            jax.ShapeDtypeStruct((N_CHIP, rows, width), jnp.bfloat16),
            jax.ShapeDtypeStruct((3, N_ROW * rows, both), jnp.bfloat16),
        ),
        in_specs=[
            pl.BlockSpec((blocks, rows, both), lambda i: (i, 0, 0)),
            pl.BlockSpec((blocks, 1, rows, 2 * both), lambda i: (i % 2, i // 2, 0, 0)),
            pl.BlockSpec(quant.shape, lambda i: (0, 0, 0)),
        ],
        out_specs=(
            pl.BlockSpec((blocks, rows, width), lambda i: (i, 0, 0)),
            pl.BlockSpec((3, blocks * rows, both), lambda i: (0, i, 0)),
        ),
        compiler_params=WIDE,
        cost_estimate=cost(4 * 512 * 896 * 512, 8 << 20),
    )(grad_hidden, pre_half.reshape((N_ROW // 2, 2, rows, 2 * both)), quant)


def latent_grads_kernel(place_ref, acts_ref, out_ref, tokens_ref, own_ref, sent_ref, rows_ref):
    rows = tokens_ref.shape[1]
    for block in range(2 * N_Y):
        flip = (block >> 2) & 1
        offset = 2 * (block & 3) + (block >> 3)
        chip = (place_ref[0] ^ flip) * N_Y + (place_ref[1] ^ offset)
        rows_ref[pl.ds(pl.multiple_of(chip * rows, rows), rows), :] = tokens_ref[block]
    inner = own_ref.shape[1]
    for n in range(3):
        half = out_ref[...] if n == 2 else rows_ref[...]
        grad = contract_first(acts_ref[n], half)
        own_ref[n] = grad[:inner]
        sent_ref[n] = grad[inner:].astype(jnp.bfloat16)


def latent_grads(place, acts, out_half, token_blocks):
    inner, width = acts.shape[2] // 2, out_half.shape[1]
    return pl.pallas_call(
        latent_grads_kernel,
        out_shape=(
            jax.ShapeDtypeStruct((3, inner, width), jnp.float32),
            jax.ShapeDtypeStruct((3, inner, width), jnp.bfloat16),
        ),
        in_specs=[SMEM] + [VMEM] * 3,
        out_specs=(VMEM, VMEM),
        scratch_shapes=[pltpu.VMEM(out_half.shape, jnp.bfloat16)],
        compiler_params=PARAMS,
        cost_estimate=cost(6 * 512 * 896 * 512, 8 << 20),
    )(place, acts, out_half, token_blocks)


def join_kernel(own_ref, other_ref, *refs):
    for n, ref in enumerate(refs[:3]):
        ref[...] = (own_ref[n] + other_ref[n].astype(jnp.float32)).astype(jnp.bfloat16)
    refs[3][...] = jnp.zeros(refs[3].shape, jnp.float32)


def join(own, other):
    grad = jax.ShapeDtypeStruct(own.shape[1:], jnp.bfloat16)
    return pl.pallas_call(
        join_kernel,
        out_shape=(grad, grad, grad, jax.ShapeDtypeStruct((8, LANES), jnp.float32)),
        in_specs=[VMEM] * 2,
        out_specs=(VMEM,) * 4,
        compiler_params=PARAMS,
        cost_estimate=cost(1 << 20, 5 << 20),
    )(own, other)


def total_kernel(parts_ref, after_ref, total_ref):
    total_ref[...] = jnp.sum(parts_ref[...].astype(jnp.float32), axis=0).astype(jnp.bfloat16)


def total(parts, after):
    return pl.pallas_call(
        total_kernel,
        out_shape=jax.ShapeDtypeStruct(parts.shape[1:], jnp.bfloat16),
        in_specs=[VMEM] * 2,
        out_specs=VMEM,
        compiler_params=PARAMS,
        cost_estimate=cost(1 << 18, 1 << 19),
    )(parts, after)


def copy_kernel(values_ref, after_ref, copy_ref):
    copy_ref[...] = values_ref[...]


def copy_after(values, after):
    return pl.pallas_call(
        copy_kernel,
        out_shape=jax.ShapeDtypeStruct(values.shape, values.dtype),
        in_specs=[VMEM, ANY],
        out_specs=VMEM,
        cost_estimate=cost(1, 1 << 16),
    )(values, after)


def exchanged(blocks, axis, *steps):
    count = N_CHIP if axis == CHIP else N_Y
    others = [lax.ppermute(blocks, axis, [(k, k ^ step) for k in range(count)]) for step in steps]
    return jnp.concatenate([blocks] + others, axis=0)


def far_work(tokens, done, tile, gate_t, up_t):
    other_latents = swapped(jnp.stack([gate_t, up_t]))
    blocks = exchanged(copy_after(tokens, done)[None], "y", 2, 4, 6)
    return blocks, clipped_latents(tile, gate_t, up_t, other_latents)


def own_half(core, gate_pre, up_pre):
    inner = gate_pre.shape[1]
    pre = jnp.concatenate([gate_pre, up_pre], axis=1).reshape((2, -1, 2 * inner))
    own = lax.dynamic_index_in_dim(pre, core, 0, keepdims=False)
    other = swapped(lax.dynamic_index_in_dim(pre, 1 - core, 0, keepdims=False))
    rows = jnp.concatenate(
        [own[:, :inner], other[:, :inner], own[:, inner:], other[:, inner:]], axis=1
    )
    other = lax.ppermute(rows, "xh", [(0, 1), (1, 0)])
    pair = jnp.where(
        lax.axis_index("xh") == 0, jnp.stack([rows, other]), jnp.stack([other, rows])
    )
    return (pair.reshape((-1, 4 * inner)),)


def in_branch(work, *operands):
    def nothing(*operands):
        shapes = jax.eval_shape(work, *operands)
        return tuple(jnp.zeros(leaf.shape, leaf.dtype) for leaf in shapes)

    def always(*operands):
        return tuple(work(*operands))

    return lax.cond(lax.axis_index("z") < 8, always, nothing, *operands)


def shards(tokens, grad_out, gate_pre, up_pre, gate_latent, up_latent, down_latent):
    core = lax.axis_index("core")
    place = jnp.stack([lax.axis_index("xl"), lax.axis_index("y")]).astype(jnp.int32)
    gate_t, up_t = gate_latent.T, up_latent.T
    sent = first(grad_out, gate_t, up_t, down_latent)

    def gathers(sent, core, gate_pre, up_pre, down):
        received = lax.all_to_all(sent, CHIP, 0, 0)
        down_other = swapped(down)
        (pre_rows,) = in_branch(own_half, core, gate_pre, up_pre)
        return (received, down_other, pre_rows, sums_tile(received, pre_rows))

    received, down_other, pre_rows, tile = in_branch(
        gathers, sent, core, gate_pre, up_pre, down_latent
    )
    pre_half = lax.all_gather(pre_rows, "z", axis=0, tiled=True)

    def exchanges(received, tile, tokens, gate_t, up_t, down, down_other):
        tile = lax.all_to_all(tile, ROW + ("core",), 0, 0)
        out_half, both = laid_out(received, down, down_other)
        partial = hidden_partial(tile, out_half, both)
        parts = lax.all_to_all(partial, ROW, 0, 0)
        far, quant = in_branch(far_work, tokens, partial, tile, gate_t, up_t)
        token_blocks = exchanged(far, CHIP, N_Y, 1, N_Y + 1)
        grad_hidden = lax.all_to_all(spread(parts, far), ROW, 0, 0)
        return (out_half, quant, grad_hidden, token_blocks)

    out_half, quant, grad_hidden, token_blocks = in_branch(
        exchanges, received, tile, tokens, gate_t, up_t, down_latent, down_other
    )

    partial, acts = act_partial(grad_hidden, pre_half, quant)
    parts = lax.all_to_all(partial, CHIP, 0, 0)

    def joined(place, acts, out_half, token_blocks):
        own, sent = latent_grads(place, acts, out_half, token_blocks)
        return join(own, swapped(sent))

    grad_gate, grad_up, grad_down, done = in_branch(joined, place, acts, out_half, token_blocks)
    grad_tokens = total(parts, done)
    return (grad_tokens, grad_gate.T, grad_up.T, grad_down)


def solution(mesh):
    fine = Mesh(mesh.devices.reshape((2, 8, 2, 8, 2)), ROW + CHIP + ("core",))
    col = CHIP + ("core",)
    in_specs = (
        P(col, ROW),
        P(col, ROW),
        P(ROW, col),
        P(ROW, col),
        P(ROW, col),
        P(ROW, col),
        P(col, ROW),
    )
    out_specs = (P(col, ROW), P(ROW, col), P(ROW, col), P(col, ROW))
    return jax.shard_map(shards, mesh=fine, in_specs=in_specs, out_specs=out_specs, check_vma=False)
```

```python
import jax
import jax.numpy as jnp
from jax import lax
from jax.experimental import pallas as pl
from jax.experimental.pallas import tpu as pltpu
from jax.sharding import Mesh, PartitionSpec as P

EMBED_SIZE = 8192
GATE_INNER_SIZE = 14336
N_ROW = 16
N_CHIP = 16
ROW = ("xh", "z")
CHIP = ("xl", "y")
EXTRA = 16
N_Y = 8
LANES = 128
VMEM = pl.BlockSpec(memory_space=pltpu.VMEM)
SMEM = pl.BlockSpec(memory_space=pltpu.SMEM)
ANY = pl.BlockSpec(memory_space=pl.ANY)
WIDE = pltpu.CompilerParams(vmem_limit_bytes=58 * 1024 * 1024)
PARAMS = pltpu.CompilerParams(vmem_limit_bytes=40 * 1024 * 1024)


def cost(flops, bytes_accessed):
    return pl.CostEstimate(flops=flops, bytes_accessed=bytes_accessed, transcendentals=0)


def contract_last(left, right):
    return lax.dot_general(
        left, right, (((1,), (1,)), ((), ())), preferred_element_type=jnp.float32
    )


def contract_first(left, right):
    return lax.dot_general(
        left, right, (((0,), (0,)), ((), ())), preferred_element_type=jnp.float32
    )


def matmul(left, right):
    return lax.dot_general(
        left, right, (((1,), (0,)), ((), ())), preferred_element_type=jnp.float32
    )


def swiglu_grads(grad_hidden, gate_pre, up_pre):
    gate_f = gate_pre.astype(jnp.float32)
    up_f = up_pre.astype(jnp.float32)
    sigma = jax.nn.sigmoid(gate_f)
    silu_gate = gate_f * sigma
    slope = sigma * (1.0 + gate_f - silu_gate)
    grad_gpre = (grad_hidden * (up_f * slope)).astype(jnp.bfloat16)
    grad_upre = (grad_hidden * silu_gate).astype(jnp.bfloat16)
    hidden = (silu_gate * up_f).astype(jnp.bfloat16)
    return (grad_gpre, grad_upre, hidden)


def swapped(values):
    return lax.ppermute(values, "core", [(0, 1), (1, 0)])


def pieces_of(totals):
    pieces = []
    for total in totals:
        for _ in range(3):
            piece = total.astype(jnp.bfloat16).astype(jnp.float32)
            pieces.append(piece)
            total = total - piece
    pieces.append(jnp.zeros((EXTRA - len(pieces), totals[0].shape[1]), jnp.float32))
    return jnp.concatenate(pieces, axis=0).astype(jnp.bfloat16)


def totals_of(pieces):
    return [jnp.sum(pieces[3 * k : 3 * k + 3], axis=0, keepdims=True) for k in range(3)]


def first_kernel(out_ref, gate_ref, up_ref, down_ref, sent_ref):
    sums = []
    for ref in (gate_ref, up_ref, down_ref):
        total = jnp.sum(jnp.abs(ref[...].astype(jnp.float32)), axis=0, keepdims=True)
        sums.append(jnp.broadcast_to(jnp.sum(total, axis=1, keepdims=True), (1, LANES)))
    blocks = [out_ref[:, j * LANES : (j + 1) * LANES] for j in range(out_ref.shape[1] // LANES)]
    block = jnp.concatenate(blocks + [pieces_of(sums)], axis=0)
    for k in range(N_CHIP):
        sent_ref[k] = block


def first(grad_out, gate_t, up_t, down):
    rows, width = grad_out.shape
    return pl.pallas_call(
        first_kernel,
        out_shape=jax.ShapeDtypeStruct((N_CHIP, rows * width // LANES + EXTRA, LANES), jnp.bfloat16),
        in_specs=[VMEM] * 4,
        out_specs=VMEM,
        compiler_params=WIDE,
        cost_estimate=cost(1 << 20, 5 << 19),
    )(grad_out, gate_t, up_t, down)


def tile_kernel(extra_ref, tile_ref):
    sums = totals_of(jnp.sum(extra_ref[...].astype(jnp.float32), axis=0))
    tile = jnp.concatenate(sums + [jnp.zeros((5, LANES), jnp.float32)], axis=0)
    tile_ref[...] = jnp.broadcast_to(tile[None], tile_ref.shape)


def sums_tile(received):
    rows = received.shape[1] - EXTRA
    return pl.pallas_call(
        tile_kernel,
        grid=(1,),
        out_shape=jax.ShapeDtypeStruct((2 * N_ROW, 8, LANES), jnp.float32),
        in_specs=[
            pl.BlockSpec((N_CHIP, EXTRA, LANES), lambda i: (0, rows // EXTRA, 0)),
        ],
        out_specs=pl.BlockSpec((2 * N_ROW, 8, LANES), lambda i: (0, 0, 0)),
        compiler_params=PARAMS,
        cost_estimate=cost(1 << 16, 1 << 18),
    )(received)


def scale_of(tile_ref, which):
    total = jnp.sum(tile_ref[...], axis=0)[which : which + 1, 0:1]
    return total / float(EMBED_SIZE * GATE_INNER_SIZE) + 1e-05


def clipped(values, scale):
    return jnp.clip(values.astype(jnp.float32), -scale, scale).astype(jnp.bfloat16)


def laid_out_kernel(received_ref, down_ref, other_ref, out_ref, both_ref):
    width = out_ref.shape[1]
    rows = (received_ref.shape[1] - EXTRA) * LANES // width
    for j in range(width // LANES):
        block = received_ref[:, j * rows : (j + 1) * rows, :].reshape((-1, LANES))
        out_ref[:, j * LANES : (j + 1) * LANES] = block
    both_ref[0] = down_ref[...]
    both_ref[1] = other_ref[...]


def laid_out(received, down, other):
    inner, width = down.shape
    rows = (received.shape[1] - EXTRA) * LANES // width
    return pl.pallas_call(
        laid_out_kernel,
        out_shape=(
            jax.ShapeDtypeStruct((N_CHIP * rows, width), jnp.bfloat16),
            jax.ShapeDtypeStruct((2, inner, width), jnp.bfloat16),
        ),
        in_specs=[VMEM] * 3,
        out_specs=(VMEM, VMEM),
        compiler_params=PARAMS,
        cost_estimate=cost(1 << 10, 3 << 20),
    )(received, down, other)


def partial_kernel(tile_ref, out_ref, both_ref, partial_ref):
    inner, width = both_ref.shape[1:]
    quant = clipped(both_ref[...].reshape((2 * inner, width)), scale_of(tile_ref, 2))
    rows = out_ref.shape[0] // 4
    blocks = partial_ref.shape[0] // 4
    for n in range(4):
        partial = contract_last(out_ref[n * rows : (n + 1) * rows, :], quant).astype(jnp.bfloat16)
        partial_ref[n * blocks : (n + 1) * blocks] = partial.reshape((blocks, -1, 2 * inner))


def hidden_partial(tile, out_half, both):
    inner = both.shape[1]
    rows = out_half.shape[0] // N_CHIP
    return pl.pallas_call(
        partial_kernel,
        out_shape=jax.ShapeDtypeStruct((N_ROW, rows, 2 * inner), jnp.bfloat16),
        in_specs=[VMEM] * 3,
        out_specs=VMEM,
        compiler_params=PARAMS,
        cost_estimate=cost(2 * 512 * 896 * 512, 4 << 20),
    )(tile, out_half, both)


def spread_kernel(parts_ref, after_ref, sent_ref):
    total = jnp.sum(parts_ref[...].astype(jnp.float32), axis=0).astype(jnp.bfloat16)
    for k in range(N_ROW):
        sent_ref[k] = total


def spread(parts, after):
    return pl.pallas_call(
        spread_kernel,
        out_shape=jax.ShapeDtypeStruct(parts.shape, jnp.bfloat16),
        in_specs=[VMEM, ANY],
        out_specs=VMEM,
        compiler_params=PARAMS,
        cost_estimate=cost(1 << 19, 2 << 20),
    )(parts, after)


def clip_kernel(tile_ref, gate_ref, up_ref, other_ref, quant_ref):
    inner = gate_ref.shape[0]
    for n, ref in enumerate((gate_ref, up_ref)):
        scale = scale_of(tile_ref, n)
        quant_ref[n, 0:inner, :] = clipped(ref[...], scale)
        quant_ref[n, inner:, :] = clipped(other_ref[n], scale)


def clipped_latents(tile, gate_t, up_t, other):
    inner, width = gate_t.shape
    return pl.pallas_call(
        clip_kernel,
        out_shape=jax.ShapeDtypeStruct((2, 2 * inner, width), jnp.bfloat16),
        in_specs=[VMEM] * 4,
        out_specs=VMEM,
        compiler_params=PARAMS,
        cost_estimate=cost(1 << 20, 4 << 20),
    )(tile, gate_t, up_t, other)


def act_kernel(hid_ref, pre_ref, quant_ref, partial_ref, acts_ref):
    both = hid_ref.shape[2]
    grad_hidden = hid_ref[...].reshape((-1, both)).astype(jnp.float32)
    pre = pre_ref[...].reshape((-1, 2 * both))
    acts = swiglu_grads(grad_hidden, pre[:, :both], pre[:, both:])
    partial = matmul(acts[0], quant_ref[0]) + matmul(acts[1], quant_ref[1])
    partial_ref[...] = partial.astype(jnp.bfloat16).reshape(partial_ref.shape)
    for n, act in enumerate(acts):
        acts_ref[n] = act


def act_partial(grad_hidden, pre_half, quant):
    blocks, steps = 4, N_ROW // 4
    rows, both = grad_hidden.shape[1:]
    width = quant.shape[2]
    return pl.pallas_call(
        act_kernel,
        grid=(steps,),
        out_shape=(
            jax.ShapeDtypeStruct((N_CHIP, rows, width), jnp.bfloat16),
            jax.ShapeDtypeStruct((3, N_ROW * rows, both), jnp.bfloat16),
        ),
        in_specs=[
            pl.BlockSpec((blocks, rows, both), lambda i: (i, 0, 0)),
            pl.BlockSpec((blocks, 1, rows, 2 * both), lambda i: (i % 2, i // 2, 0, 0)),
            pl.BlockSpec(quant.shape, lambda i: (0, 0, 0)),
        ],
        out_specs=(
            pl.BlockSpec((blocks, rows, width), lambda i: (i, 0, 0)),
            pl.BlockSpec((3, blocks * rows, both), lambda i: (0, i, 0)),
        ),
        compiler_params=WIDE,
        cost_estimate=cost(4 * 512 * 896 * 512, 8 << 20),
    )(grad_hidden, pre_half.reshape((N_ROW // 2, 2, rows, 2 * both)), quant)


def latent_grads_kernel(place_ref, acts_ref, out_ref, tokens_ref, own_ref, sent_ref, rows_ref):
    rows = tokens_ref.shape[1]
    for block in range(2 * N_Y):
        flip = (block >> 2) & 1
        offset = 2 * (block & 3) + (block >> 3)
        chip = (place_ref[0] ^ flip) * N_Y + (place_ref[1] ^ offset)
        rows_ref[pl.ds(pl.multiple_of(chip * rows, rows), rows), :] = tokens_ref[block]
    inner = own_ref.shape[1]
    for n in range(3):
        half = out_ref[...] if n == 2 else rows_ref[...]
        grad = contract_first(acts_ref[n], half)
        own_ref[n] = grad[:inner]
        sent_ref[n] = grad[inner:].astype(jnp.bfloat16)


def latent_grads(place, acts, out_half, token_blocks):
    inner, width = acts.shape[2] // 2, out_half.shape[1]
    return pl.pallas_call(
        latent_grads_kernel,
        out_shape=(
            jax.ShapeDtypeStruct((3, inner, width), jnp.float32),
            jax.ShapeDtypeStruct((3, inner, width), jnp.bfloat16),
        ),
        in_specs=[SMEM] + [VMEM] * 3,
        out_specs=(VMEM, VMEM),
        scratch_shapes=[pltpu.VMEM(out_half.shape, jnp.bfloat16)],
        compiler_params=PARAMS,
        cost_estimate=cost(6 * 512 * 896 * 512, 8 << 20),
    )(place, acts, out_half, token_blocks)


def join_kernel(own_ref, other_ref, *refs):
    for n, ref in enumerate(refs[:3]):
        ref[...] = (own_ref[n] + other_ref[n].astype(jnp.float32)).astype(jnp.bfloat16)
    refs[3][...] = jnp.zeros(refs[3].shape, jnp.float32)


def join(own, other):
    grad = jax.ShapeDtypeStruct(own.shape[1:], jnp.bfloat16)
    return pl.pallas_call(
        join_kernel,
        out_shape=(grad, grad, grad, jax.ShapeDtypeStruct((8, LANES), jnp.float32)),
        in_specs=[VMEM] * 2,
        out_specs=(VMEM,) * 4,
        compiler_params=PARAMS,
        cost_estimate=cost(1 << 20, 5 << 20),
    )(own, other)


def total_kernel(parts_ref, after_ref, total_ref):
    total_ref[...] = jnp.sum(parts_ref[...].astype(jnp.float32), axis=0).astype(jnp.bfloat16)


def total(parts, after):
    return pl.pallas_call(
        total_kernel,
        out_shape=jax.ShapeDtypeStruct(parts.shape[1:], jnp.bfloat16),
        in_specs=[VMEM] * 2,
        out_specs=VMEM,
        compiler_params=PARAMS,
        cost_estimate=cost(1 << 18, 1 << 19),
    )(parts, after)


def copy_kernel(values_ref, after_ref, copy_ref):
    copy_ref[...] = values_ref[...]


def copy_after(values, after):
    return pl.pallas_call(
        copy_kernel,
        out_shape=jax.ShapeDtypeStruct(values.shape, values.dtype),
        in_specs=[VMEM, ANY],
        out_specs=VMEM,
        cost_estimate=cost(1, 1 << 16),
    )(values, after)


def exchanged(blocks, axis, *steps):
    count = N_CHIP if axis == CHIP else N_Y
    others = [lax.ppermute(blocks, axis, [(k, k ^ step) for k in range(count)]) for step in steps]
    return jnp.concatenate([blocks] + others, axis=0)


def far_work(tokens, done, tile, gate_t, up_t):
    other_latents = swapped(jnp.stack([gate_t, up_t]))
    blocks = exchanged(copy_after(tokens, done)[None], "y", 2, 4, 6)
    return blocks, clipped_latents(tile, gate_t, up_t, other_latents)


def half_of(ref, core):
    rows = ref.shape[0] // 2
    return ref[pl.ds(pl.multiple_of(core * rows, rows), rows), :]


def pre_rows_kernel(mine_ref, gate_pre_ref, up_pre_ref, near_ref, far_ref, both_ref, after_ref, rows_ref):
    rows, inner = gate_pre_ref.shape[0] // 2, gate_pre_ref.shape[1]
    core, xh = mine_ref[0], mine_ref[1]
    near, far, both = near_ref[...], far_ref[...], both_ref[...]
    own = [half_of(gate_pre_ref, core), near[:, :inner], half_of(up_pre_ref, core), near[:, inner:]]
    other = [far[:, :inner], both[:, :inner], far[:, inner:], both[:, inner:]]
    for at, parts in ((xh, own), (1 - xh, other)):
        rows_ref[pl.ds(pl.multiple_of(at * rows, rows), rows), :] = jnp.concatenate(parts, axis=1)


def own_half(mine, gate_pre, up_pre, after):
    rows, inner = gate_pre.shape
    pre = jnp.concatenate([gate_pre, up_pre], axis=1).reshape((2, -1, 2 * inner))
    own = lax.dynamic_index_in_dim(pre, mine[0], 0, keepdims=False)
    sent = lax.dynamic_index_in_dim(pre, 1 - mine[0], 0, keepdims=False)
    near = swapped(sent)
    far = lax.ppermute(own, "xh", [(0, 1), (1, 0)])
    both = lax.ppermute(sent, ("xh", "core"), [(k, k ^ 3) for k in range(4)])
    return pl.pallas_call(
        pre_rows_kernel,
        out_shape=jax.ShapeDtypeStruct((rows, 4 * inner), jnp.bfloat16),
        in_specs=[SMEM] + [VMEM] * 5 + [ANY],
        out_specs=VMEM,
        compiler_params=PARAMS,
        cost_estimate=cost(1 << 10, 1 << 19),
    )(mine, gate_pre, up_pre, near, far, both, after)


def in_branch(work, *operands):
    def nothing(*operands):
        shapes = jax.eval_shape(work, *operands)
        return tuple(jnp.zeros(leaf.shape, leaf.dtype) for leaf in shapes)

    def always(*operands):
        return tuple(work(*operands))

    return lax.cond(lax.axis_index("z") < 8, always, nothing, *operands)


def shards(tokens, grad_out, gate_pre, up_pre, gate_latent, up_latent, down_latent):
    mine = jnp.stack([lax.axis_index("core"), lax.axis_index("xh")]).astype(jnp.int32)
    place = jnp.stack([lax.axis_index("xl"), lax.axis_index("y")]).astype(jnp.int32)
    gate_t, up_t = gate_latent.T, up_latent.T
    sent = first(grad_out, gate_t, up_t, down_latent)

    received = lax.all_to_all(sent, CHIP, 0, 0)
    down_other = swapped(down_latent)
    pre_rows = own_half(mine, gate_pre, up_pre, sent)
    pre_half = lax.all_gather(pre_rows, "z", axis=0, tiled=True)

    def exchanges(received, tokens, gate_t, up_t, down, down_other):
        tile = lax.all_to_all(sums_tile(received), ROW + ("core",), 0, 0)
        out_half, both = laid_out(received, down, down_other)
        partial = hidden_partial(tile, out_half, both)
        parts = lax.all_to_all(partial, ROW, 0, 0)
        far, quant = in_branch(far_work, tokens, partial, tile, gate_t, up_t)
        token_blocks = exchanged(far, CHIP, N_Y, 1, N_Y + 1)
        grad_hidden = lax.all_to_all(spread(parts, far), ROW, 0, 0)
        return (out_half, quant, grad_hidden, token_blocks)

    out_half, quant, grad_hidden, token_blocks = in_branch(
        exchanges, received, tokens, gate_t, up_t, down_latent, down_other
    )

    partial, acts = act_partial(grad_hidden, pre_half, quant)
    parts = lax.all_to_all(partial, CHIP, 0, 0)

    def joined(place, acts, out_half, token_blocks):
        own, sent = latent_grads(place, acts, out_half, token_blocks)
        return join(own, swapped(sent))

    grad_gate, grad_up, grad_down, done = in_branch(joined, place, acts, out_half, token_blocks)
    grad_tokens = total(parts, done)
    return (grad_tokens, grad_gate.T, grad_up.T, grad_down)


def solution(mesh):
    fine = Mesh(mesh.devices.reshape((2, 8, 2, 8, 2)), ROW + CHIP + ("core",))
    col = CHIP + ("core",)
    in_specs = (
        P(col, ROW),
        P(col, ROW),
        P(ROW, col),
        P(ROW, col),
        P(ROW, col),
        P(ROW, col),
        P(col, ROW),
    )
    out_specs = (P(col, ROW), P(ROW, col), P(ROW, col), P(col, ROW))
    return jax.shard_map(shards, mesh=fine, in_specs=in_specs, out_specs=out_specs, check_vma=False)
```

```python
import jax
import jax.numpy as jnp
from jax import lax
from jax.experimental import pallas as pl
from jax.experimental.pallas import tpu as pltpu
from jax.sharding import Mesh, PartitionSpec as P

EMBED_SIZE = 8192
GATE_INNER_SIZE = 14336
N_ROW = 16
N_CHIP = 16
ROW = ("xh", "z")
CHIP = ("xl", "y")
EXTRA = 16
N_Y = 8
LANES = 128
VMEM = pl.BlockSpec(memory_space=pltpu.VMEM)
SMEM = pl.BlockSpec(memory_space=pltpu.SMEM)
ANY = pl.BlockSpec(memory_space=pl.ANY)
WIDE = pltpu.CompilerParams(vmem_limit_bytes=58 * 1024 * 1024)
PARAMS = pltpu.CompilerParams(vmem_limit_bytes=40 * 1024 * 1024)


def cost(flops, bytes_accessed):
    return pl.CostEstimate(flops=flops, bytes_accessed=bytes_accessed, transcendentals=0)


def contract_last(left, right):
    return lax.dot_general(
        left, right, (((1,), (1,)), ((), ())), preferred_element_type=jnp.float32
    )


def contract_first(left, right):
    return lax.dot_general(
        left, right, (((0,), (0,)), ((), ())), preferred_element_type=jnp.float32
    )


def matmul(left, right):
    return lax.dot_general(
        left, right, (((1,), (0,)), ((), ())), preferred_element_type=jnp.float32
    )


def swiglu_grads(grad_hidden, gate_pre, up_pre):
    gate_f = gate_pre.astype(jnp.float32)
    up_f = up_pre.astype(jnp.float32)
    sigma = jax.nn.sigmoid(gate_f)
    silu_gate = gate_f * sigma
    slope = sigma * (1.0 + gate_f - silu_gate)
    grad_gpre = (grad_hidden * (up_f * slope)).astype(jnp.bfloat16)
    grad_upre = (grad_hidden * silu_gate).astype(jnp.bfloat16)
    hidden = (silu_gate * up_f).astype(jnp.bfloat16)
    return (grad_gpre, grad_upre, hidden)


def swapped(values):
    return lax.ppermute(values, "core", [(0, 1), (1, 0)])


def pieces_of(totals):
    pieces = []
    for total in totals:
        for _ in range(3):
            piece = total.astype(jnp.bfloat16).astype(jnp.float32)
            pieces.append(piece)
            total = total - piece
    pieces.append(jnp.zeros((EXTRA - len(pieces), totals[0].shape[1]), jnp.float32))
    return jnp.concatenate(pieces, axis=0).astype(jnp.bfloat16)


def totals_of(pieces):
    return [jnp.sum(pieces[3 * k : 3 * k + 3], axis=0, keepdims=True) for k in range(3)]


def first_kernel(out_ref, gate_ref, up_ref, down_ref, sent_ref):
    sums = []
    for ref in (gate_ref, up_ref, down_ref):
        total = jnp.sum(jnp.abs(ref[...].astype(jnp.float32)), axis=0, keepdims=True)
        sums.append(jnp.broadcast_to(jnp.sum(total, axis=1, keepdims=True), (1, LANES)))
    blocks = [out_ref[:, j * LANES : (j + 1) * LANES] for j in range(out_ref.shape[1] // LANES)]
    block = jnp.concatenate(blocks + [pieces_of(sums)], axis=0)
    for k in range(N_CHIP):
        sent_ref[k] = block


def first(grad_out, gate_t, up_t, down):
    rows, width = grad_out.shape
    return pl.pallas_call(
        first_kernel,
        out_shape=jax.ShapeDtypeStruct((N_CHIP, rows * width // LANES + EXTRA, LANES), jnp.bfloat16),
        in_specs=[VMEM] * 4,
        out_specs=VMEM,
        compiler_params=WIDE,
        cost_estimate=cost(1 << 20, 5 << 19),
    )(grad_out, gate_t, up_t, down)


def tile_kernel(extra_ref, after_ref, tile_ref):
    sums = totals_of(jnp.sum(extra_ref[...].astype(jnp.float32), axis=0))
    tile = jnp.concatenate(sums + [jnp.zeros((5, LANES), jnp.float32)], axis=0)
    tile_ref[...] = jnp.broadcast_to(tile[None], tile_ref.shape)


def sums_tile(received, after):
    rows = received.shape[1] - EXTRA
    return pl.pallas_call(
        tile_kernel,
        grid=(1,),
        out_shape=jax.ShapeDtypeStruct((2 * N_ROW, 8, LANES), jnp.float32),
        in_specs=[
            pl.BlockSpec((N_CHIP, EXTRA, LANES), lambda i: (0, rows // EXTRA, 0)),
            ANY,
        ],
        out_specs=pl.BlockSpec((2 * N_ROW, 8, LANES), lambda i: (0, 0, 0)),
        compiler_params=PARAMS,
        cost_estimate=cost(1 << 16, 1 << 18),
    )(received, after)


def scale_of(tile_ref, which):
    total = jnp.sum(tile_ref[...], axis=0)[which : which + 1, 0:1]
    return total / float(EMBED_SIZE * GATE_INNER_SIZE) + 1e-05


def clipped(values, scale):
    return jnp.clip(values.astype(jnp.float32), -scale, scale).astype(jnp.bfloat16)


def laid_out_kernel(received_ref, down_ref, other_ref, out_ref, both_ref):
    width = out_ref.shape[1]
    rows = (received_ref.shape[1] - EXTRA) * LANES // width
    for j in range(width // LANES):
        block = received_ref[:, j * rows : (j + 1) * rows, :].reshape((-1, LANES))
        out_ref[:, j * LANES : (j + 1) * LANES] = block
    both_ref[0] = down_ref[...]
    both_ref[1] = other_ref[...]


def laid_out(received, down, other):
    inner, width = down.shape
    rows = (received.shape[1] - EXTRA) * LANES // width
    return pl.pallas_call(
        laid_out_kernel,
        out_shape=(
            jax.ShapeDtypeStruct((N_CHIP * rows, width), jnp.bfloat16),
            jax.ShapeDtypeStruct((2, inner, width), jnp.bfloat16),
        ),
        in_specs=[VMEM] * 3,
        out_specs=(VMEM, VMEM),
        compiler_params=PARAMS,
        cost_estimate=cost(1 << 10, 3 << 20),
    )(received, down, other)


def partial_kernel(tile_ref, out_ref, both_ref, partial_ref):
    inner, width = both_ref.shape[1:]
    quant = clipped(both_ref[...].reshape((2 * inner, width)), scale_of(tile_ref, 2))
    rows = out_ref.shape[0] // 4
    blocks = partial_ref.shape[0] // 4
    for n in range(4):
        partial = contract_last(out_ref[n * rows : (n + 1) * rows, :], quant).astype(jnp.bfloat16)
        partial_ref[n * blocks : (n + 1) * blocks] = partial.reshape((blocks, -1, 2 * inner))


def hidden_partial(tile, out_half, both):
    inner = both.shape[1]
    rows = out_half.shape[0] // N_CHIP
    return pl.pallas_call(
        partial_kernel,
        out_shape=jax.ShapeDtypeStruct((N_ROW, rows, 2 * inner), jnp.bfloat16),
        in_specs=[VMEM] * 3,
        out_specs=VMEM,
        compiler_params=PARAMS,
        cost_estimate=cost(2 * 512 * 896 * 512, 4 << 20),
    )(tile, out_half, both)


def spread_kernel(parts_ref, after_ref, sent_ref):
    total = jnp.sum(parts_ref[...].astype(jnp.float32), axis=0).astype(jnp.bfloat16)
    for k in range(N_ROW):
        sent_ref[k] = total


def spread(parts, after):
    return pl.pallas_call(
        spread_kernel,
        out_shape=jax.ShapeDtypeStruct(parts.shape, jnp.bfloat16),
        in_specs=[VMEM, ANY],
        out_specs=VMEM,
        compiler_params=PARAMS,
        cost_estimate=cost(1 << 19, 2 << 20),
    )(parts, after)


def clip_kernel(tile_ref, gate_ref, up_ref, other_ref, quant_ref):
    inner = gate_ref.shape[0]
    for n, ref in enumerate((gate_ref, up_ref)):
        scale = scale_of(tile_ref, n)
        quant_ref[n, 0:inner, :] = clipped(ref[...], scale)
        quant_ref[n, inner:, :] = clipped(other_ref[n], scale)


def clipped_latents(tile, gate_t, up_t, other):
    inner, width = gate_t.shape
    return pl.pallas_call(
        clip_kernel,
        out_shape=jax.ShapeDtypeStruct((2, 2 * inner, width), jnp.bfloat16),
        in_specs=[VMEM] * 4,
        out_specs=VMEM,
        compiler_params=PARAMS,
        cost_estimate=cost(1 << 20, 4 << 20),
    )(tile, gate_t, up_t, other)


def act_kernel(hid_ref, pre_ref, quant_ref, partial_ref, acts_ref):
    both = hid_ref.shape[2]
    grad_hidden = hid_ref[...].reshape((-1, both)).astype(jnp.float32)
    acts = swiglu_grads(grad_hidden, pre_ref[:, :both], pre_ref[:, both:])
    partial = matmul(acts[0], quant_ref[0]) + matmul(acts[1], quant_ref[1])
    partial_ref[...] = partial.astype(jnp.bfloat16).reshape(partial_ref.shape)
    for n, act in enumerate(acts):
        acts_ref[n] = act


def act_partial(grad_hidden, pre_half, quant):
    blocks, steps = 4, N_ROW // 4
    rows, both = grad_hidden.shape[1:]
    width = quant.shape[2]
    return pl.pallas_call(
        act_kernel,
        grid=(steps,),
        out_shape=(
            jax.ShapeDtypeStruct((N_CHIP, rows, width), jnp.bfloat16),
            jax.ShapeDtypeStruct((3, N_ROW * rows, both), jnp.bfloat16),
        ),
        in_specs=[
            pl.BlockSpec((blocks, rows, both), lambda i: (i, 0, 0)),
            pl.BlockSpec((blocks * rows, 2 * both), lambda i: (i, 0)),
            pl.BlockSpec(quant.shape, lambda i: (0, 0, 0)),
        ],
        out_specs=(
            pl.BlockSpec((blocks, rows, width), lambda i: (i, 0, 0)),
            pl.BlockSpec((3, blocks * rows, both), lambda i: (0, i, 0)),
        ),
        compiler_params=WIDE,
        cost_estimate=cost(4 * 512 * 896 * 512, 8 << 20),
    )(grad_hidden, pre_half, quant)


def latent_grads_kernel(place_ref, acts_ref, out_ref, tokens_ref, own_ref, sent_ref, rows_ref):
    rows = tokens_ref.shape[1]
    for block in range(2 * N_Y):
        flip, bits = block & 1, block >> 1
        offset = 2 * (bits & 3) + bits // 4
        chip = (place_ref[0] ^ flip) * N_Y + (place_ref[1] ^ offset)
        rows_ref[pl.ds(pl.multiple_of(chip * rows, rows), rows), :] = tokens_ref[block]
    inner = own_ref.shape[1]
    for n in range(3):
        half = out_ref[...] if n == 2 else rows_ref[...]
        grad = contract_first(acts_ref[n], half)
        own_ref[n] = grad[:inner]
        sent_ref[n] = grad[inner:].astype(jnp.bfloat16)


def latent_grads(place, acts, out_half, token_blocks):
    inner, width = acts.shape[2] // 2, out_half.shape[1]
    return pl.pallas_call(
        latent_grads_kernel,
        out_shape=(
            jax.ShapeDtypeStruct((3, inner, width), jnp.float32),
            jax.ShapeDtypeStruct((3, inner, width), jnp.bfloat16),
        ),
        in_specs=[SMEM] + [VMEM] * 3,
        out_specs=(VMEM, VMEM),
        scratch_shapes=[pltpu.VMEM(out_half.shape, jnp.bfloat16)],
        compiler_params=PARAMS,
        cost_estimate=cost(6 * 512 * 896 * 512, 8 << 20),
    )(place, acts, out_half, token_blocks)


def join_kernel(own_ref, other_ref, *refs):
    for n, ref in enumerate(refs[:3]):
        ref[...] = (own_ref[n] + other_ref[n].astype(jnp.float32)).astype(jnp.bfloat16)
    refs[3][...] = jnp.zeros(refs[3].shape, jnp.float32)


def join(own, other):
    grad = jax.ShapeDtypeStruct(own.shape[1:], jnp.bfloat16)
    return pl.pallas_call(
        join_kernel,
        out_shape=(grad, grad, grad, jax.ShapeDtypeStruct((8, LANES), jnp.float32)),
        in_specs=[VMEM] * 2,
        out_specs=(VMEM,) * 4,
        compiler_params=PARAMS,
        cost_estimate=cost(1 << 20, 5 << 20),
    )(own, other)


def total_kernel(parts_ref, after_ref, total_ref):
    total_ref[...] = jnp.sum(parts_ref[...].astype(jnp.float32), axis=0).astype(jnp.bfloat16)


def total(parts, after):
    return pl.pallas_call(
        total_kernel,
        out_shape=jax.ShapeDtypeStruct(parts.shape[1:], jnp.bfloat16),
        in_specs=[VMEM] * 2,
        out_specs=VMEM,
        compiler_params=PARAMS,
        cost_estimate=cost(1 << 18, 1 << 19),
    )(parts, after)


def copy_kernel(values_ref, after_ref, copy_ref):
    copy_ref[...] = values_ref[...]


def copy_after(values, after):
    return pl.pallas_call(
        copy_kernel,
        out_shape=jax.ShapeDtypeStruct(values.shape, values.dtype),
        in_specs=[VMEM, ANY],
        out_specs=VMEM,
        cost_estimate=cost(1, 1 << 16),
    )(values, after)


def exchanged(blocks, axis, *steps):
    count = 2 if axis == "xl" else N_Y
    others = [lax.ppermute(blocks, axis, [(k, k ^ step) for k in range(count)]) for step in steps]
    return jnp.concatenate([blocks] + others, axis=0)


def near_work(tokens):
    return (exchanged(tokens[None], "xl", 1),)


def far_work(pair, done, tile, gate_t, up_t):
    other_latents = swapped(jnp.stack([gate_t, up_t]))
    blocks = exchanged(copy_after(pair, done), "y", 2, 4, 6)
    return blocks, clipped_latents(tile, gate_t, up_t, other_latents)


def own_half(core, gate_pre, up_pre):
    inner = gate_pre.shape[1]
    pre = jnp.concatenate([gate_pre, up_pre], axis=1).reshape((2, -1, 2 * inner))
    own = lax.dynamic_index_in_dim(pre, core, 0, keepdims=False)
    other = swapped(lax.dynamic_index_in_dim(pre, 1 - core, 0, keepdims=False))
    rows = jnp.concatenate(
        [own[:, :inner], other[:, :inner], own[:, inner:], other[:, inner:]], axis=1
    )
    return rows


def in_branch(work, *operands):
    def nothing(*operands):
        shapes = jax.eval_shape(work, *operands)
        return tuple(jnp.zeros(leaf.shape, leaf.dtype) for leaf in shapes)

    def always(*operands):
        return tuple(work(*operands))

    return lax.cond(lax.axis_index("z") < 8, always, nothing, *operands)


def shards(tokens, grad_out, gate_pre, up_pre, gate_latent, up_latent, down_latent):
    core = lax.axis_index("core")
    place = jnp.stack([lax.axis_index("xl"), lax.axis_index("y")]).astype(jnp.int32)
    gate_t, up_t = gate_latent.T, up_latent.T
    pre_half = lax.all_gather(own_half(core, gate_pre, up_pre), ROW, axis=0, tiled=True)
    sent = first(grad_out, gate_t, up_t, down_latent)

    def exchanges(sent, tokens, gate_t, up_t, down):
        received = lax.all_to_all(sent, CHIP, 0, 0)
        down_other = swapped(down)
        (pair,) = in_branch(near_work, tokens)
        tile = lax.all_to_all(sums_tile(received, pair), ROW + ("core",), 0, 0)
        out_half, both = laid_out(received, down, down_other)
        partial = hidden_partial(tile, out_half, both)
        parts = lax.all_to_all(partial, ROW, 0, 0)
        far, quant = in_branch(far_work, pair, partial, tile, gate_t, up_t)
        token_blocks = exchanged(far, "y", 1)
        grad_hidden = lax.all_to_all(spread(parts, far), ROW, 0, 0)
        return (out_half, quant, grad_hidden, token_blocks)

    out_half, quant, grad_hidden, token_blocks = in_branch(
        exchanges, sent, tokens, gate_t, up_t, down_latent
    )

    partial, acts = act_partial(grad_hidden, pre_half, quant)
    parts = lax.all_to_all(partial, CHIP, 0, 0)

    def joined(place, acts, out_half, token_blocks):
        own, sent = latent_grads(place, acts, out_half, token_blocks)
        return join(own, swapped(sent))

    grad_gate, grad_up, grad_down, done = in_branch(joined, place, acts, out_half, token_blocks)
    grad_tokens = total(parts, done)
    return (grad_tokens, grad_gate.T, grad_up.T, grad_down)


def solution(mesh):
    fine = Mesh(mesh.devices.reshape((2, 8, 2, 8, 2)), ROW + CHIP + ("core",))
    col = CHIP + ("core",)
    in_specs = (
        P(col, ROW),
        P(col, ROW),
        P(ROW, col),
        P(ROW, col),
        P(ROW, col),
        P(ROW, col),
        P(col, ROW),
    )
    out_specs = (P(col, ROW), P(ROW, col), P(ROW, col), P(col, ROW))
    return jax.shard_map(shards, mesh=fine, in_specs=in_specs, out_specs=out_specs, check_vma=False)
```

```python
import jax
import jax.numpy as jnp
from jax import lax
from jax.experimental import pallas as pl
from jax.experimental.pallas import tpu as pltpu
from jax.sharding import Mesh, PartitionSpec as P

EMBED_SIZE = 8192
GATE_INNER_SIZE = 14336
N_ROW = 16
N_CHIP = 16
ROW = ("xh", "z")
CHIP = ("xl", "y")
EXTRA = 16
N_Y = 8
LANES = 128
VMEM = pl.BlockSpec(memory_space=pltpu.VMEM)
SMEM = pl.BlockSpec(memory_space=pltpu.SMEM)
ANY = pl.BlockSpec(memory_space=pl.ANY)
WIDE = pltpu.CompilerParams(vmem_limit_bytes=58 * 1024 * 1024)
PARAMS = pltpu.CompilerParams(vmem_limit_bytes=40 * 1024 * 1024)


def cost(flops, bytes_accessed):
    return pl.CostEstimate(flops=flops, bytes_accessed=bytes_accessed, transcendentals=0)


def contract_last(left, right):
    return lax.dot_general(
        left, right, (((1,), (1,)), ((), ())), preferred_element_type=jnp.float32
    )


def contract_first(left, right):
    return lax.dot_general(
        left, right, (((0,), (0,)), ((), ())), preferred_element_type=jnp.float32
    )


def matmul(left, right):
    return lax.dot_general(
        left, right, (((1,), (0,)), ((), ())), preferred_element_type=jnp.float32
    )


def swiglu_grads(grad_hidden, gate_pre, up_pre):
    gate_f = gate_pre.astype(jnp.float32)
    up_f = up_pre.astype(jnp.float32)
    sigma = jax.nn.sigmoid(gate_f)
    silu_gate = gate_f * sigma
    slope = sigma * (1.0 + gate_f - silu_gate)
    grad_gpre = (grad_hidden * (up_f * slope)).astype(jnp.bfloat16)
    grad_upre = (grad_hidden * silu_gate).astype(jnp.bfloat16)
    hidden = (silu_gate * up_f).astype(jnp.bfloat16)
    return (grad_gpre, grad_upre, hidden)


def swapped(values):
    return lax.ppermute(values, "core", [(0, 1), (1, 0)])


def pieces_of(totals):
    pieces = []
    for total in totals:
        for _ in range(3):
            piece = total.astype(jnp.bfloat16).astype(jnp.float32)
            pieces.append(piece)
            total = total - piece
    pieces.append(jnp.zeros((EXTRA - len(pieces), totals[0].shape[1]), jnp.float32))
    return jnp.concatenate(pieces, axis=0).astype(jnp.bfloat16)


def totals_of(pieces):
    return [jnp.sum(pieces[3 * k : 3 * k + 3], axis=0, keepdims=True) for k in range(3)]


def half_of(ref, core):
    rows = ref.shape[0] // 2
    return ref[pl.ds(pl.multiple_of(core * rows, rows), rows), :]


def first_kernel(core_ref, gate_pre_ref, up_pre_ref, gate_ref, up_ref, down_ref, sent_ref, sums_ref):
    rows, inner = gate_pre_ref.shape[0] // 2, gate_pre_ref.shape[1]
    lanes = sent_ref.shape[1] // 2
    sums = []
    for ref in (gate_ref, up_ref, down_ref):
        total = jnp.sum(jnp.abs(ref[...].astype(jnp.float32)), axis=0, keepdims=True)
        sums.append(jnp.broadcast_to(jnp.sum(total, axis=1, keepdims=True), (1, 2 * lanes)))
    sent_ref[...] = jnp.zeros(sent_ref.shape, sent_ref.dtype)
    sent_ref[0:rows, 0:inner] = half_of(gate_pre_ref, 1 - core_ref[0])
    sent_ref[0:rows, lanes : lanes + inner] = half_of(up_pre_ref, 1 - core_ref[0])
    sent_ref[rows:, :] = pieces_of(sums)
    tile = jnp.concatenate(sums + [jnp.zeros((5, 2 * lanes), jnp.float32)], axis=0)
    sums_ref[...] = tile[:, :LANES]


def first(core, gate_pre, up_pre, gate_t, up_t, down):
    rows, inner = gate_pre.shape
    lanes = -(-inner // LANES) * LANES
    return pl.pallas_call(
        first_kernel,
        out_shape=(
            jax.ShapeDtypeStruct((rows // 2 + EXTRA, 2 * lanes), jnp.bfloat16),
            jax.ShapeDtypeStruct((8, LANES), jnp.float32),
        ),
        in_specs=[SMEM] + [VMEM] * 5,
        out_specs=(VMEM, VMEM),
        compiler_params=WIDE,
        cost_estimate=cost(1 << 20, 3 << 19),
    )(core, gate_pre, up_pre, gate_t, up_t, down)


def second_kernel(core_ref, gate_pre_ref, up_pre_ref, other_ref, sums_ref, out_ref, pre_ref, sent_ref):
    rows, inner = gate_pre_ref.shape[0] // 2, gate_pre_ref.shape[1]
    lanes = other_ref.shape[1] // 2
    pre_ref[...] = jnp.concatenate(
        [
            half_of(gate_pre_ref, core_ref[0]),
            other_ref[0:rows, 0:inner],
            half_of(up_pre_ref, core_ref[0]),
            other_ref[0:rows, lanes : lanes + inner],
        ],
        axis=1,
    )
    others = totals_of(other_ref[rows:, :LANES].astype(jnp.float32))
    extra = pieces_of([sums_ref[n : n + 1, :] + others[n] for n in range(3)])
    blocks = [out_ref[:, j * LANES : (j + 1) * LANES] for j in range(out_ref.shape[1] // LANES)]
    block = jnp.concatenate(blocks + [extra], axis=0)
    for k in range(N_CHIP):
        sent_ref[k] = block


def second(core, gate_pre, up_pre, other, sums, grad_out):
    rows, width = grad_out.shape
    inner = gate_pre.shape[1]
    return pl.pallas_call(
        second_kernel,
        out_shape=(
            jax.ShapeDtypeStruct((rows, 4 * inner), jnp.bfloat16),
            jax.ShapeDtypeStruct((N_CHIP, rows * width // LANES + EXTRA, LANES), jnp.bfloat16),
        ),
        in_specs=[SMEM] + [VMEM] * 5,
        out_specs=(VMEM, VMEM),
        compiler_params=WIDE,
        cost_estimate=cost(1 << 16, 1 << 20),
    )(core, gate_pre, up_pre, other, sums, grad_out)


def tile_kernel(extra_ref, after_ref, tile_ref):
    sums = totals_of(jnp.sum(extra_ref[...].astype(jnp.float32), axis=0))
    tile = jnp.concatenate(sums + [jnp.zeros((5, LANES), jnp.float32)], axis=0)
    tile_ref[...] = jnp.broadcast_to(tile[None], tile_ref.shape)


def sums_tile(received, after):
    rows = received.shape[1] - EXTRA
    return pl.pallas_call(
        tile_kernel,
        grid=(1,),
        out_shape=jax.ShapeDtypeStruct((N_ROW, 8, LANES), jnp.float32),
        in_specs=[
            pl.BlockSpec((N_CHIP, EXTRA, LANES), lambda i: (0, rows // EXTRA, 0)),
            ANY,
        ],
        out_specs=pl.BlockSpec((N_ROW, 8, LANES), lambda i: (0, 0, 0)),
        compiler_params=PARAMS,
        cost_estimate=cost(1 << 16, 1 << 18),
    )(received, after)


def scale_of(tile_ref, which):
    total = jnp.sum(tile_ref[...], axis=0)[which : which + 1, 0:1]
    return total / float(EMBED_SIZE * GATE_INNER_SIZE) + 1e-05


def clipped(values, scale):
    return jnp.clip(values.astype(jnp.float32), -scale, scale).astype(jnp.bfloat16)


def laid_out_kernel(received_ref, down_ref, other_ref, out_ref, both_ref):
    width = out_ref.shape[1]
    rows = (received_ref.shape[1] - EXTRA) * LANES // width
    for j in range(width // LANES):
        block = received_ref[:, j * rows : (j + 1) * rows, :].reshape((-1, LANES))
        out_ref[:, j * LANES : (j + 1) * LANES] = block
    both_ref[0] = down_ref[...]
    both_ref[1] = other_ref[...]


def laid_out(received, down, other):
    inner, width = down.shape
    rows = (received.shape[1] - EXTRA) * LANES // width
    return pl.pallas_call(
        laid_out_kernel,
        out_shape=(
            jax.ShapeDtypeStruct((N_CHIP * rows, width), jnp.bfloat16),
            jax.ShapeDtypeStruct((2, inner, width), jnp.bfloat16),
        ),
        in_specs=[VMEM] * 3,
        out_specs=(VMEM, VMEM),
        compiler_params=PARAMS,
        cost_estimate=cost(1 << 10, 3 << 20),
    )(received, down, other)


def partial_kernel(tile_ref, out_ref, both_ref, partial_ref):
    inner, width = both_ref.shape[1:]
    quant = clipped(both_ref[...].reshape((2 * inner, width)), scale_of(tile_ref, 2))
    rows = out_ref.shape[0] // 4
    blocks = partial_ref.shape[0] // 4
    for n in range(4):
        partial = contract_last(out_ref[n * rows : (n + 1) * rows, :], quant).astype(jnp.bfloat16)
        partial_ref[n * blocks : (n + 1) * blocks] = partial.reshape((blocks, -1, 2 * inner))


def hidden_partial(tile, out_half, both):
    inner = both.shape[1]
    rows = out_half.shape[0] // N_CHIP
    return pl.pallas_call(
        partial_kernel,
        out_shape=jax.ShapeDtypeStruct((N_ROW, rows, 2 * inner), jnp.bfloat16),
        in_specs=[VMEM] * 3,
        out_specs=VMEM,
        compiler_params=PARAMS,
        cost_estimate=cost(2 * 512 * 896 * 512, 4 << 20),
    )(tile, out_half, both)


def spread_kernel(parts_ref, after_ref, sent_ref):
    total = jnp.sum(parts_ref[...].astype(jnp.float32), axis=0).astype(jnp.bfloat16)
    for k in range(N_ROW):
        sent_ref[k] = total


def spread(parts, after):
    return pl.pallas_call(
        spread_kernel,
        out_shape=jax.ShapeDtypeStruct(parts.shape, jnp.bfloat16),
        in_specs=[VMEM, ANY],
        out_specs=VMEM,
        compiler_params=PARAMS,
        cost_estimate=cost(1 << 19, 2 << 20),
    )(parts, after)


def clip_kernel(tile_ref, gate_ref, up_ref, other_ref, quant_ref):
    inner = gate_ref.shape[0]
    for n, ref in enumerate((gate_ref, up_ref)):
        scale = scale_of(tile_ref, n)
        quant_ref[n, 0:inner, :] = clipped(ref[...], scale)
        quant_ref[n, inner:, :] = clipped(other_ref[n], scale)


def clipped_latents(tile, gate_t, up_t, other):
    inner, width = gate_t.shape
    return pl.pallas_call(
        clip_kernel,
        out_shape=jax.ShapeDtypeStruct((2, 2 * inner, width), jnp.bfloat16),
        in_specs=[VMEM] * 4,
        out_specs=VMEM,
        compiler_params=PARAMS,
        cost_estimate=cost(1 << 20, 4 << 20),
    )(tile, gate_t, up_t, other)


def act_kernel(hid_ref, pre_ref, quant_ref, partial_ref, acts_ref):
    both = hid_ref.shape[2]
    grad_hidden = hid_ref[...].reshape((-1, both)).astype(jnp.float32)
    acts = swiglu_grads(grad_hidden, pre_ref[:, :both], pre_ref[:, both:])
    partial = matmul(acts[0], quant_ref[0]) + matmul(acts[1], quant_ref[1])
    partial_ref[...] = partial.astype(jnp.bfloat16).reshape(partial_ref.shape)
    for n, act in enumerate(acts):
        acts_ref[n] = act


def act_partial(grad_hidden, pre_half, quant):
    blocks, steps = 4, N_ROW // 4
    rows, both = grad_hidden.shape[1:]
    width = quant.shape[2]
    return pl.pallas_call(
        act_kernel,
        grid=(steps,),
        out_shape=(
            jax.ShapeDtypeStruct((N_CHIP, rows, width), jnp.bfloat16),
            jax.ShapeDtypeStruct((3, N_ROW * rows, both), jnp.bfloat16),
        ),
        in_specs=[
            pl.BlockSpec((blocks, rows, both), lambda i: (i, 0, 0)),
            pl.BlockSpec((blocks * rows, 2 * both), lambda i: (i, 0)),
            pl.BlockSpec(quant.shape, lambda i: (0, 0, 0)),
        ],
        out_specs=(
            pl.BlockSpec((blocks, rows, width), lambda i: (i, 0, 0)),
            pl.BlockSpec((3, blocks * rows, both), lambda i: (0, i, 0)),
        ),
        compiler_params=WIDE,
        cost_estimate=cost(4 * 512 * 896 * 512, 8 << 20),
    )(grad_hidden, pre_half, quant)


def latent_grads_kernel(place_ref, acts_ref, out_ref, tokens_ref, own_ref, sent_ref, rows_ref):
    rows = tokens_ref.shape[1]
    for block in range(2 * N_Y):
        flip, bits = block & 1, block >> 1
        offset = 2 * (bits & 3) + bits // 4
        chip = (place_ref[0] ^ flip) * N_Y + (place_ref[1] ^ offset)
        rows_ref[pl.ds(pl.multiple_of(chip * rows, rows), rows), :] = tokens_ref[block]
    inner = own_ref.shape[1]
    for n in range(3):
        half = out_ref[...] if n == 2 else rows_ref[...]
        grad = contract_first(acts_ref[n], half)
        own_ref[n] = grad[:inner]
        sent_ref[n] = grad[inner:].astype(jnp.bfloat16)


def latent_grads(place, acts, out_half, token_blocks):
    inner, width = acts.shape[2] // 2, out_half.shape[1]
    return pl.pallas_call(
        latent_grads_kernel,
        out_shape=(
            jax.ShapeDtypeStruct((3, inner, width), jnp.float32),
            jax.ShapeDtypeStruct((3, inner, width), jnp.bfloat16),
        ),
        in_specs=[SMEM] + [VMEM] * 3,
        out_specs=(VMEM, VMEM),
        scratch_shapes=[pltpu.VMEM(out_half.shape, jnp.bfloat16)],
        compiler_params=PARAMS,
        cost_estimate=cost(6 * 512 * 896 * 512, 8 << 20),
    )(place, acts, out_half, token_blocks)


def join_kernel(own_ref, other_ref, *refs):
    for n, ref in enumerate(refs[:3]):
        ref[...] = (own_ref[n] + other_ref[n].astype(jnp.float32)).astype(jnp.bfloat16)
    refs[3][...] = jnp.zeros(refs[3].shape, jnp.float32)


def join(own, other):
    grad = jax.ShapeDtypeStruct(own.shape[1:], jnp.bfloat16)
    return pl.pallas_call(
        join_kernel,
        out_shape=(grad, grad, grad, jax.ShapeDtypeStruct((8, LANES), jnp.float32)),
        in_specs=[VMEM] * 2,
        out_specs=(VMEM,) * 4,
        compiler_params=PARAMS,
        cost_estimate=cost(1 << 20, 5 << 20),
    )(own, other)


def total_kernel(parts_ref, after_ref, total_ref):
    total_ref[...] = jnp.sum(parts_ref[...].astype(jnp.float32), axis=0).astype(jnp.bfloat16)


def total(parts, after):
    return pl.pallas_call(
        total_kernel,
        out_shape=jax.ShapeDtypeStruct(parts.shape[1:], jnp.bfloat16),
        in_specs=[VMEM] * 2,
        out_specs=VMEM,
        compiler_params=PARAMS,
        cost_estimate=cost(1 << 18, 1 << 19),
    )(parts, after)


def copy_kernel(values_ref, after_ref, copy_ref):
    copy_ref[...] = values_ref[...]


def copy_after(values, after):
    return pl.pallas_call(
        copy_kernel,
        out_shape=jax.ShapeDtypeStruct(values.shape, values.dtype),
        in_specs=[VMEM, ANY],
        out_specs=VMEM,
        cost_estimate=cost(1, 1 << 16),
    )(values, after)


def exchanged(blocks, axis, *steps):
    count = 2 if axis == "xl" else N_Y
    others = [lax.ppermute(blocks, axis, [(k, k ^ step) for k in range(count)]) for step in steps]
    return jnp.concatenate([blocks] + others, axis=0)


def near_work(tokens):
    return (exchanged(tokens[None], "xl", 1),)


def far_work(pair, done, tile, gate_t, up_t):
    other_latents = swapped(jnp.stack([gate_t, up_t]))
    blocks = exchanged(copy_after(pair, done), "y", 2, 4, 6)
    return blocks, clipped_latents(tile, gate_t, up_t, other_latents)


def in_branch(work, *operands):
    def nothing(*operands):
        shapes = jax.eval_shape(work, *operands)
        return tuple(jnp.zeros(leaf.shape, leaf.dtype) for leaf in shapes)

    def always(*operands):
        return tuple(work(*operands))

    return lax.cond(lax.axis_index("z") < 8, always, nothing, *operands)


def shards(tokens, grad_out, gate_pre, up_pre, gate_latent, up_latent, down_latent):
    core = lax.axis_index("core").astype(jnp.int32).reshape((1,))
    place = jnp.stack([lax.axis_index("xl"), lax.axis_index("y")]).astype(jnp.int32)
    gate_t, up_t = gate_latent.T, up_latent.T
    sent, sums = first(core, gate_pre, up_pre, gate_t, up_t, down_latent)
    pre_rows, sent = second(core, gate_pre, up_pre, swapped(sent), sums, grad_out)
    pre_half = lax.all_gather(pre_rows, ROW, axis=0, tiled=True)

    def exchanges(sent, tokens, gate_t, up_t, down):
        received = lax.all_to_all(sent, CHIP, 0, 0)
        down_other = swapped(down)
        (pair,) = in_branch(near_work, tokens)
        tile = lax.all_to_all(sums_tile(received, pair), ROW, 0, 0)
        out_half, both = laid_out(received, down, down_other)
        partial = hidden_partial(tile, out_half, both)
        parts = lax.all_to_all(partial, ROW, 0, 0)
        far, quant = in_branch(far_work, pair, partial, tile, gate_t, up_t)
        token_blocks = exchanged(far, "y", 1)
        grad_hidden = lax.all_to_all(spread(parts, far), ROW, 0, 0)
        return (out_half, quant, grad_hidden, token_blocks)

    out_half, quant, grad_hidden, token_blocks = in_branch(
        exchanges, sent, tokens, gate_t, up_t, down_latent
    )

    partial, acts = act_partial(grad_hidden, pre_half, quant)
    parts = lax.all_to_all(partial, CHIP, 0, 0)

    def joined(place, acts, out_half, token_blocks):
        own, sent = latent_grads(place, acts, out_half, token_blocks)
        return join(own, swapped(sent))

    grad_gate, grad_up, grad_down, done = in_branch(joined, place, acts, out_half, token_blocks)
    grad_tokens = total(parts, done)
    return (grad_tokens, grad_gate.T, grad_up.T, grad_down)


def solution(mesh):
    fine = Mesh(mesh.devices.reshape((2, 8, 2, 8, 2)), ROW + CHIP + ("core",))
    col = CHIP + ("core",)
    in_specs = (
        P(col, ROW),
        P(col, ROW),
        P(ROW, col),
        P(ROW, col),
        P(ROW, col),
        P(ROW, col),
        P(col, ROW),
    )
    out_specs = (P(col, ROW), P(ROW, col), P(ROW, col), P(col, ROW))
    return jax.shard_map(shards, mesh=fine, in_specs=in_specs, out_specs=out_specs, check_vma=False)
```

```python
import jax
import jax.numpy as jnp
from jax import lax
from jax.experimental import pallas as pl
from jax.experimental.pallas import tpu as pltpu
from jax.sharding import Mesh, PartitionSpec as P

EMBED_SIZE = 8192
GATE_INNER_SIZE = 14336
N_ROW = 16
N_CHIP = 16
ROW = ("xh", "z")
CHIP = ("xl", "y")
EXTRA = 16
N_Y = 8
LANES = 128
VMEM = pl.BlockSpec(memory_space=pltpu.VMEM)
SMEM = pl.BlockSpec(memory_space=pltpu.SMEM)
ANY = pl.BlockSpec(memory_space=pl.ANY)
WIDE = pltpu.CompilerParams(vmem_limit_bytes=58 * 1024 * 1024)
PARAMS = pltpu.CompilerParams(vmem_limit_bytes=40 * 1024 * 1024)


def cost(flops, bytes_accessed):
    return pl.CostEstimate(flops=flops, bytes_accessed=bytes_accessed, transcendentals=0)


def contract_last(left, right):
    return lax.dot_general(
        left, right, (((1,), (1,)), ((), ())), preferred_element_type=jnp.float32
    )


def contract_first(left, right):
    return lax.dot_general(
        left, right, (((0,), (0,)), ((), ())), preferred_element_type=jnp.float32
    )


def matmul(left, right):
    return lax.dot_general(
        left, right, (((1,), (0,)), ((), ())), preferred_element_type=jnp.float32
    )


def swiglu_grads(grad_hidden, gate_pre, up_pre):
    gate_f = gate_pre.astype(jnp.float32)
    up_f = up_pre.astype(jnp.float32)
    sigma = jax.nn.sigmoid(gate_f)
    silu_gate = gate_f * sigma
    slope = sigma * (1.0 + gate_f - silu_gate)
    grad_gpre = (grad_hidden * (up_f * slope)).astype(jnp.bfloat16)
    grad_upre = (grad_hidden * silu_gate).astype(jnp.bfloat16)
    hidden = (silu_gate * up_f).astype(jnp.bfloat16)
    return (grad_gpre, grad_upre, hidden)


def swapped(values):
    return lax.ppermute(values, "core", [(0, 1), (1, 0)])


def pieces_of(totals):
    pieces = []
    for total in totals:
        for _ in range(3):
            piece = total.astype(jnp.bfloat16).astype(jnp.float32)
            pieces.append(piece)
            total = total - piece
    pieces.append(jnp.zeros((EXTRA - len(pieces), totals[0].shape[1]), jnp.float32))
    return jnp.concatenate(pieces, axis=0).astype(jnp.bfloat16)


def totals_of(pieces):
    return [jnp.sum(pieces[3 * k : 3 * k + 3], axis=0, keepdims=True) for k in range(3)]


def first_kernel(out_ref, gate_ref, up_ref, down_ref, sent_ref):
    sums = []
    for ref in (gate_ref, up_ref, down_ref):
        total = jnp.sum(jnp.abs(ref[...].astype(jnp.float32)), axis=0, keepdims=True)
        sums.append(jnp.broadcast_to(jnp.sum(total, axis=1, keepdims=True), (1, LANES)))
    blocks = [out_ref[:, j * LANES : (j + 1) * LANES] for j in range(out_ref.shape[1] // LANES)]
    block = jnp.concatenate(blocks + [pieces_of(sums)], axis=0)
    for k in range(N_CHIP):
        sent_ref[k] = block


def first(grad_out, gate_t, up_t, down):
    rows, width = grad_out.shape
    return pl.pallas_call(
        first_kernel,
        out_shape=jax.ShapeDtypeStruct((N_CHIP, rows * width // LANES + EXTRA, LANES), jnp.bfloat16),
        in_specs=[VMEM] * 4,
        out_specs=VMEM,
        compiler_params=WIDE,
        cost_estimate=cost(1 << 20, 5 << 19),
    )(grad_out, gate_t, up_t, down)


def tile_kernel(extra_ref, after_ref, tile_ref):
    sums = totals_of(jnp.sum(extra_ref[...].astype(jnp.float32), axis=0))
    tile = jnp.concatenate(sums + [jnp.zeros((5, LANES), jnp.float32)], axis=0)
    tile_ref[...] = jnp.broadcast_to(tile[None], tile_ref.shape)


def sums_tile(received, after):
    rows = received.shape[1] - EXTRA
    return pl.pallas_call(
        tile_kernel,
        grid=(1,),
        out_shape=jax.ShapeDtypeStruct((2 * N_ROW, 8, LANES), jnp.float32),
        in_specs=[
            pl.BlockSpec((N_CHIP, EXTRA, LANES), lambda i: (0, rows // EXTRA, 0)),
            ANY,
        ],
        out_specs=pl.BlockSpec((2 * N_ROW, 8, LANES), lambda i: (0, 0, 0)),
        compiler_params=PARAMS,
        cost_estimate=cost(1 << 16, 1 << 18),
    )(received, after)


def scale_of(tile_ref, which):
    total = jnp.sum(tile_ref[...], axis=0)[which : which + 1, 0:1]
    return total / float(EMBED_SIZE * GATE_INNER_SIZE) + 1e-05


def clipped(values, scale):
    return jnp.clip(values.astype(jnp.float32), -scale, scale).astype(jnp.bfloat16)


def laid_out_kernel(received_ref, down_ref, other_ref, out_ref, both_ref):
    width = out_ref.shape[1]
    rows = (received_ref.shape[1] - EXTRA) * LANES // width
    for j in range(width // LANES):
        block = received_ref[:, j * rows : (j + 1) * rows, :].reshape((-1, LANES))
        out_ref[:, j * LANES : (j + 1) * LANES] = block
    both_ref[0] = down_ref[...]
    both_ref[1] = other_ref[...]


def laid_out(received, down, other):
    inner, width = down.shape
    rows = (received.shape[1] - EXTRA) * LANES // width
    return pl.pallas_call(
        laid_out_kernel,
        out_shape=(
            jax.ShapeDtypeStruct((N_CHIP * rows, width), jnp.bfloat16),
            jax.ShapeDtypeStruct((2, inner, width), jnp.bfloat16),
        ),
        in_specs=[VMEM] * 3,
        out_specs=(VMEM, VMEM),
        compiler_params=PARAMS,
        cost_estimate=cost(1 << 10, 3 << 20),
    )(received, down, other)


def partial_kernel(tile_ref, out_ref, both_ref, partial_ref):
    inner, width = both_ref.shape[1:]
    quant = clipped(both_ref[...].reshape((2 * inner, width)), scale_of(tile_ref, 2))
    rows = out_ref.shape[0] // 4
    blocks = partial_ref.shape[0] // 4
    for n in range(4):
        partial = contract_last(out_ref[n * rows : (n + 1) * rows, :], quant).astype(jnp.bfloat16)
        partial_ref[n * blocks : (n + 1) * blocks] = partial.reshape((blocks, -1, 2 * inner))


def hidden_partial(tile, out_half, both):
    inner = both.shape[1]
    rows = out_half.shape[0] // N_CHIP
    return pl.pallas_call(
        partial_kernel,
        out_shape=jax.ShapeDtypeStruct((N_ROW, rows, 2 * inner), jnp.bfloat16),
        in_specs=[VMEM] * 3,
        out_specs=VMEM,
        compiler_params=PARAMS,
        cost_estimate=cost(2 * 512 * 896 * 512, 4 << 20),
    )(tile, out_half, both)


def spread_kernel(parts_ref, after_ref, sent_ref):
    total = jnp.sum(parts_ref[...].astype(jnp.float32), axis=0).astype(jnp.bfloat16)
    for k in range(N_ROW):
        sent_ref[k] = total


def spread(parts, after):
    return pl.pallas_call(
        spread_kernel,
        out_shape=jax.ShapeDtypeStruct(parts.shape, jnp.bfloat16),
        in_specs=[VMEM, ANY],
        out_specs=VMEM,
        compiler_params=PARAMS,
        cost_estimate=cost(1 << 19, 2 << 20),
    )(parts, after)


def clip_kernel(tile_ref, gate_ref, up_ref, other_ref, quant_ref):
    inner = gate_ref.shape[0]
    for n, ref in enumerate((gate_ref, up_ref)):
        scale = scale_of(tile_ref, n)
        quant_ref[n, 0:inner, :] = clipped(ref[...], scale)
        quant_ref[n, inner:, :] = clipped(other_ref[n], scale)


def clipped_latents(tile, gate_t, up_t, other):
    inner, width = gate_t.shape
    return pl.pallas_call(
        clip_kernel,
        out_shape=jax.ShapeDtypeStruct((2, 2 * inner, width), jnp.bfloat16),
        in_specs=[VMEM] * 4,
        out_specs=VMEM,
        compiler_params=PARAMS,
        cost_estimate=cost(1 << 20, 4 << 20),
    )(tile, gate_t, up_t, other)


def act_kernel(hid_ref, pre_ref, quant_ref, partial_ref, acts_ref):
    both = hid_ref.shape[2]
    grad_hidden = hid_ref[...].reshape((-1, both)).astype(jnp.float32)
    pre = pre_ref[...].reshape((-1, 2 * both))
    acts = swiglu_grads(grad_hidden, pre[:, :both], pre[:, both:])
    partial = matmul(acts[0], quant_ref[0]) + matmul(acts[1], quant_ref[1])
    partial_ref[...] = partial.astype(jnp.bfloat16).reshape(partial_ref.shape)
    for n, act in enumerate(acts):
        acts_ref[n] = act


def act_partial(grad_hidden, pre_half, quant):
    blocks, steps = 4, N_ROW // 4
    rows, both = grad_hidden.shape[1:]
    width = quant.shape[2]
    return pl.pallas_call(
        act_kernel,
        grid=(steps,),
        out_shape=(
            jax.ShapeDtypeStruct((N_CHIP, rows, width), jnp.bfloat16),
            jax.ShapeDtypeStruct((3, N_ROW * rows, both), jnp.bfloat16),
        ),
        in_specs=[
            pl.BlockSpec((blocks, rows, both), lambda i: (i, 0, 0)),
            pl.BlockSpec((blocks, 1, rows, 2 * both), lambda i: (i % 2, i // 2, 0, 0)),
            pl.BlockSpec(quant.shape, lambda i: (0, 0, 0)),
        ],
        out_specs=(
            pl.BlockSpec((blocks, rows, width), lambda i: (i, 0, 0)),
            pl.BlockSpec((3, blocks * rows, both), lambda i: (0, i, 0)),
        ),
        compiler_params=WIDE,
        cost_estimate=cost(4 * 512 * 896 * 512, 8 << 20),
    )(grad_hidden, pre_half.reshape((N_ROW // 2, 2, rows, 2 * both)), quant)


def latent_grads_kernel(place_ref, acts_ref, out_ref, tokens_ref, own_ref, sent_ref, rows_ref):
    rows = tokens_ref.shape[1]
    for block in range(2 * N_Y):
        flip = (block >> 2) & 1
        offset = 2 * (block & 3) + (block >> 3)
        chip = (place_ref[0] ^ flip) * N_Y + (place_ref[1] ^ offset)
        rows_ref[pl.ds(pl.multiple_of(chip * rows, rows), rows), :] = tokens_ref[block]
    inner = own_ref.shape[1]
    for n in range(3):
        half = out_ref[...] if n == 2 else rows_ref[...]
        grad = contract_first(acts_ref[n], half)
        own_ref[n] = grad[:inner]
        sent_ref[n] = grad[inner:].astype(jnp.bfloat16)


def latent_grads(place, acts, out_half, token_blocks):
    inner, width = acts.shape[2] // 2, out_half.shape[1]
    return pl.pallas_call(
        latent_grads_kernel,
        out_shape=(
            jax.ShapeDtypeStruct((3, inner, width), jnp.float32),
            jax.ShapeDtypeStruct((3, inner, width), jnp.bfloat16),
        ),
        in_specs=[SMEM] + [VMEM] * 3,
        out_specs=(VMEM, VMEM),
        scratch_shapes=[pltpu.VMEM(out_half.shape, jnp.bfloat16)],
        compiler_params=PARAMS,
        cost_estimate=cost(6 * 512 * 896 * 512, 8 << 20),
    )(place, acts, out_half, token_blocks)


def join_kernel(own_ref, other_ref, *refs):
    for n, ref in enumerate(refs[:3]):
        ref[...] = (own_ref[n] + other_ref[n].astype(jnp.float32)).astype(jnp.bfloat16)
    refs[3][...] = jnp.zeros(refs[3].shape, jnp.float32)


def join(own, other):
    grad = jax.ShapeDtypeStruct(own.shape[1:], jnp.bfloat16)
    return pl.pallas_call(
        join_kernel,
        out_shape=(grad, grad, grad, jax.ShapeDtypeStruct((8, LANES), jnp.float32)),
        in_specs=[VMEM] * 2,
        out_specs=(VMEM,) * 4,
        compiler_params=PARAMS,
        cost_estimate=cost(1 << 20, 5 << 20),
    )(own, other)


def total_kernel(parts_ref, after_ref, total_ref):
    total_ref[...] = jnp.sum(parts_ref[...].astype(jnp.float32), axis=0).astype(jnp.bfloat16)


def total(parts, after):
    return pl.pallas_call(
        total_kernel,
        out_shape=jax.ShapeDtypeStruct(parts.shape[1:], jnp.bfloat16),
        in_specs=[VMEM] * 2,
        out_specs=VMEM,
        compiler_params=PARAMS,
        cost_estimate=cost(1 << 18, 1 << 19),
    )(parts, after)


def copy_kernel(values_ref, after_ref, copy_ref):
    copy_ref[...] = values_ref[...]


def copy_after(values, after):
    return pl.pallas_call(
        copy_kernel,
        out_shape=jax.ShapeDtypeStruct(values.shape, values.dtype),
        in_specs=[VMEM, ANY],
        out_specs=VMEM,
        cost_estimate=cost(1, 1 << 16),
    )(values, after)


def exchanged(blocks, axis, *steps):
    count = N_CHIP if axis == CHIP else N_Y
    others = [lax.ppermute(blocks, axis, [(k, k ^ step) for k in range(count)]) for step in steps]
    return jnp.concatenate([blocks] + others, axis=0)


def far_work(tokens, done, tile, gate_t, up_t):
    other_latents = swapped(jnp.stack([gate_t, up_t]))
    blocks = exchanged(copy_after(tokens, done)[None], "y", 2, 4, 6)
    return blocks, clipped_latents(tile, gate_t, up_t, other_latents)


def half_of(ref, core):
    rows = ref.shape[0] // 2
    return ref[pl.ds(pl.multiple_of(core * rows, rows), rows), :]


def pre_rows_kernel(mine_ref, gate_pre_ref, up_pre_ref, near_ref, far_ref, both_ref, rows_ref):
    rows, inner = gate_pre_ref.shape[0] // 2, gate_pre_ref.shape[1]
    core, xh = mine_ref[0], mine_ref[1]
    near, far, both = near_ref[...], far_ref[...], both_ref[...]
    own = [half_of(gate_pre_ref, core), near[:, :inner], half_of(up_pre_ref, core), near[:, inner:]]
    other = [far[:, :inner], both[:, :inner], far[:, inner:], both[:, inner:]]
    for at, parts in ((xh, own), (1 - xh, other)):
        rows_ref[pl.ds(pl.multiple_of(at * rows, rows), rows), :] = jnp.concatenate(parts, axis=1)


def own_half(mine, gate_pre, up_pre):
    rows, inner = gate_pre.shape
    pre = jnp.concatenate([gate_pre, up_pre], axis=1).reshape((2, -1, 2 * inner))
    own = lax.dynamic_index_in_dim(pre, mine[0], 0, keepdims=False)
    sent = lax.dynamic_index_in_dim(pre, 1 - mine[0], 0, keepdims=False)
    near = swapped(sent)
    far = lax.ppermute(own, "xh", [(0, 1), (1, 0)])
    both = lax.ppermute(sent, ("xh", "core"), [(k, k ^ 3) for k in range(4)])
    rows_pair = pl.pallas_call(
        pre_rows_kernel,
        out_shape=jax.ShapeDtypeStruct((rows, 4 * inner), jnp.bfloat16),
        in_specs=[SMEM] + [VMEM] * 5,
        out_specs=VMEM,
        compiler_params=PARAMS,
        cost_estimate=cost(1 << 10, 1 << 19),
    )(mine, gate_pre, up_pre, near, far, both)
    return (rows_pair,)


def in_branch(work, *operands):
    def nothing(*operands):
        shapes = jax.eval_shape(work, *operands)
        return tuple(jnp.zeros(leaf.shape, leaf.dtype) for leaf in shapes)

    def always(*operands):
        return tuple(work(*operands))

    return lax.cond(lax.axis_index("z") < 8, always, nothing, *operands)


def shards(tokens, grad_out, gate_pre, up_pre, gate_latent, up_latent, down_latent):
    mine = jnp.stack([lax.axis_index("core"), lax.axis_index("xh")]).astype(jnp.int32)
    place = jnp.stack([lax.axis_index("xl"), lax.axis_index("y")]).astype(jnp.int32)
    gate_t, up_t = gate_latent.T, up_latent.T
    sent = first(grad_out, gate_t, up_t, down_latent)

    def gathers(sent, mine, gate_pre, up_pre, down):
        received = lax.all_to_all(sent, CHIP, 0, 0)
        down_other = swapped(down)
        (pre_rows,) = in_branch(own_half, mine, gate_pre, up_pre)
        return (received, down_other, pre_rows, sums_tile(received, pre_rows))

    received, down_other, pre_rows, tile = in_branch(
        gathers, sent, mine, gate_pre, up_pre, down_latent
    )
    pre_half = lax.all_gather(pre_rows, "z", axis=0, tiled=True)

    def exchanges(received, tile, tokens, gate_t, up_t, down, down_other):
        tile = lax.all_to_all(tile, ROW + ("core",), 0, 0)
        out_half, both = laid_out(received, down, down_other)
        partial = hidden_partial(tile, out_half, both)
        parts = lax.all_to_all(partial, ROW, 0, 0)
        far, quant = in_branch(far_work, tokens, partial, tile, gate_t, up_t)
        token_blocks = exchanged(far, CHIP, N_Y, 1, N_Y + 1)
        grad_hidden = lax.all_to_all(spread(parts, far), ROW, 0, 0)
        return (out_half, quant, grad_hidden, token_blocks)

    out_half, quant, grad_hidden, token_blocks = in_branch(
        exchanges, received, tile, tokens, gate_t, up_t, down_latent, down_other
    )

    partial, acts = act_partial(grad_hidden, pre_half, quant)
    parts = lax.all_to_all(partial, CHIP, 0, 0)

    def joined(place, acts, out_half, token_blocks):
        own, sent = latent_grads(place, acts, out_half, token_blocks)
        return join(own, swapped(sent))

    grad_gate, grad_up, grad_down, done = in_branch(joined, place, acts, out_half, token_blocks)
    grad_tokens = total(parts, done)
    return (grad_tokens, grad_gate.T, grad_up.T, grad_down)


def solution(mesh):
    fine = Mesh(mesh.devices.reshape((2, 8, 2, 8, 2)), ROW + CHIP + ("core",))
    col = CHIP + ("core",)
    in_specs = (
        P(col, ROW),
        P(col, ROW),
        P(ROW, col),
        P(ROW, col),
        P(ROW, col),
        P(ROW, col),
        P(col, ROW),
    )
    out_specs = (P(col, ROW), P(ROW, col), P(ROW, col), P(col, ROW))
    return jax.shard_map(shards, mesh=fine, in_specs=in_specs, out_specs=out_specs, check_vma=False)
```
